256 devices in a mesh: phase: 16 (over x_hi, z), space: 16 (over y, x_lo, core).
Axes of the slice: x: 4 (x_hi: 2, x_lo: 2; x = x_hi * 2 + x_lo), y: 4, z: 8, core: 2. Of those that a mesh axis runs over, the one named last changes fastest.
Arguments:
- previous: float32 [32, 2, 5, 128, 1024], P('phase', None, None, 'space'), may hold values from -6 to 6
- forcing: float32 [32, 2, 5, 128, 1024], P('phase', None, None, 'space'), may hold values from -6 to 6
- jacobians: float32 [4, 5, 5], replicated, may hold values from -2.5 to 2.5
- coupling: float32 [4, 128, 1024], P(None, 'space'), may hold values from 0.1 to 0.3
- diagonal: float32 [128, 1024], P('space'), may hold values from 3 to 6
- inertia: float32 [128, 1024], P('space'), may hold values from 0.5 to 4
- pressure_weights: float32 [5], replicated, may hold values from -1 to 1
- surface_cells: int32 [131072], P('space'), may hold values from 0 to 8191
- modal_weights: float32 [131072], P('space'), may hold values from -0.015625 to 0.015625
- phase_index: int32 [32], replicated, may hold values from 0 to 31, each once
Outputs:
- final_state: float32 [32, 2, 5, 128, 1024], P('phase', None, None, 'space')
- influence: float32 [32, 2, 131072], P('phase', None, 'space')
- modal_work: float32 [32, 2], P('phase')
The draws below stay inside these ranges and needn't reach their ends.
Inputs may be any that keep to these rules, and one draw needn't show every extreme that they name: `phase_index`: each number from 0 to 31 appears once. `surface_cells`: entry s names the cell (row within the block) * 1024 + cell within the row, of the block of rows that begins at row (s // 8192) * 8.
All inputs are finite; a program needn't handle non-finite values.
Results may differ from the reference program's by a relative error of at most 0.0003.
Values sent between devices are 32-bit elements; how exact they have to be, the bound alone decides.
No kernel may reach another device: no remote copies, remote signals or barrier semaphores. Data moves between devices by JAX's collectives and lax.ppermute only.
A program may use at most 128 MiB of HBM per device.

```python
import math
import jax
import jax.numpy as jnp
from jax import lax

CJ = 8
CK = 1024
SURF_DEV = 8192
ITERS = 6
BLADES = 32
NJ = 128
SURF = 131072


def place_ends(result, stream_key, low, high):
    place = [jax.random.randint(jax.random.fold_in(stream_key, axis), (), 0, length) for axis, length in enumerate(result.shape)]
    longest = result.shape.index(max(result.shape))
    beside = place[:longest] + [(place[longest] + 1) % result.shape[longest]] + place[longest + 1:]
    return result.at[tuple(place)].set(low).at[tuple(beside)].set(high)


def block_levels(key, dims, cuts, smallest, largest):
    def one(axis_at, blocks):
        draws = jax.random.uniform(jax.random.fold_in(jax.random.fold_in(key, 6), axis_at), (blocks,), jnp.float32, smallest / len(cuts), largest / len(cuts))
        return jnp.repeat(jnp.exp(draws), dims[axis_at] // blocks).reshape((-1,) + (1,) * (len(dims) - axis_at - 1))

    loudness = one(*cuts[0])
    for cut in cuts[1:]:
        loudness = loudness * one(*cut)
    return loudness


def centred(own_key, shape, width, reach, cuts=(), kind=jnp.bfloat16):
    values = width * jax.random.normal(own_key, shape, jnp.float32)
    if cuts:
        values = values * block_levels(own_key, shape, cuts, -0.22, 0.18)
    return jnp.clip(values, -reach, reach).astype(kind)


def setup_inputs(seed: int = 0) -> dict:
    keys = jax.random.split(jax.random.key(seed), 11)
    previous = centred(keys[0], (BLADES, 2, 5, NJ, CK), 1.0, 6.0, ((0, 16), (3, 16)), jnp.float32)
    forcing = centred(keys[1], (BLADES, 2, 5, NJ, CK), 1.0, 6.0, ((0, 16), (3, 16)), jnp.float32)
    jacobians = centred(keys[2], (4, 5, 5), 5 ** -0.5, 2.5, (), jnp.float32)
    coupling = jnp.clip(jnp.exp(math.log(0.3) - 1.0986123 * jax.random.uniform(keys[3], (4, NJ, CK), jnp.float32) ** block_levels(keys[3], (4, NJ, CK), ((1, 16),), -0.2, 0.2)), 0.1, 0.3)
    diagonal = jnp.clip(3.0 + 3.0 * jax.random.uniform(keys[4], (NJ, CK), jnp.float32) ** block_levels(keys[4], (NJ, CK), ((0, 16),), -0.2, 0.2), 3.0, 6.0)
    inertia = jnp.clip(jnp.exp(math.log(4.0) - 2.0794415 * jax.random.uniform(keys[5], (NJ, CK), jnp.float32) ** block_levels(keys[5], (NJ, CK), ((0, 16),), -0.2, 0.2)), 0.5, 4.0)
    pressure_weights = jnp.clip(jax.random.uniform(keys[6], (5,), jnp.float32, -1.0, 1.0), -1.0, 1.0)
    surface_cells = place_ends(jax.random.randint(keys[7], (SURF,), 0, CJ * CK), jax.random.fold_in(keys[7], 1), 0, (CJ * CK) - 1).astype(jnp.int32)
    modal_weights = centred(keys[8], (SURF,), SURF ** -0.5, 0.015625, ((0, 16),), jnp.float32)
    phase_index = jax.random.permutation(keys[9], BLADES).astype(jnp.int32)
    return dict(previous=previous, forcing=forcing, jacobians=jacobians, coupling=coupling, diagonal=diagonal, inertia=inertia, pressure_weights=pressure_weights, surface_cells=surface_cells, modal_weights=modal_weights, phase_index=phase_index)


highest = lax.Precision.HIGHEST
relax_factor = 0.8


def rotate(layer_part, cos_phase, sin_phase):
    real_part = layer_part[0]
    imag_part = layer_part[1]
    return jnp.stack([cos_phase * real_part - sin_phase * imag_part, sin_phase * real_part + cos_phase * imag_part], axis=0)


def relax_once(state_now, force_phase, jacobians, coupling, diagonal, inertia, cos_phase, sin_phase):
    ghost_below = rotate(state_now[:, :, -1:], cos_phase, -sin_phase)
    ghost_above = rotate(state_now[:, :, :1], cos_phase, sin_phase)
    padded = jnp.concatenate([ghost_below, state_now, ghost_above], axis=2)
    row_before = padded[:, :, :-2]
    row_after = padded[:, :, 2:]
    zero_col = jnp.zeros_like(state_now[..., :1])
    col_before = jnp.concatenate([zero_col, state_now[..., :-1]], axis=3)
    col_after = jnp.concatenate([state_now[..., 1:], zero_col], axis=3)
    coupled = jnp.zeros_like(state_now)
    for direction, neighbour in enumerate((row_before, row_after, col_before, col_after)):
        coupled = coupled + coupling[direction] * jnp.einsum("vw,cwjk->cvjk", jacobians[direction], neighbour, precision=highest)
    rest = force_phase - coupled
    rest_re = rest[0]
    rest_im = rest[1]
    denom = diagonal * diagonal + inertia * inertia
    solved = jnp.stack([(diagonal * rest_re + inertia * rest_im) / denom, (diagonal * rest_im - inertia * rest_re) / denom], axis=0)
    return (1.0 - relax_factor) * state_now + relax_factor * solved


def reference(previous, forcing, jacobians, coupling, diagonal, inertia, pressure_weights, surface_cells, modal_weights, phase_index):
    blades = phase_index.shape[0]
    owner = jnp.arange(surface_cells.shape[0], dtype=jnp.int32) // SURF_DEV
    flat_cells = owner * (CJ * CK) + surface_cells
    angles = (2.0 * math.pi / blades) * phase_index.astype(jnp.float32)

    def solve_phase(inputs):
        start_state, force_phase, angle = inputs
        cos_phase = jnp.cos(angle)
        sin_phase = jnp.sin(angle)
        state_now = start_state
        for sweep_step in range(ITERS):
            state_now = relax_once(state_now, force_phase, jacobians, coupling, diagonal, inertia, cos_phase, sin_phase)
        pressure = jnp.einsum("v,cvjk->cjk", pressure_weights, state_now, precision=highest)
        surface = pressure.reshape(2, -1)[:, flat_cells]
        return state_now, surface

    final_state, surface = lax.map(solve_phase, (previous, forcing, angles))
    slots = jnp.arange(blades, dtype=jnp.int32)
    turns = (slots[:, None] * phase_index[None, :]) % blades
    table_angle = (2.0 * math.pi / blades) * turns.astype(jnp.float32)
    cos_table = jnp.cos(table_angle) / blades
    sin_table = jnp.sin(table_angle) / blades
    real_part = surface[:, 0]
    imag_part = surface[:, 1]
    infl_re = jnp.dot(cos_table, real_part, precision=highest) - jnp.dot(sin_table, imag_part, precision=highest)
    infl_im = jnp.dot(sin_table, real_part, precision=highest) + jnp.dot(cos_table, imag_part, precision=highest)
    influence = jnp.stack([infl_re, infl_im], axis=1)
    modal_work = jnp.einsum("bcs,s->bc", influence, modal_weights, precision=highest)
    return final_state, influence, modal_work
```

```python
import functools
import math

import jax
import jax.numpy as jnp
from jax import lax
from jax.experimental import pallas as pl
from jax.experimental.pallas import tpu as pltpu
from jax.sharding import PartitionSpec as P

ITERS = 6
WIDTH = 2
RELAX = 0.8
LANES = 128
HIGHEST = lax.Precision.HIGHEST

VMEM = pl.BlockSpec(memory_space=pltpu.VMEM)
SMEM = pl.BlockSpec(memory_space=pltpu.SMEM)


def call(kernel, name, out_shapes, scratch, flops, *operands, smem=0):
    return pl.pallas_call(
        kernel,
        name=name,
        out_shape=[jax.ShapeDtypeStruct(s, d) for s, d in out_shapes],
        in_specs=[SMEM] * smem + [VMEM] * (len(operands) - smem),
        out_specs=[VMEM] * len(out_shapes),
        scratch_shapes=scratch,
        compiler_params=pltpu.CompilerParams(vmem_limit_bytes=40 * 1024 * 1024),
        cost_estimate=pl.CostEstimate(
            flops=flops, bytes_accessed=1 << 20, transcendentals=0
        ),
    )(*operands)


def pack_kernel(x_ref, f_ref, cpl_ref, diag_ref, inert_ref, coef_ref, up_ref, down_ref):
    diag = diag_ref[...]
    inert = inert_ref[...]
    scale = RELAX / (diag * diag + inert * inert)
    coef_ref[0:4] = cpl_ref[...]
    coef_ref[4] = diag * scale
    coef_ref[5] = inert * scale
    for i in range(20):
        p, c, v = i // 10, i // 5 % 2, i % 5
        up_ref[2 * i : 2 * i + 2, :] = x_ref[p, c, v, 6:8, :]
        down_ref[2 * i : 2 * i + 2, :] = x_ref[p, c, v, 0:2, :]
        up_ref[40 + i : 41 + i, :] = f_ref[p, c, v, 7:8, :]
        down_ref[40 + i : 41 + i, :] = f_ref[p, c, v, 0:1, :]
    for i in range(6):
        up_ref[60 + i : 61 + i, :] = coef_ref[i, 7:8, :]
        down_ref[60 + i : 61 + i, :] = coef_ref[i, 0:1, :]


def lane_shift(ref, lead, kt, count):
    here = ref[(*lead, slice(None), pl.ds(pl.multiple_of(kt * LANES, LANES), LANES))]
    left = ref[
        (*lead, slice(None), pl.ds(pl.multiple_of(jnp.maximum(kt - 1, 0) * LANES, LANES), LANES))
    ]
    right = ref[
        (*lead, slice(None), pl.ds(pl.multiple_of(jnp.minimum(kt + 1, count - 1) * LANES, LANES), LANES))
    ]
    lane = lax.broadcasted_iota(jnp.int32, here.shape, 1)
    left = jnp.where(kt > 0, pltpu.roll(left, 1, 1), 0.0)
    right = jnp.where(kt < count - 1, pltpu.roll(right, LANES - 1, 1), 0.0)
    before = jnp.where(lane == 0, left, pltpu.roll(here, 1, 1))
    after = jnp.where(lane == LANES - 1, right, pltpu.roll(here, LANES - 1, 1))
    return here, before, after


def apply(jac_ref, coef, forcing, neighbours):
    rest = list(forcing)
    for d in range(4):
        scaled = [coef[d] * n for n in neighbours[d]]
        for v in range(5):
            total = jac_ref[(d * 5 + v) * 5] * scaled[0]
            for w in range(1, 5):
                total = total + jac_ref[(d * 5 + v) * 5 + w] * scaled[w]
            rest[v] = rest[v] - total
    return rest


def sweep_kernel(
    first, last, jac_ref, rot_ref, x_ref, f_ref, coef_ref, lo_ref, hi_ref, *refs
):
    if first:
        x_out, up_ref, down_ref, gf_ref, gcoef_ref, gx_ref, x1_ref, gx1_ref = refs
    else:
        gf_ref, gcoef_ref, *refs = refs
        if last:
            x_out, gx_ref, x1_ref, gx1_ref = refs
        else:
            x_out, up_ref, down_ref, gx_ref, x1_ref, gx1_ref = refs
    cells = x_ref.shape[-1]
    tiles = cells // LANES

    gap = jnp.zeros((4, cells), jnp.float32)
    for p in range(2):
        lo_c, lo_s = rot_ref[4 * p], rot_ref[4 * p + 1]
        hi_c, hi_s = rot_ref[4 * p + 2], rot_ref[4 * p + 3]
        for v in range(5):
            re, im = 10 * p + v, 10 * p + 5 + v

            def turned(ref, at_re, at_im, rows, c, s):
                a = ref[at_re : at_re + rows, :]
                b = ref[at_im : at_im + rows, :]
                return c * a - s * b, s * a + c * b

            lo = turned(lo_ref, 2 * re, 2 * im, 2, lo_c, lo_s)
            hi = turned(hi_ref, 2 * re, 2 * im, 2, hi_c, hi_s)
            for c, i in enumerate((re, im)):
                gx_ref[i, 0:2, :] = hi[c]
                gx_ref[i, 2:6, :] = gap
                gx_ref[i, 6:8, :] = lo[c]
            if first:
                lo = turned(lo_ref, 40 + re, 40 + im, 1, lo_c, lo_s)
                hi = turned(hi_ref, 40 + re, 40 + im, 1, hi_c, hi_s)
                for c, i in enumerate((re, im)):
                    gf_ref[i] = jnp.zeros((8, cells), jnp.float32)
                    gf_ref[i, 0:1, :] = hi[c]
                    gf_ref[i, 7:8, :] = lo[c]
    if first:
        for i in range(6):
            gcoef_ref[i] = jnp.zeros((8, cells), jnp.float32)
            gcoef_ref[i, 0:1, :] = hi_ref[60 + i : 61 + i, :]
            gcoef_ref[i, 7:8, :] = lo_ref[60 + i : 61 + i, :]

    row = lax.broadcasted_iota(jnp.int32, (8, LANES), 0)

    def both(own, ghost, own_lead, ghost_lead, kt):
        here, left, right = lane_shift(own, own_lead, kt, tiles)
        ghere, gleft, gright = lane_shift(ghost, ghost_lead, kt, tiles)
        down, gdown = pltpu.roll(here, 1, 0), pltpu.roll(ghere, 1, 0)
        up, gup = pltpu.roll(here, 7, 0), pltpu.roll(ghere, 7, 0)
        mine = (
            here,
            jnp.where(row == 0, gdown, down),
            jnp.where(row == 7, gup, up),
            left,
            right,
        )
        theirs = (
            ghere,
            jnp.where(row == 0, down, gdown),
            jnp.where(row == 7, up, gup),
            gleft,
            gright,
        )
        return mine, theirs

    def own_only(own, ghost, own_lead, ghost_lead, kt):
        here, left, right = lane_shift(own, own_lead, kt, tiles)
        at = pl.ds(pl.multiple_of(kt * LANES, LANES), LANES)
        ghere = ghost[(*ghost_lead, slice(None), at)]
        return (
            here,
            jnp.where(row == 0, pltpu.roll(ghere, 1, 0), pltpu.roll(here, 1, 0)),
            jnp.where(row == 7, pltpu.roll(ghere, 7, 0), pltpu.roll(here, 7, 0)),
            left,
            right,
        )

    def new_values(coef, parts, forcing):
        rests = [
            apply(jac_ref, coef, forcing[c], [[n[1 + d] for n in parts[c]] for d in range(4)])
            for c in range(2)
        ]
        old = [[n[0] for n in parts[c]] for c in range(2)]
        out_re, out_im = [], []
        for v in range(5):
            re, im = rests[0][v], rests[1][v]
            out_re.append((1.0 - RELAX) * old[0][v] + (coef[4] * re + coef[5] * im))
            out_im.append((1.0 - RELAX) * old[1][v] + (coef[4] * im - coef[5] * re))
        return out_re, out_im

    def lanes(kt):
        return pl.ds(pl.multiple_of(kt * LANES, LANES), LANES)

    def one(kt, _):
        at = lanes(kt)
        coef = [coef_ref[i, :, at] for i in range(6)]
        gcoef = [gcoef_ref[i, :, at] for i in range(6)]
        for p in range(2):
            mine, theirs = [[], []], [[], []]
            for c in range(2):
                for v in range(5):
                    a, b = both(x_ref, gx_ref, (p, c, v), (10 * p + 5 * c + v,), kt)
                    mine[c].append(a)
                    theirs[c].append(b)
            new = new_values(
                coef, mine, [[f_ref[p, c, v, :, at] for v in range(5)] for c in range(2)]
            )
            gnew = new_values(
                gcoef,
                theirs,
                [[gf_ref[10 * p + 5 * c + v, :, at] for v in range(5)] for c in range(2)],
            )
            for c in range(2):
                for v in range(5):
                    i = 10 * p + 5 * c + v
                    x1_ref[i, :, at] = new[c][v]
                    gx1_ref[i, :, at] = gnew[c][v]
        return 0

    def two(kt, _):
        at = lanes(kt)
        coef = [coef_ref[i, :, at] for i in range(6)]
        for p in range(2):
            mine = [
                [
                    own_only(x1_ref, gx1_ref, (10 * p + 5 * c + v,), (10 * p + 5 * c + v,), kt)
                    for v in range(5)
                ]
                for c in range(2)
            ]
            new = new_values(
                coef, mine, [[f_ref[p, c, v, :, at] for v in range(5)] for c in range(2)]
            )
            for c in range(2):
                for v in range(5):
                    i = 10 * p + 5 * c + v
                    x_out[p, c, v, :, at] = new[c][v]
                    if not last:
                        up_ref[2 * i : 2 * i + 2, at] = new[c][v][6:8, :]
                        down_ref[2 * i : 2 * i + 2, at] = new[c][v][0:2, :]
        return 0

    lax.fori_loop(0, tiles, one, 0)
    lax.fori_loop(0, tiles, two, 0)


def gather_kernel(pw_ref, x_ref, idx_ref, weight_ref, out_ref, table_ref, sum_ref):
    cells = x_ref.shape[-1]
    chunk = idx_ref.shape[-1]
    parts = idx_ref.shape[0]
    wide = 256
    groups = cells // wide
    for i in range(4):
        value = pw_ref[0] * x_ref[i // 2, i % 2, 0]
        for v in range(1, 5):
            value = value + pw_ref[v] * x_ref[i // 2, i % 2, v]
        for g in range(groups):
            part = value[:, g * wide : (g + 1) * wide]
            high = part.astype(jnp.bfloat16).astype(jnp.float32)
            at = (i * groups + g) * 8
            table_ref[at : at + 8, :] = high
            table_ref[32 * groups + at : 32 * groups + at + 8, :] = part - high
    table = table_ref[...].astype(jnp.bfloat16)
    sum_ref[...] = jnp.zeros_like(sum_ref)
    half = 32 * groups

    def one(d, _):
        idx = idx_ref[d]
        low = jnp.broadcast_to(idx & (wide - 1), (wide, chunk))
        hot = (lax.broadcasted_iota(jnp.int32, (wide, chunk), 0) == low).astype(jnp.float32).astype(jnp.bfloat16)
        both = jnp.dot(table, hot, preferred_element_type=jnp.float32)
        found = both[:half] + both[half:]
        top = jnp.broadcast_to(idx >> 8, (8, chunk))
        row = lax.broadcasted_iota(jnp.int32, (8, chunk), 0) * groups
        res = []
        for i in range(4):
            total = jnp.zeros((8, chunk), jnp.float32)
            for g in range(groups):
                at = (i * groups + g) * 8
                total = total + jnp.where(top == row + g, found[at : at + 8], 0.0)
            res.append(jnp.sum(total, axis=0, keepdims=True))
        res = jnp.concatenate(res, axis=0)
        out_ref[d, :, 0:chunk] = res
        sum_ref[...] += res * weight_ref[d]
        return 0

    lax.fori_loop(0, parts, one, 0)
    work = jnp.broadcast_to(jnp.sum(sum_ref[...], axis=1, keepdims=True), (4, LANES))
    for d in range(parts):
        out_ref[d, :, chunk : chunk + LANES] = work


def phase_kernel(table_ref, x_ref, out_ref, work_ref):
    parts = x_ref.shape[0]
    chunk = out_ref.shape[-1]
    rows = jnp.concatenate([x_ref[d] for d in range(parts)], axis=0)
    y = jnp.dot(table_ref[...], rows, precision=HIGHEST, preferred_element_type=jnp.float32)
    for d in range(parts):
        out_ref[d] = y[4 * d : 4 * d + 4, :chunk]
        work_ref[d] = y[4 * d : 4 * d + 4, chunk:]


def place_kernel(x_ref, out_ref):
    chunk = x_ref.shape[-1]
    for d in range(x_ref.shape[0]):
        for m in range(2):
            out_ref[m, :, d * chunk : (d + 1) * chunk] = x_ref[d, 2 * m : 2 * m + 2, :]


def phase_table(phase_index, blades):
    ids = jnp.arange(blades, dtype=jnp.int32)
    turns = ids[:, None] * phase_index[None, :] % blades
    angle = 2.0 * math.pi / blades * turns.astype(jnp.float32)
    cos, sin = jnp.cos(angle) / blades, jnp.sin(angle) / blades
    top = jnp.stack([cos, -sin], axis=2).reshape(blades, 2 * blades)
    bottom = jnp.stack([sin, cos], axis=2).reshape(blades, 2 * blades)
    return jnp.stack([top, bottom], axis=1).reshape(2 * blades, 2 * blades)


def per_device(
    previous,
    forcing,
    jacobians,
    coupling,
    diagonal,
    inertia,
    pressure_weights,
    surface_cells,
    modal_weights,
    phase_index,
):
    f32 = jnp.float32
    blades = phase_index.shape[0]
    cells = previous.shape[-1]
    entries = surface_cells.shape[0]
    devices = lax.axis_size("phase")
    count = lax.axis_size("space")
    here = lax.axis_index("space")
    forward = [(i, (i + 1) % count) for i in range(count)]
    backward = [((i + 1) % count, i) for i in range(count)]

    local_index = lax.dynamic_slice_in_dim(phase_index, lax.axis_index("phase") * 2, 2)
    angles = 2.0 * math.pi / blades * local_index.astype(f32)
    cos, sin = jnp.cos(angles), jnp.sin(angles)
    first, last = here == 0, here == count - 1
    turn = jnp.stack(
        [
            jnp.where(first, cos, 1.0),
            jnp.where(first, -sin, 0.0),
            jnp.where(last, cos, 1.0),
            jnp.where(last, sin, 0.0),
        ],
        axis=1,
    ).reshape(8)
    jac = jacobians.reshape(100)
    table = phase_table(phase_index, blades)

    coef, up, down = call(
        pack_kernel,
        "pack",
        [((6, 8, cells), f32), ((66, cells), f32), ((66, cells), f32)],
        [],
        1 << 20,
        previous,
        forcing,
        coupling,
        diagonal,
        inertia,
    )
    state = previous
    ghosts = ()
    steps = ITERS // WIDTH
    scratch = [pltpu.VMEM((20, 8, cells), f32)] * 3
    for step in range(steps):
        lo = lax.ppermute(up, "space", forward)
        hi = lax.ppermute(down, "space", backward)
        outs = [(previous.shape, f32)]
        if step < steps - 1:
            outs += [((40, cells), f32)] * 2
        if step == 0:
            outs += [((20, 8, cells), f32), ((6, 8, cells), f32)]
        got = call(
            functools.partial(sweep_kernel, step == 0, step == steps - 1),
            "sweeps",
            outs,
            scratch,
            20 << 20,
            jac,
            turn,
            state,
            forcing,
            coef,
            lo,
            hi,
            *ghosts,
            smem=2,
        )
        state = got[0]
        if step < steps - 1:
            up, down = got[1], got[2]
        if step == 0:
            ghosts = (got[3], got[4])

    chunk = entries // devices
    (mine,) = call(
        gather_kernel,
        "surface",
        [((devices, 4, chunk + LANES), f32)],
        [pltpu.VMEM((256, 256), f32), pltpu.VMEM((4, chunk), f32)],
        1 << 28,
        pressure_weights,
        state,
        surface_cells.reshape(devices, 1, chunk),
        modal_weights.reshape(devices, 1, chunk),
        smem=1,
    )
    every = lax.all_to_all(mine, "phase", 0, 0, tiled=True)
    turned, work = call(
        phase_kernel,
        "phases",
        [((devices, 4, chunk), f32), ((devices, 4, LANES), f32)],
        [],
        1 << 24,
        table,
        every,
    )
    work = lax.dynamic_index_in_dim(work, lax.axis_index("phase"), 0, keepdims=False)
    blocks = lax.all_to_all(turned, "phase", 0, 0, tiled=True)
    for bit in (1, 2, 4, 8):
        work = work + lax.ppermute(work, "space", [(i, i ^ bit) for i in range(count)])
    (influence,) = call(
        place_kernel, "place", [((2, 2, entries), f32)], [], 1 << 16, blocks
    )
    return state, influence, work[:, 0].reshape(2, 2)


def solution(mesh):
    in_specs = (
        P("phase", None, None, "space", None),
        P("phase", None, None, "space", None),
        P(),
        P(None, "space", None),
        P("space", None),
        P("space", None),
        P(),
        P("space"),
        P("space"),
        P(),
    )
    out_specs = (P("phase", None, None, "space", None), P("phase", None, "space"), P("phase", None))
    return jax.shard_map(
        per_device, mesh=mesh, in_specs=in_specs, out_specs=out_specs, check_vma=False
    )
```

```python
import functools
import math

import jax
import jax.numpy as jnp
from jax import lax
from jax.experimental import pallas as pl
from jax.experimental.pallas import tpu as pltpu
from jax.sharding import PartitionSpec as P

ITERS = 6
WIDTH = 2
RELAX = 0.8
LANES = 128
WIDE = 256
HIGHEST = lax.Precision.HIGHEST

VMEM = pl.BlockSpec(memory_space=pltpu.VMEM)
SMEM = pl.BlockSpec(memory_space=pltpu.SMEM)
HBM = pl.BlockSpec(memory_space=pl.ANY)


def call(kernel, name, out_shapes, scratch, flops, operands, in_specs, out_specs=None):
    return pl.pallas_call(
        kernel,
        name=name,
        out_shape=[jax.ShapeDtypeStruct(s, d) for s, d in out_shapes],
        in_specs=in_specs,
        out_specs=out_specs or [VMEM] * len(out_shapes),
        scratch_shapes=scratch,
        compiler_params=pltpu.CompilerParams(vmem_limit_bytes=40 * 1024 * 1024),
        cost_estimate=pl.CostEstimate(
            flops=flops, bytes_accessed=1 << 20, transcendentals=0
        ),
    )(*operands)


def pack_kernel(
    x_hbm, f_hbm, cpl_hbm, diag_hbm, inert_hbm, coef_ref, up_ref, down_ref, x_ref, f_ref, diag_ref, inert_ref, sems
):
    copies = [
        pltpu.make_async_copy(src, dst, sems.at[i])
        for i, (src, dst) in enumerate(
            [(x_hbm.at[p, c], x_ref.at[p, c]) for p in range(2) for c in range(2)]
            + [
                (diag_hbm, diag_ref),
                (inert_hbm, inert_ref),
                (cpl_hbm, coef_ref.at[0:4]),
            ]
            + [(f_hbm.at[p, c], f_ref.at[p, c]) for p in range(2) for c in range(2)]
        )
    ]
    for copy in copies:
        copy.start()
    for copy in copies[0:4]:
        copy.wait()
    for i in range(20):
        p, c, v = i // 10, i // 5 % 2, i % 5
        up_ref[2 * i : 2 * i + 2, :] = x_ref[p, c, v, 6:8, :]
        down_ref[2 * i : 2 * i + 2, :] = x_ref[p, c, v, 0:2, :]
    for copy in copies[4:7]:
        copy.wait()
    diag = diag_ref[...]
    inert = inert_ref[...]
    scale = RELAX / (diag * diag + inert * inert)
    coef_ref[4] = diag * scale
    coef_ref[5] = inert * scale
    for i in range(6):
        up_ref[60 + i : 61 + i, :] = coef_ref[i, 7:8, :]
        down_ref[60 + i : 61 + i, :] = coef_ref[i, 0:1, :]
    for copy in copies[7:11]:
        copy.wait()
    for i in range(20):
        p, c, v = i // 10, i // 5 % 2, i % 5
        up_ref[40 + i : 41 + i, :] = f_ref[p, c, v, 7:8, :]
        down_ref[40 + i : 41 + i, :] = f_ref[p, c, v, 0:1, :]


def tables_kernel(jac_ref, one_ref, two_ref, a_ref):
    j = lax.broadcasted_iota(jnp.int32, (8, 64), 0)
    k = lax.broadcasted_iota(jnp.int32, (8, 64), 1)
    k1 = lax.broadcasted_iota(jnp.int32, (1, 64), 1)

    def own(low, high):
        def column(d, w):
            if d == 0:
                return jnp.where(j == 0, low(w), 8 * w + j - 1)
            if d == 1:
                return jnp.where(j == 7, high(w), 8 * w + j + 1)
            return 8 * w + j

        return column

    def fill(column):
        for d in range(4):
            masks = [k == column(d, w) for w in range(5)]
            for v in range(5):
                total = jnp.zeros((8, 64), jnp.float32)
                for w in range(5):
                    total = jnp.where(masks[w], jac_ref[d, v, w], total)
                a_ref[40 * d + 8 * v : 40 * d + 8 * v + 8, :] = total

    def split(out_ref, rows):
        a = a_ref[0:rows, :]
        high = a.astype(jnp.bfloat16).astype(jnp.float32)
        out_ref[...] = jnp.concatenate([high, high, a - high], axis=1).astype(jnp.bfloat16)

    fill(own(lambda w: 41 + 2 * w, lambda w: 50 + 2 * w))
    a_ref[160:224, :] = jnp.zeros((64, 64), jnp.float32)
    for d in range(4):
        for g in range(2):
            start, stride = (
                ((40, 2), (0, 8), (41, 2), (41, 2)),
                ((7, 8), (51, 2), (50, 2), (50, 2)),
            )[g][d]
            for v in range(5):
                total = jnp.zeros((1, 64), jnp.float32)
                for w in range(5):
                    total = jnp.where(k1 == start + stride * w, jac_ref[d, v, w], total)
                at = 160 + 16 * d + 5 * g + v
                a_ref[at : at + 1, :] = total
    split(one_ref, 224)
    fill(own(lambda w: 40 + w, lambda w: 45 + w))
    split(two_ref, 160)


def hot_kernel(idx_ref, hot_ref):
    shape = hot_ref.shape[1:]

    def one(d, _):
        low = jnp.broadcast_to(idx_ref[d] & (WIDE - 1), shape)
        hot = jnp.where(lax.broadcasted_iota(jnp.int32, shape, 0) == low, 1.0, 0.0)
        hot_ref[d] = hot.astype(jnp.bfloat16)
        return 0

    lax.fori_loop(0, hot_ref.shape[0], one, 0)


def sweep_kernel(first, last, rot_ref, x_ref, f_ref, coef_ref, lo_ref, hi_ref, one_ref, two_ref, *refs):
    if last:
        gf_ref, gcoef_ref, pw_ref, idx_ref, hot_ref, weight_ref, x_hbm, out_ref, *refs = refs
        x_out, table_ref, sum_ref, sem, b_ref, y_ref = refs
    elif first:
        x_out, up_ref, down_ref, gf_ref, gcoef_ref, b_ref, y_ref = refs
    else:
        gf_ref, gcoef_ref, x_out, up_ref, down_ref, b_ref, y_ref = refs
    cells = x_ref.shape[-1]

    def turned(ref, at_re, at_im, rows, c, s):
        a = ref[at_re : at_re + rows, :]
        b = ref[at_im : at_im + rows, :]
        return c * a - s * b, s * a + c * b

    if first:
        for i in range(6):
            gcoef_ref[i, 0:5, :] = jnp.broadcast_to(lo_ref[60 + i : 61 + i, :], (5, cells))
            gcoef_ref[i, 5:16, :] = jnp.broadcast_to(hi_ref[60 + i : 61 + i, :], (11, cells))

    lane = lax.broadcasted_iota(jnp.int32, (8, cells), 1)

    def before(y):
        return jnp.where(lane == 0, 0.0, pltpu.roll(y, 1, 1))

    def after(y):
        return jnp.where(lane == cells - 1, 0.0, pltpu.roll(y, cells - 1, 1))

    def products(table_ref, rows):
        table = table_ref[...]
        for c in range(2):
            b = b_ref[c]
            high = b.astype(jnp.bfloat16)
            low = (b - high.astype(jnp.float32)).astype(jnp.bfloat16)
            y_ref[c, 0:rows, :] = jnp.dot(
                table,
                jnp.concatenate([high, low, high], axis=0),
                preferred_element_type=jnp.float32,
            )

    def renew(coef, forcing, old, at, stride):
        rest = []
        for c in range(2):
            y = [y_ref[c, at + stride * d : at + stride * d + 8, :] for d in range(4)]
            rest.append(
                forcing[c] - coef[0] * y[0] - coef[1] * y[1] - coef[2] * before(y[2]) - coef[3] * after(y[3])
            )
        re, im = rest
        return (
            (1.0 - RELAX) * old[0] + (coef[4] * re + coef[5] * im),
            (1.0 - RELAX) * old[1] + (coef[4] * im - coef[5] * re),
        )

    for p in range(2):
        lo_c, lo_s = rot_ref[4 * p], rot_ref[4 * p + 1]
        hi_c, hi_s = rot_ref[4 * p + 2], rot_ref[4 * p + 3]
        re, im = 20 * p, 20 * p + 10
        lo = turned(lo_ref, re, im, 10, lo_c, lo_s)
        hi = turned(hi_ref, re, im, 10, hi_c, hi_s)
        for c in range(2):
            b_ref[c, 0:40, :] = x_ref[p, c].reshape(40, cells)
            b_ref[c, 40:50, :] = lo[c]
            b_ref[c, 50:60, :] = hi[c]
            b_ref[c, 60:64, :] = jnp.zeros((4, cells), jnp.float32)
        if first:
            lo = turned(lo_ref, 40 + re // 2, 40 + im // 2, 5, lo_c, lo_s)
            hi = turned(hi_ref, 40 + re // 2, 40 + im // 2, 5, hi_c, hi_s)
            for c in range(2):
                gf_ref[p, c, 0:5, :] = lo[c]
                gf_ref[p, c, 5:10, :] = hi[c]
                gf_ref[p, c, 10:16, :] = jnp.zeros((6, cells), jnp.float32)

        products(one_ref, 224)
        ghost = []
        for c in range(2):
            old = [b_ref[c, 41 + 2 * v : 42 + 2 * v, :] for v in range(5)]
            old += [b_ref[c, 50 + 2 * v : 51 + 2 * v, :] for v in range(5)]
            ghost.append(jnp.concatenate(old + [jnp.zeros((6, cells), jnp.float32)], axis=0))
        for half in range(2):
            rows = slice(8 * half, 8 * half + 8)
            new = renew(
                [gcoef_ref[i, rows, :] for i in range(6)],
                [gf_ref[p, c, rows, :] for c in range(2)],
                [ghost[c][rows] for c in range(2)],
                160 + 8 * half,
                16,
            )
            for c in range(2):
                b_ref[c, 40 + 8 * half : 48 + 8 * half, :] = new[c]
        coef = [coef_ref[i] for i in range(6)]
        for v in range(5):
            new = renew(
                coef,
                [f_ref[p, c, v] for c in range(2)],
                [b_ref[c, 8 * v : 8 * v + 8, :] for c in range(2)],
                8 * v,
                40,
            )
            for c in range(2):
                b_ref[c, 8 * v : 8 * v + 8, :] = new[c]
        for c in range(2):
            b_ref[c, 50:64, :] = jnp.zeros((14, cells), jnp.float32)

        products(two_ref, 160)
        for v in range(5):
            new = renew(
                coef,
                [f_ref[p, c, v] for c in range(2)],
                [b_ref[c, 8 * v : 8 * v + 8, :] for c in range(2)],
                8 * v,
                40,
            )
            for c in range(2):
                x_out[p, c, v] = new[c]
                if not last:
                    i = 10 * p + 5 * c + v
                    up_ref[2 * i : 2 * i + 2, :] = new[c][6:8, :]
                    down_ref[2 * i : 2 * i + 2, :] = new[c][0:2, :]
    if last:
        copy = pltpu.make_async_copy(x_out, x_hbm, sem)
        copy.start()
        surface(pw_ref, x_out, idx_ref, hot_ref, weight_ref, out_ref, table_ref, sum_ref)
        copy.wait()


def surface(pw_ref, x_ref, idx_ref, hot_ref, weight_ref, out_ref, table_ref, sum_ref):
    cells = x_ref.shape[-1]
    chunk = idx_ref.shape[-1]
    parts = idx_ref.shape[0]
    groups = cells // WIDE
    half = 32 * groups
    for i in range(4):
        value = pw_ref[0] * x_ref[i // 2, i % 2, 0]
        for v in range(1, 5):
            value = value + pw_ref[v] * x_ref[i // 2, i % 2, v]
        for g in range(groups):
            part = value[:, g * WIDE : (g + 1) * WIDE]
            high = part.astype(jnp.bfloat16).astype(jnp.float32)
            at = (i * groups + g) * 8
            table_ref[at : at + 8, :] = high
            table_ref[half + at : half + at + 8, :] = part - high
    table = table_ref[...].astype(jnp.bfloat16)
    sum_ref[...] = jnp.zeros_like(sum_ref)

    def one(d, _):
        both = jnp.dot(table, hot_ref[d], preferred_element_type=jnp.float32)
        found = both[:half] + both[half:]
        top = jnp.broadcast_to(idx_ref[d] >> 8, (8, chunk))
        row = lax.broadcasted_iota(jnp.int32, (8, chunk), 0) * groups
        masks = [top == row + g for g in range(groups)]
        res = []
        for i in range(4):
            total = jnp.zeros((8, chunk), jnp.float32)
            for g in range(groups):
                at = (i * groups + g) * 8
                total = jnp.where(masks[g], found[at : at + 8], total)
            res.append(jnp.sum(total, axis=0, keepdims=True))
        res = jnp.concatenate(res, axis=0)
        out_ref[d, :, 0:chunk] = res
        sum_ref[...] += res * weight_ref[d]
        return 0

    lax.fori_loop(0, parts, one, 0)
    work = jnp.broadcast_to(jnp.sum(sum_ref[...], axis=1, keepdims=True), (4, LANES))
    for d in range(parts):
        out_ref[d, :, chunk : chunk + LANES] = work


def phase_kernel(table_ref, x_ref, out_ref, work_ref):
    parts = x_ref.shape[0]
    chunk = out_ref.shape[-1]
    rows = jnp.concatenate([x_ref[d] for d in range(parts)], axis=0)
    y = jnp.dot(table_ref[...], rows, precision=HIGHEST, preferred_element_type=jnp.float32)
    for d in range(parts):
        out_ref[d] = y[4 * d : 4 * d + 4, :chunk]
        work_ref[d] = y[4 * d : 4 * d + 4, chunk:]


def place_kernel(x_ref, work_ref, out_ref, modal_ref):
    chunk = x_ref.shape[-1]
    for d in range(x_ref.shape[0]):
        for m in range(2):
            out_ref[m, :, d * chunk : (d + 1) * chunk] = x_ref[d, 2 * m : 2 * m + 2, :]
    lane = lax.broadcasted_iota(jnp.int32, (1, 2), 1)
    for m in range(2):
        re = jnp.broadcast_to(work_ref[2 * m : 2 * m + 1, 0:1], (1, 2))
        im = jnp.broadcast_to(work_ref[2 * m + 1 : 2 * m + 2, 0:1], (1, 2))
        modal_ref[m : m + 1, :] = jnp.where(lane == 0, re, im)


def phase_table(phase_index, blades):
    ids = jnp.arange(blades, dtype=jnp.int32)
    turns = ids[:, None] * phase_index[None, :] % blades
    angle = 2.0 * math.pi / blades * turns.astype(jnp.float32)
    cos, sin = jnp.cos(angle) / blades, jnp.sin(angle) / blades
    top = jnp.stack([cos, -sin], axis=2).reshape(blades, 2 * blades)
    bottom = jnp.stack([sin, cos], axis=2).reshape(blades, 2 * blades)
    return jnp.stack([top, bottom], axis=1).reshape(2 * blades, 2 * blades)


def per_device(
    previous,
    forcing,
    jacobians,
    coupling,
    diagonal,
    inertia,
    pressure_weights,
    surface_cells,
    modal_weights,
    phase_index,
):
    f32 = jnp.float32
    blades = phase_index.shape[0]
    cells = previous.shape[-1]
    entries = surface_cells.shape[0]
    devices = lax.axis_size("phase")
    count = lax.axis_size("space")
    here = lax.axis_index("space")
    forward = [(i, (i + 1) % count) for i in range(count)]
    backward = [((i + 1) % count, i) for i in range(count)]

    local_index = lax.dynamic_slice_in_dim(phase_index, lax.axis_index("phase") * 2, 2)
    angles = 2.0 * math.pi / blades * local_index.astype(f32)
    cos, sin = jnp.cos(angles), jnp.sin(angles)
    first, last = here == 0, here == count - 1
    turn = jnp.stack(
        [
            jnp.where(first, cos, 1.0),
            jnp.where(first, -sin, 0.0),
            jnp.where(last, cos, 1.0),
            jnp.where(last, sin, 0.0),
        ],
        axis=1,
    ).reshape(8)
    table = phase_table(phase_index, blades)
    chunk = entries // devices
    idx = surface_cells.reshape(devices, 1, chunk)

    coef, up, down = call(
        pack_kernel,
        "pack",
        [((6, 8, cells), f32), ((66, cells), f32), ((66, cells), f32)],
        [
            pltpu.VMEM(previous.shape, f32),
            pltpu.VMEM(previous.shape, f32),
            pltpu.VMEM((8, cells), f32),
            pltpu.VMEM((8, cells), f32),
            pltpu.SemaphoreType.DMA((11,)),
        ],
        1 << 20,
        [previous, forcing, coupling, diagonal, inertia],
        [HBM] * 5,
    )
    one, two = call(
        tables_kernel,
        "tables",
        [((224, 192), jnp.bfloat16), ((160, 192), jnp.bfloat16)],
        [pltpu.VMEM((224, 64), f32)],
        1 << 20,
        [jacobians],
        [SMEM],
    )
    (hot,) = call(
        hot_kernel,
        "onehot",
        [((devices, WIDE, chunk), jnp.bfloat16)],
        [],
        8 << 20,
        [idx],
        [VMEM],
    )
    state = previous
    steps = ITERS // WIDTH
    work_space = [pltpu.VMEM((2, 64, cells), f32), pltpu.VMEM((2, 224, cells), f32)]
    ghosts = ()
    for step in range(steps):
        lo = lax.ppermute(up, "space", forward)
        hi = lax.ppermute(down, "space", backward)
        operands = [turn, state, forcing, coef, lo, hi, one, two, *ghosts]
        specs = [SMEM] + [VMEM] * (len(operands) - 1)
        kernel = functools.partial(sweep_kernel, step == 0, step == steps - 1)
        if step < steps - 1:
            outs = [(previous.shape, f32)] + [((40, cells), f32)] * 2
            if step == 0:
                outs += [((2, 2, 16, cells), f32), ((6, 16, cells), f32)]
            got = call(kernel, "sweeps", outs, work_space, 20 << 20, operands, specs)
            state, up, down = got[:3]
            if step == 0:
                ghosts = got[3:]
        else:
            state, mine = call(
                kernel,
                "sweeps_surface",
                [(previous.shape, f32), ((devices, 4, chunk + LANES), f32)],
                [
                    pltpu.VMEM(previous.shape, f32),
                    pltpu.VMEM((256, WIDE), f32),
                    pltpu.VMEM((4, chunk), f32),
                    pltpu.SemaphoreType.DMA,
                ]
                + work_space,
                40 << 20,
                operands
                + [pressure_weights, idx, hot, modal_weights.reshape(devices, 1, chunk)],
                specs + [SMEM] + [VMEM] * 3,
                [HBM, VMEM],
            )

    every = lax.all_to_all(mine, "phase", 0, 0, tiled=True)
    turned, work = call(
        phase_kernel,
        "phases",
        [((devices, 4, chunk), f32), ((devices, 4, LANES), f32)],
        [],
        1 << 24,
        [table, every],
        [VMEM] * 2,
    )
    work = lax.dynamic_index_in_dim(work, lax.axis_index("phase"), 0, keepdims=False)
    blocks = lax.all_to_all(turned, "phase", 0, 0, tiled=True)

    def across(bits):
        return lax.ppermute(work, "space", [(i, i ^ bits) for i in range(count)])

    work = (work + across(4)) + (across(8) + across(12))
    work = work + across(2)
    work = work + across(1)
    influence, modal_work = call(
        place_kernel,
        "place",
        [((2, 2, entries), f32), ((2, 2), f32)],
        [],
        1 << 16,
        [blocks, work],
        [VMEM] * 2,
    )
    return state, influence, modal_work


def solution(mesh):
    in_specs = (
        P("phase", None, None, "space", None),
        P("phase", None, None, "space", None),
        P(),
        P(None, "space", None),
        P("space", None),
        P("space", None),
        P(),
        P("space"),
        P("space"),
        P(),
    )
    out_specs = (P("phase", None, None, "space", None), P("phase", None, "space"), P("phase", None))
    return jax.shard_map(
        per_device, mesh=mesh, in_specs=in_specs, out_specs=out_specs, check_vma=False
    )
```

```python
import functools
import math

import jax
import jax.numpy as jnp
from jax import lax
from jax.experimental import pallas as pl
from jax.experimental.pallas import tpu as pltpu
from jax.sharding import PartitionSpec as P

ITERS = 6
WIDTH = 2
RELAX = 0.8
LANES = 128
WIDE = 256
HIGHEST = lax.Precision.HIGHEST

VMEM = pl.BlockSpec(memory_space=pltpu.VMEM)
SMEM = pl.BlockSpec(memory_space=pltpu.SMEM)
HBM = pl.BlockSpec(memory_space=pltpu.HBM)


def call(kernel, name, out_shapes, scratch, flops, operands, in_specs, out_specs=None):
    return pl.pallas_call(
        kernel,
        name=name,
        out_shape=[jax.ShapeDtypeStruct(s, d) for s, d in out_shapes],
        in_specs=in_specs,
        out_specs=out_specs or [VMEM] * len(out_shapes),
        scratch_shapes=scratch,
        compiler_params=pltpu.CompilerParams(vmem_limit_bytes=40 * 1024 * 1024),
        cost_estimate=pl.CostEstimate(
            flops=flops, bytes_accessed=1 << 20, transcendentals=0
        ),
    )(*operands)


def pack_kernel(
    x_hbm, f_hbm, cpl_hbm, diag_hbm, inert_hbm, coef_ref, up_ref, down_ref, x_ref, f_ref, diag_ref, inert_ref, sems
):
    copies = [
        pltpu.make_async_copy(src, dst, sems.at[i])
        for i, (src, dst) in enumerate(
            [(x_hbm.at[p, c], x_ref.at[p, c]) for p in range(2) for c in range(2)]
            + [
                (diag_hbm, diag_ref),
                (inert_hbm, inert_ref),
                (cpl_hbm, coef_ref.at[0:4]),
            ]
            + [(f_hbm.at[p, c], f_ref.at[p, c]) for p in range(2) for c in range(2)]
        )
    ]
    for copy in copies:
        copy.start()
    for i in range(4):
        p, c = i // 2, i % 2
        copies[i].wait()
        for v in range(5):
            for r in range(2):
                at = 8 * v + 4 * p + 2 * r + c
                up_ref[at : at + 1, :] = x_ref[p, c, v, 6 + r : 7 + r, :]
                down_ref[at : at + 1, :] = x_ref[p, c, v, r : r + 1, :]
    for copy in copies[4:7]:
        copy.wait()
    diag = diag_ref[...]
    inert = inert_ref[...]
    scale = RELAX / (diag * diag + inert * inert)
    coef_ref[4] = diag * scale
    coef_ref[5] = inert * scale
    for i in range(6):
        up_ref[60 + i : 61 + i, :] = coef_ref[i, 7:8, :]
        down_ref[60 + i : 61 + i, :] = coef_ref[i, 0:1, :]
    for i in range(4):
        p, c = i // 2, i % 2
        copies[7 + i].wait()
        for v in range(5):
            at = 40 + 4 * v + 2 * p + c
            up_ref[at : at + 1, :] = f_ref[p, c, v, 7:8, :]
            down_ref[at : at + 1, :] = f_ref[p, c, v, 0:1, :]


def tables_kernel(jac_ref, rot_ref, own_ref, plain_ref, lo_ref, hi_ref):
    def split(a):
        high = a.astype(jnp.bfloat16).astype(jnp.float32)
        return jnp.concatenate([high, high, a - high], axis=1).astype(jnp.bfloat16)

    j = lax.broadcasted_iota(jnp.int32, (8, 48), 0)
    k = lax.broadcasted_iota(jnp.int32, (8, 48), 1)
    tiles = []
    for d in range(4):
        near = (jnp.where(j == 0, -99, j - 1), jnp.where(j == 7, -99, j + 1), j, j)[d]
        for v in range(5):
            total = jnp.zeros((8, 48), jnp.float32)
            for w in range(5):
                total = jnp.where(k == 8 * w + near, jac_ref[d, v, w], total)
            tiles.append(total)
    own_ref[...] = split(jnp.concatenate(tiles, axis=0))

    row = lax.broadcasted_iota(jnp.int32, (8, 80), 0)
    col = lax.broadcasted_iota(jnp.int32, (8, 80), 1)
    second = col >= 40
    inner = jnp.where(second, col - 40, col)
    var = inner >> 3
    from_row = jnp.where(second, 2, 0) + ((inner >> 1) & 1)
    to_row = 1 + ((row >> 1) & 1)
    part, from_part = row & 1, inner & 1
    phase = row >> 2
    same_phase = phase == ((inner >> 2) & 1)

    def turn(c, s):
        cos = jnp.where(phase == 0, rot_ref[c], rot_ref[4 + c])
        sin = jnp.where(phase == 0, rot_ref[s], rot_ref[4 + s])
        return jnp.where(part == from_part, cos, jnp.where(part == 0, -sin, sin))

    straight = jnp.where(part == from_part, 1.0, 0.0)
    factors = (
        straight,
        jnp.where(second, straight, turn(0, 1)),
        jnp.where(second, turn(2, 3), straight),
    )
    tiles = [[], [], []]
    for d in range(5):
        near = to_row + (-1, 1, 0, 0, 0)[d]
        here = same_phase & (from_row == near)
        for v in range(5):
            if d == 4:
                value = jnp.where(var == v, 1.0 - RELAX, 0.0)
            else:
                value = jnp.zeros((8, 80), jnp.float32)
                for w in range(5):
                    value = jnp.where(var == w, jac_ref[d, v, w], value)
            value = jnp.where(here, value, 0.0)
            for i in range(3):
                tiles[i].append(value * factors[i])
    for i, ref in enumerate((plain_ref, lo_ref, hi_ref)):
        ref[...] = split(jnp.concatenate(tiles[i], axis=0))


def hot_kernel(idx_ref, weight_ref, hot_ref, cell_ref, sum_ref):
    shape = hot_ref.shape[1:]
    chunk = shape[1]
    groups = cell_ref.shape[1] // WIDE
    rows = 8 * groups
    sum_ref[...] = jnp.zeros_like(sum_ref)

    def one(d, _):
        idx = idx_ref[d]
        low = jnp.broadcast_to(idx & (WIDE - 1), shape)
        hot = jnp.where(lax.broadcasted_iota(jnp.int32, shape, 0) == low, 1.0, 0.0).astype(jnp.bfloat16)
        hot_ref[d] = hot
        top = jnp.broadcast_to(idx >> 8, (rows, chunk))
        row = lax.broadcasted_iota(jnp.int32, (rows, chunk), 0)
        weight = jnp.where(top == (row & 7) * groups + (row >> 3), jnp.broadcast_to(weight_ref[d], (rows, chunk)), 0.0)
        parts = []
        for _ in range(3):
            part = weight.astype(jnp.bfloat16).astype(jnp.float32)
            parts.append(part)
            weight = weight - part
        sum_ref[...] += lax.dot_general(
            jnp.concatenate(parts, axis=0).astype(jnp.bfloat16),
            hot,
            (((1,), (1,)), ((), ())),
            preferred_element_type=jnp.float32,
        )
        return 0

    lax.fori_loop(0, hot_ref.shape[0], one, 0, unroll=2)
    for g in range(groups):
        total = sum_ref[8 * g : 8 * g + 8, :]
        for i in range(1, 3):
            total = total + sum_ref[rows * i + 8 * g : rows * i + 8 * g + 8, :]
        cell_ref[:, g * WIDE : (g + 1) * WIDE] = total


def multiply(table, b):
    high = b.astype(jnp.bfloat16)
    low = (b - high.astype(jnp.float32)).astype(jnp.bfloat16)
    return jnp.dot(
        table,
        jnp.concatenate([high, low, high], axis=0),
        preferred_element_type=jnp.float32,
    )


def remainder(y, coef, forcing):
    cells = forcing.shape[-1]
    lane = lax.broadcasted_iota(jnp.int32, (8, cells), 1)
    before = jnp.where(lane == 0, 0.0, pltpu.roll(y[2], 1, 1))
    after = jnp.where(lane == cells - 1, 0.0, pltpu.roll(y[3], cells - 1, 1))
    return forcing - coef[0] * y[0] - coef[1] * y[1] - coef[2] * before - coef[3] * after


def pre_kernel(first, x_ref, f_ref, coef_ref, own_ref, *refs):
    if first:
        next_ref, mid_ref, ef_ref, ecoef_ref, b_ref, y_ref = refs
    else:
        edge_refs, (next_ref, mid_ref, b_ref, y_ref) = refs[:2], refs[2:]
    cells = x_ref.shape[-1]
    if first:
        row = lax.broadcasted_iota(jnp.int32, (8, cells), 0)
        for h in range(2):
            for i in range(6):
                tile = jnp.where(
                    (row >> 1) & 1 == 0,
                    jnp.broadcast_to(coef_ref[i, 6 * h : 6 * h + 1, :], (8, cells)),
                    jnp.broadcast_to(coef_ref[i, 6 * h + 1 : 6 * h + 2, :], (8, cells)),
                )
                ecoef_ref[h, i] = jnp.where(row & 1 == 0, tile, -tile) if i == 5 else tile
            for n in range(20):
                p, c, v = n // 10, n // 5 % 2, n % 5
                for r in range(2):
                    at = 4 * p + 2 * r + c
                    ef_ref[h, v, at : at + 1, :] = f_ref[p, c, v, 6 * h + r : 6 * h + r + 1, :]
    for c in range(2):
        b_ref[c, 40:48, :] = jnp.zeros((8, cells), jnp.float32)
    coef = [coef_ref[i] for i in range(6)]
    for p in range(2):
        for c in range(2):
            b_ref[c, 0:40, :] = x_ref[p, c].reshape(40, cells)
            if not first:
                for h in range(2):
                    for v in range(5):
                        for r in range(2):
                            at, to = 8 * v + 4 * p + 2 * r + c, 8 * v + 6 * h + r
                            b_ref[c, to : to + 1, :] = edge_refs[h][at : at + 1, :]
        for sweep in range(2):
            for c in range(2):
                y_ref[c] = multiply(own_ref[...], b_ref[c])
            for v in range(5):
                re, im = (
                    remainder(
                        [y_ref[c, 40 * d + 8 * v : 40 * d + 8 * v + 8, :] for d in range(4)],
                        coef,
                        f_ref[p, c, v],
                    )
                    for c in range(2)
                )
                add = (coef[4] * re + coef[5] * im, coef[4] * im - coef[5] * re)
                for c in range(2):
                    new = (1.0 - RELAX) * b_ref[c, 8 * v : 8 * v + 8, :] + add[c]
                    if sweep == 0:
                        b_ref[c, 8 * v : 8 * v + 8, :] = new
                        for h in range(2):
                            for r in range(2):
                                at = 8 * v + 4 * p + 2 * r + c
                                mid_ref[h, at : at + 1, :] = new[4 * h + r + 1 : 4 * h + r + 2, :]
                    else:
                        next_ref[p, c, v] = new


def post_kernel(first, last, rot_ref, plain_ref, lo_turn_ref, hi_turn_ref, ef_ref, ecoef_ref, lo_ref, hi_ref, up_ref, down_ref, mid_ref, *refs):
    if first:
        down_out, up_out, gf_ref, gcoef_ref = refs
    elif last:
        gf_ref, gcoef_ref, cell_ref, part_work_ref, pw_ref, down_out, up_out, press_ref, work_ref = refs
    else:
        gf_ref, gcoef_ref, down_out, up_out = refs
    cells = lo_ref.shape[-1]
    row = lax.broadcasted_iota(jnp.int32, (8, cells), 0)

    if first:
        for h in range(2):
            rows = (lo_ref, down_ref) if h == 0 else (up_ref, hi_ref)
            for i in range(6):
                tile = jnp.where(
                    (row >> 1) & 1 == 0,
                    jnp.broadcast_to(rows[0][60 + i : 61 + i, :], (8, cells)),
                    jnp.broadcast_to(rows[1][60 + i : 61 + i, :], (8, cells)),
                )
                gcoef_ref[h, i] = jnp.where(row & 1 == 0, tile, -tile) if i == 5 else tile
            ghost, base = (lo_ref, 0) if h == 0 else (hi_ref, 2)
            for v in range(5):
                for p in range(2):
                    cos, sin = rot_ref[4 * p + base], rot_ref[4 * p + base + 1]
                    at = 40 + 4 * v + 2 * p
                    re = ghost[at : at + 1, :]
                    im = ghost[at + 1 : at + 2, :]
                    turned = (cos * re - sin * im, sin * re + cos * im)
                    to = 4 * p + 2 * h
                    gf_ref[h, v, to : to + 1, :] = turned[0]
                    gf_ref[h, v, to + 1 : to + 2, :] = turned[1]
                    to = 4 * p + 2 - 2 * h
                    gf_ref[h, v, to : to + 2, :] = (down_ref if h == 0 else up_ref)[at : at + 2, :]

    def sweep(table, b, coef, forcing):
        y = multiply(table[...], b)
        new = []
        for v in range(5):
            at = [40 * d + 8 * v for d in range(5)]
            rest = remainder([y[at[d] : at[d] + 8] for d in range(4)], coef, forcing[v])
            partner = jnp.where(row & 1 == 0, pltpu.roll(rest, 7, 0), pltpu.roll(rest, 1, 0))
            new.append(y[at[4] : at[4] + 8] + coef[4] * rest + coef[5] * partner)
        return jnp.concatenate(new, axis=0)

    mids = []
    for h in range(2):
        pair = (up_ref, hi_ref) if h else (lo_ref, down_ref)
        mids.append(
            sweep(
                hi_turn_ref if h else lo_turn_ref,
                jnp.concatenate([ref[0:40, :] for ref in pair], axis=0),
                [gcoef_ref[h, i] for i in range(6)],
                [gf_ref[h, v] for v in range(5)],
            )
        )
    for h in range(2):
        new = sweep(
            plain_ref,
            jnp.concatenate([mid_ref[1], mids[1]] if h else [mids[0], mid_ref[0]], axis=0),
            [ecoef_ref[h, i] for i in range(6)],
            [ef_ref[h, v] for v in range(5)],
        )
        (up_out if h else down_out)[...] = new
        if last:
            press = pw_ref[0] * new[0:8]
            for v in range(1, 5):
                press = press + pw_ref[v] * new[8 * v : 8 * v + 8]
            press_ref[h] = press
            weight = jnp.where(
                (row >> 1) & 1 == 0,
                jnp.broadcast_to(cell_ref[6 * h : 6 * h + 1, :], (8, cells)),
                jnp.broadcast_to(cell_ref[6 * h + 1 : 6 * h + 2, :], (8, cells)),
            )
            work = weight * press if h == 0 else work + weight * press
    if last:
        work = jnp.broadcast_to(jnp.sum(work, axis=1, keepdims=True), (8, LANES))
        both = work + pltpu.roll(work, 6, 0)
        work_ref[0:2, :] = both[0:2] + part_work_ref[0:2, :]
        work_ref[2:4, :] = both[4:6] + part_work_ref[2:4, :]


def inner_kernel(pw_ref, x_ref, idx_ref, hot_ref, cell_ref, out_ref, work_ref, table_ref):
    cells = x_ref.shape[-1]
    chunk = idx_ref.shape[-1]
    parts = idx_ref.shape[0]
    groups = cells // WIDE
    half = 16 * groups
    row = lax.broadcasted_iota(jnp.int32, (8, cells), 0)
    kept = (row >= 2) & (row < 6)
    press = []
    for i in range(4):
        value = pw_ref[0] * x_ref[i // 2, i % 2, 0]
        for v in range(1, 5):
            value = value + pw_ref[v] * x_ref[i // 2, i % 2, v]
        value = jnp.where(kept, value, 0.0)
        press.append(value)
        work = jnp.sum(jnp.sum(value * cell_ref[...], axis=1, keepdims=True), axis=0, keepdims=True)
        work_ref[i : i + 1, :] = jnp.broadcast_to(work, (1, LANES))
    for i in range(2):
        value = press[2 * i] + pltpu.roll(press[2 * i + 1], 4, 0)
        high = value.astype(jnp.bfloat16).astype(jnp.float32)
        for g in range(groups):
            at = (i * groups + g) * 8
            table_ref[at : at + 8, :] = high[:, g * WIDE : (g + 1) * WIDE]
            table_ref[half + at : half + at + 8, :] = (value - high)[:, g * WIDE : (g + 1) * WIDE]
    table = table_ref[...].astype(jnp.bfloat16)
    row = lax.broadcasted_iota(jnp.int32, (8, chunk), 0)
    place = jnp.where((row >= 2) & (row < 6), row, (row + 4) & 7) * groups
    mine = (row >= 2) & (row < 6)

    def one(d, _):
        both = jnp.dot(table, hot_ref[d], preferred_element_type=jnp.float32)
        found = both[:half] + both[half:]
        top = jnp.broadcast_to(idx_ref[d] >> 8, (8, chunk))
        res = []
        for i in range(2):
            total = jnp.zeros((8, chunk), jnp.float32)
            for g in range(groups):
                at = (i * groups + g) * 8
                total = jnp.where(top == place + g, found[at : at + 8], total)
            res.append(jnp.sum(jnp.where(mine, total, 0.0), axis=0, keepdims=True))
            res.append(jnp.sum(jnp.where(mine, 0.0, total), axis=0, keepdims=True))
        out_ref[d] = jnp.concatenate(res, axis=0)
        return 0

    lax.fori_loop(0, parts, one, 0, unroll=4)


def surface_kernel(press_ref, idx_ref, hot_ref, inner_ref, work_ref, out_ref):
    cells = press_ref.shape[-1]
    chunk = idx_ref.shape[-1]
    parts = idx_ref.shape[0]
    groups = cells // WIDE
    half = 16 * groups
    tiles = [press_ref[h, :, g * WIDE : (g + 1) * WIDE] for h in range(2) for g in range(groups)]
    value = jnp.concatenate(tiles, axis=0)
    high = value.astype(jnp.bfloat16)
    low = (value - high.astype(jnp.float32)).astype(jnp.bfloat16)
    table = jnp.concatenate([high, low], axis=0)
    row = lax.broadcasted_iota(jnp.int32, (8, chunk), 0)
    place = ((row >> 1) & 1) * groups

    def one(d, _):
        both = jnp.dot(table, hot_ref[d], preferred_element_type=jnp.float32)
        found = both[:half] + both[half:]
        top = jnp.broadcast_to(idx_ref[d] >> 8, (8, chunk))
        total = jnp.zeros((8, chunk), jnp.float32)
        for h in range(2):
            for g in range(groups):
                at = (h * groups + g) * 8
                total = jnp.where(top == place + (6 * h * groups + g), found[at : at + 8], total)
        total = total + pltpu.roll(total, 6, 0)
        out_ref[d, 0:2, 0:chunk] = inner_ref[d, 0:2, :] + total[0:2]
        out_ref[d, 2:4, 0:chunk] = inner_ref[d, 2:4, :] + total[4:6]
        out_ref[d, :, chunk : chunk + LANES] = work_ref[...]
        return 0

    lax.fori_loop(0, parts, one, 0, unroll=4)


def merge_kernel(x_ref, down_ref, up_ref, out_ref):
    for n in range(20):
        p, c, v = n // 10, n // 5 % 2, n % 5
        out_ref[p, c, v] = x_ref[p, c, v]
        for h, ref in enumerate((down_ref, up_ref)):
            for r in range(2):
                at, to = 8 * v + 4 * p + 2 * r + c, 6 * h + r
                out_ref[p, c, v, to : to + 1, :] = ref[at : at + 1, :]


def work_kernel(table_ref, x_ref, work_ref):
    chunk = x_ref.shape[-1] - LANES
    rows = jnp.concatenate([x_ref[d, :, chunk:] for d in range(x_ref.shape[0])], axis=0)
    work_ref[...] = jnp.dot(
        table_ref[...], rows, precision=HIGHEST, preferred_element_type=jnp.float32
    )


def phase_kernel(table_ref, x_ref, out_ref):
    parts = x_ref.shape[0]
    chunk = out_ref.shape[-1]
    rows = jnp.concatenate([x_ref[d, :, 0:chunk] for d in range(parts)], axis=0)
    y = jnp.dot(table_ref[...], rows, precision=HIGHEST, preferred_element_type=jnp.float32)
    for d in range(parts):
        out_ref[d] = y[4 * d : 4 * d + 4]


def place_kernel(x_ref, work_ref, out_ref, modal_ref):
    chunk = x_ref.shape[-1]
    for d in range(x_ref.shape[0]):
        for m in range(2):
            out_ref[m, :, d * chunk : (d + 1) * chunk] = x_ref[d, 2 * m : 2 * m + 2, :]
    lane = lax.broadcasted_iota(jnp.int32, (1, 2), 1)
    for m in range(2):
        re = jnp.broadcast_to(work_ref[2 * m : 2 * m + 1, 0:1], (1, 2))
        im = jnp.broadcast_to(work_ref[2 * m + 1 : 2 * m + 2, 0:1], (1, 2))
        modal_ref[m : m + 1, :] = jnp.where(lane == 0, re, im)


def phase_table(phase_index, blades):
    ids = jnp.arange(blades, dtype=jnp.int32)
    turns = ids[:, None] * phase_index[None, :] % blades
    angle = 2.0 * math.pi / blades * turns.astype(jnp.float32)
    cos, sin = jnp.cos(angle) / blades, jnp.sin(angle) / blades
    top = jnp.stack([cos, -sin], axis=2).reshape(blades, 2 * blades)
    bottom = jnp.stack([sin, cos], axis=2).reshape(blades, 2 * blades)
    return jnp.stack([top, bottom], axis=1).reshape(2 * blades, 2 * blades)


def per_device(
    previous,
    forcing,
    jacobians,
    coupling,
    diagonal,
    inertia,
    pressure_weights,
    surface_cells,
    modal_weights,
    phase_index,
):
    f32 = jnp.float32
    blades = phase_index.shape[0]
    cells = previous.shape[-1]
    entries = surface_cells.shape[0]
    devices = lax.axis_size("phase")
    count = lax.axis_size("space")
    here = lax.axis_index("space")
    forward = [(i, (i + 1) % count) for i in range(count)]
    backward = [((i + 1) % count, i) for i in range(count)]

    local_index = lax.dynamic_slice_in_dim(phase_index, lax.axis_index("phase") * 2, 2)
    angles = 2.0 * math.pi / blades * local_index.astype(f32)
    cos, sin = jnp.cos(angles), jnp.sin(angles)
    low_end, high_end = here == 0, here == count - 1
    turn = jnp.stack(
        [
            jnp.where(low_end, cos, 1.0),
            jnp.where(low_end, -sin, 0.0),
            jnp.where(high_end, cos, 1.0),
            jnp.where(high_end, sin, 0.0),
        ],
        axis=1,
    ).reshape(8)
    table = phase_table(phase_index, blades)
    chunk = entries // devices
    idx = surface_cells.reshape(devices, 1, chunk)

    coef, up, down, state, forcing = call(
        pack_kernel,
        "pack",
        [((6, 8, cells), f32), ((66, cells), f32), ((66, cells), f32)]
        + [(previous.shape, f32)] * 2,
        [
            pltpu.VMEM((8, cells), f32),
            pltpu.VMEM((8, cells), f32),
            pltpu.SemaphoreType.DMA((11,)),
        ],
        1 << 20,
        [
            pltpu.with_memory_space_constraint(a, pltpu.HBM)
            for a in (previous, forcing, coupling, diagonal, inertia)
        ],
        [HBM] * 5,
    )
    bf16 = jnp.bfloat16
    own, *tables = call(
        tables_kernel,
        "tables",
        [((160, 144), bf16)] + [((200, 240), bf16)] * 3,
        [],
        1 << 20,
        [jacobians, turn],
        [SMEM] * 2,
    )
    hot, cell_weight = call(
        hot_kernel,
        "onehot",
        [((devices, WIDE, chunk), bf16), ((8, cells), f32)],
        [pltpu.VMEM((96 * cells // 1024, WIDE), f32)],
        8 << 20,
        [idx, modal_weights.reshape(devices, 1, chunk)],
        [VMEM] * 2,
    )
    steps = ITERS // WIDTH
    edge_shape = (2, 5, 8, cells)
    for step in range(steps):
        first, last = step == 0, step == steps - 1
        lo = lax.ppermute(up, "space", forward)
        hi = lax.ppermute(down, "space", backward)
        operands = [state, forcing, coef, own] + ([] if first else [down, up])
        got = call(
            functools.partial(pre_kernel, first),
            "pre",
            [(previous.shape, f32), ((2, 40, cells), f32)]
            + ([(edge_shape, f32), ((2, 6, 8, cells), f32)] if first else []),
            [pltpu.VMEM((2, 48, cells), f32), pltpu.VMEM((2, 160, cells), f32)],
            40 << 20,
            operands,
            [VMEM] * len(operands),
        )
        state, mid = got[:2]
        if first:
            edges = got[2:]
            ghosts = ()
        if step == 1:
            mid, hot, cell_weight = lax.optimization_barrier((mid, hot, cell_weight))
        outs = [((40, cells), f32)] * 2
        operands = [turn, *tables, *edges, lo, hi, up, down, mid, *ghosts]
        specs = [SMEM] + [VMEM] * (len(operands) - 1)
        if first:
            outs += [(edge_shape, f32), ((2, 6, 8, cells), f32)]
        if last:
            inner, inner_work = call(
                inner_kernel,
                "inner",
                [((devices, 4, chunk), f32), ((4, LANES), f32)],
                [pltpu.VMEM((128, WIDE), f32)],
                20 << 20,
                [pressure_weights, state, idx, hot, cell_weight],
                [SMEM] + [VMEM] * 4,
            )
            outs += [((2, 8, cells), f32), ((4, LANES), f32)]
            operands += [cell_weight, inner_work, pressure_weights]
            specs += [VMEM, VMEM, SMEM]
        down, up, *got = call(
            functools.partial(post_kernel, first, last),
            "post",
            outs,
            [],
            20 << 20,
            operands,
            specs,
        )
        if first:
            ghosts = got
    press, work = got
    (mine,) = call(
        surface_kernel,
        "surface",
        [((devices, 4, chunk + LANES), f32)],
        [],
        1 << 28,
        [press, idx, hot, inner, work],
        [VMEM] * 5,
    )
    (state,) = call(
        merge_kernel, "merge", [(previous.shape, f32)], [], 1 << 20, [state, down, up], [VMEM] * 3
    )

    every = lax.all_to_all(mine, "phase", 0, 0, tiled=True)
    every, state = lax.optimization_barrier((every, state))
    own_table = lax.dynamic_slice_in_dim(table, lax.axis_index("phase") * 4, 4)
    (work,) = call(
        work_kernel, "work", [((4, LANES), f32)], [], 1 << 16, [own_table, every], [VMEM] * 2
    )
    work, ready = lax.optimization_barrier((work, every))

    def across(bits):
        return lax.ppermute(work, "space", [(i, i ^ bits) for i in range(count)])

    work = (work + across(4)) + (across(8) + across(12))
    work = (work + across(1)) + (across(2) + across(3))
    (turned,) = call(
        phase_kernel,
        "phases",
        [((devices, 4, chunk), f32)],
        [],
        1 << 24,
        [table, ready],
        [VMEM] * 2,
    )
    blocks = lax.all_to_all(turned, "phase", 0, 0, tiled=True)
    influence, modal_work = call(
        place_kernel,
        "place",
        [((2, 2, entries), f32), ((2, 2), f32)],
        [],
        1 << 16,
        [blocks, work],
        [VMEM] * 2,
    )
    return state, influence, modal_work


def solution(mesh):
    in_specs = (
        P("phase", None, None, "space", None),
        P("phase", None, None, "space", None),
        P(),
        P(None, "space", None),
        P("space", None),
        P("space", None),
        P(),
        P("space"),
        P("space"),
        P(),
    )
    out_specs = (P("phase", None, None, "space", None), P("phase", None, "space"), P("phase", None))
    return jax.shard_map(
        per_device, mesh=mesh, in_specs=in_specs, out_specs=out_specs, check_vma=False
    )
```

```python
import functools
import math

import jax
import jax.numpy as jnp
from jax import lax
from jax.experimental import pallas as pl
from jax.experimental.pallas import tpu as pltpu
from jax.sharding import PartitionSpec as P

ITERS = 6
WIDTH = 2
RELAX = 0.8
LANES = 128
WIDE = 256
HIGHEST = lax.Precision.HIGHEST

VMEM = pl.BlockSpec(memory_space=pltpu.VMEM)
SMEM = pl.BlockSpec(memory_space=pltpu.SMEM)
HBM = pl.BlockSpec(memory_space=pltpu.HBM)


def call(kernel, name, out_shapes, scratch, flops, operands, in_specs, out_specs=None):
    return pl.pallas_call(
        kernel,
        name=name,
        out_shape=[jax.ShapeDtypeStruct(s, d) for s, d in out_shapes],
        in_specs=in_specs,
        out_specs=out_specs or [VMEM] * len(out_shapes),
        scratch_shapes=scratch,
        compiler_params=pltpu.CompilerParams(vmem_limit_bytes=40 * 1024 * 1024),
        cost_estimate=pl.CostEstimate(
            flops=flops, bytes_accessed=1 << 20, transcendentals=0
        ),
    )(*operands)


def pack_kernel(
    x_hbm, f_hbm, cpl_hbm, diag_hbm, inert_hbm, coef_ref, up_ref, down_ref, x_ref, f_ref, diag_ref, inert_ref, sems
):
    copies = [
        pltpu.make_async_copy(src, dst, sems.at[i])
        for i, (src, dst) in enumerate(
            [(x_hbm.at[p, c], x_ref.at[p, c]) for p in range(2) for c in range(2)]
            + [
                (diag_hbm, diag_ref),
                (inert_hbm, inert_ref),
                (cpl_hbm, coef_ref.at[0:4]),
            ]
            + [(f_hbm.at[p, c], f_ref.at[p, c]) for p in range(2) for c in range(2)]
        )
    ]
    for copy in copies:
        copy.start()
    for i in range(4):
        p, c = i // 2, i % 2
        copies[i].wait()
        for v in range(5):
            for r in range(2):
                at = 8 * v + 4 * p + 2 * r + c
                up_ref[at : at + 1, :] = x_ref[p, c, v, 6 + r : 7 + r, :]
                down_ref[at : at + 1, :] = x_ref[p, c, v, r : r + 1, :]
    for copy in copies[4:7]:
        copy.wait()
    diag = diag_ref[...]
    inert = inert_ref[...]
    scale = RELAX / (diag * diag + inert * inert)
    coef_ref[4] = diag * scale
    coef_ref[5] = inert * scale
    for i in range(6):
        up_ref[60 + i : 61 + i, :] = coef_ref[i, 7:8, :]
        down_ref[60 + i : 61 + i, :] = coef_ref[i, 0:1, :]
    for i in range(4):
        p, c = i // 2, i % 2
        copies[7 + i].wait()
        for v in range(5):
            at = 40 + 4 * v + 2 * p + c
            up_ref[at : at + 1, :] = f_ref[p, c, v, 7:8, :]
            down_ref[at : at + 1, :] = f_ref[p, c, v, 0:1, :]


def tables_kernel(jac_ref, rot_ref, own_ref, plain_ref, lo_ref, hi_ref):
    def split(a):
        high = a.astype(jnp.bfloat16).astype(jnp.float32)
        return jnp.concatenate([high, high, a - high], axis=1).astype(jnp.bfloat16)

    j = lax.broadcasted_iota(jnp.int32, (8, 48), 0)
    k = lax.broadcasted_iota(jnp.int32, (8, 48), 1)
    tiles = []
    for d in range(4):
        near = (jnp.where(j == 0, -99, j - 1), jnp.where(j == 7, -99, j + 1), j, j)[d]
        for v in range(5):
            total = jnp.zeros((8, 48), jnp.float32)
            for w in range(5):
                total = jnp.where(k == 8 * w + near, jac_ref[d, v, w], total)
            tiles.append(total)
    own_ref[...] = split(jnp.concatenate(tiles, axis=0))

    row = lax.broadcasted_iota(jnp.int32, (8, 80), 0)
    col = lax.broadcasted_iota(jnp.int32, (8, 80), 1)
    second = col >= 40
    inner = jnp.where(second, col - 40, col)
    var = inner >> 3
    from_row = jnp.where(second, 2, 0) + ((inner >> 1) & 1)
    to_row = 1 + ((row >> 1) & 1)
    part, from_part = row & 1, inner & 1
    phase = row >> 2
    same_phase = phase == ((inner >> 2) & 1)

    def turn(c, s):
        cos = jnp.where(phase == 0, rot_ref[c], rot_ref[4 + c])
        sin = jnp.where(phase == 0, rot_ref[s], rot_ref[4 + s])
        return jnp.where(part == from_part, cos, jnp.where(part == 0, -sin, sin))

    straight = jnp.where(part == from_part, 1.0, 0.0)
    factors = (
        straight,
        jnp.where(second, straight, turn(0, 1)),
        jnp.where(second, turn(2, 3), straight),
    )
    tiles = [[], [], []]
    for d in range(5):
        near = to_row + (-1, 1, 0, 0, 0)[d]
        here = same_phase & (from_row == near)
        for v in range(5):
            if d == 4:
                value = jnp.where(var == v, 1.0 - RELAX, 0.0)
            else:
                value = jnp.zeros((8, 80), jnp.float32)
                for w in range(5):
                    value = jnp.where(var == w, jac_ref[d, v, w], value)
            value = jnp.where(here, value, 0.0)
            for i in range(3):
                tiles[i].append(value * factors[i])
    for i, ref in enumerate((plain_ref, lo_ref, hi_ref)):
        ref[...] = split(jnp.concatenate(tiles[i], axis=0))


def hot_kernel(idx_ref, weight_ref, hot_ref, cell_ref, sum_ref):
    shape = hot_ref.shape[1:]
    chunk = shape[1]
    groups = cell_ref.shape[1] // WIDE
    rows = 8 * groups
    sum_ref[...] = jnp.zeros_like(sum_ref)

    def one(d, _):
        idx = idx_ref[d]
        low = jnp.broadcast_to(idx & (WIDE - 1), shape)
        hot = jnp.where(lax.broadcasted_iota(jnp.int32, shape, 0) == low, 1.0, 0.0).astype(jnp.bfloat16)
        hot_ref[d] = hot
        top = jnp.broadcast_to(idx >> 8, (rows, chunk))
        row = lax.broadcasted_iota(jnp.int32, (rows, chunk), 0)
        weight = jnp.where(top == (row & 7) * groups + (row >> 3), jnp.broadcast_to(weight_ref[d], (rows, chunk)), 0.0)
        parts = []
        for _ in range(3):
            part = weight.astype(jnp.bfloat16).astype(jnp.float32)
            parts.append(part)
            weight = weight - part
        sum_ref[...] += lax.dot_general(
            jnp.concatenate(parts, axis=0).astype(jnp.bfloat16),
            hot,
            (((1,), (1,)), ((), ())),
            preferred_element_type=jnp.float32,
        )
        return 0

    lax.fori_loop(0, hot_ref.shape[0], one, 0, unroll=4)
    for g in range(groups):
        total = sum_ref[8 * g : 8 * g + 8, :]
        for i in range(1, 3):
            total = total + sum_ref[rows * i + 8 * g : rows * i + 8 * g + 8, :]
        cell_ref[:, g * WIDE : (g + 1) * WIDE] = total


def multiply(table, b):
    high = b.astype(jnp.bfloat16)
    low = (b - high.astype(jnp.float32)).astype(jnp.bfloat16)
    return jnp.dot(
        table,
        jnp.concatenate([high, low, high], axis=0),
        preferred_element_type=jnp.float32,
    )


def remainder(y, coef, forcing):
    cells = forcing.shape[-1]
    lane = lax.broadcasted_iota(jnp.int32, (8, cells), 1)
    before = jnp.where(lane == 0, 0.0, pltpu.roll(y[2], 1, 1))
    after = jnp.where(lane == cells - 1, 0.0, pltpu.roll(y[3], cells - 1, 1))
    return forcing - coef[0] * y[0] - coef[1] * y[1] - coef[2] * before - coef[3] * after


def pre_kernel(first, x_ref, f_ref, coef_ref, own_ref, *refs):
    if first:
        next_ref, mid_ref, ef_ref, ecoef_ref, b_ref, y_ref = refs
    else:
        edge_refs, (next_ref, mid_ref, b_ref, y_ref) = refs[:2], refs[2:]
    cells = x_ref.shape[-1]
    if first:
        row = lax.broadcasted_iota(jnp.int32, (8, cells), 0)
        for h in range(2):
            for i in range(6):
                tile = jnp.where(
                    (row >> 1) & 1 == 0,
                    jnp.broadcast_to(coef_ref[i, 6 * h : 6 * h + 1, :], (8, cells)),
                    jnp.broadcast_to(coef_ref[i, 6 * h + 1 : 6 * h + 2, :], (8, cells)),
                )
                ecoef_ref[h, i] = jnp.where(row & 1 == 0, tile, -tile) if i == 5 else tile
            for n in range(20):
                p, c, v = n // 10, n // 5 % 2, n % 5
                for r in range(2):
                    at = 4 * p + 2 * r + c
                    ef_ref[h, v, at : at + 1, :] = f_ref[p, c, v, 6 * h + r : 6 * h + r + 1, :]
    for c in range(2):
        b_ref[c, 40:48, :] = jnp.zeros((8, cells), jnp.float32)
    coef = [coef_ref[i] for i in range(6)]
    for p in range(2):
        for c in range(2):
            b_ref[c, 0:40, :] = x_ref[p, c].reshape(40, cells)
            if not first:
                for h in range(2):
                    for v in range(5):
                        for r in range(2):
                            at, to = 8 * v + 4 * p + 2 * r + c, 8 * v + 6 * h + r
                            b_ref[c, to : to + 1, :] = edge_refs[h][at : at + 1, :]
        for sweep in range(2):
            for c in range(2):
                y_ref[c] = multiply(own_ref[...], b_ref[c])
            for v in range(5):
                re, im = (
                    remainder(
                        [y_ref[c, 40 * d + 8 * v : 40 * d + 8 * v + 8, :] for d in range(4)],
                        coef,
                        f_ref[p, c, v],
                    )
                    for c in range(2)
                )
                add = (coef[4] * re + coef[5] * im, coef[4] * im - coef[5] * re)
                for c in range(2):
                    new = (1.0 - RELAX) * b_ref[c, 8 * v : 8 * v + 8, :] + add[c]
                    if sweep == 0:
                        b_ref[c, 8 * v : 8 * v + 8, :] = new
                        for h in range(2):
                            for r in range(2):
                                at = 8 * v + 4 * p + 2 * r + c
                                mid_ref[h, at : at + 1, :] = new[4 * h + r + 1 : 4 * h + r + 2, :]
                    else:
                        next_ref[p, c, v] = new


def post_kernel(first, last, rot_ref, plain_ref, lo_turn_ref, hi_turn_ref, ef_ref, ecoef_ref, lo_ref, hi_ref, up_ref, down_ref, mid_ref, *refs):
    if first:
        down_out, up_out, gf_ref, gcoef_ref = refs
    elif last:
        gf_ref, gcoef_ref, cell_ref, part_work_ref, pw_ref, down_out, up_out, press_ref, work_ref = refs
    else:
        gf_ref, gcoef_ref, down_out, up_out = refs
    cells = lo_ref.shape[-1]
    row = lax.broadcasted_iota(jnp.int32, (8, cells), 0)

    if first:
        for h in range(2):
            rows = (lo_ref, down_ref) if h == 0 else (up_ref, hi_ref)
            for i in range(6):
                tile = jnp.where(
                    (row >> 1) & 1 == 0,
                    jnp.broadcast_to(rows[0][60 + i : 61 + i, :], (8, cells)),
                    jnp.broadcast_to(rows[1][60 + i : 61 + i, :], (8, cells)),
                )
                gcoef_ref[h, i] = jnp.where(row & 1 == 0, tile, -tile) if i == 5 else tile
            ghost, base = (lo_ref, 0) if h == 0 else (hi_ref, 2)
            for v in range(5):
                for p in range(2):
                    cos, sin = rot_ref[4 * p + base], rot_ref[4 * p + base + 1]
                    at = 40 + 4 * v + 2 * p
                    re = ghost[at : at + 1, :]
                    im = ghost[at + 1 : at + 2, :]
                    turned = (cos * re - sin * im, sin * re + cos * im)
                    to = 4 * p + 2 * h
                    gf_ref[h, v, to : to + 1, :] = turned[0]
                    gf_ref[h, v, to + 1 : to + 2, :] = turned[1]
                    to = 4 * p + 2 - 2 * h
                    gf_ref[h, v, to : to + 2, :] = (down_ref if h == 0 else up_ref)[at : at + 2, :]

    def sweep(table, b, coef, forcing):
        y = multiply(table[...], b)
        new = []
        for v in range(5):
            at = [40 * d + 8 * v for d in range(5)]
            rest = remainder([y[at[d] : at[d] + 8] for d in range(4)], coef, forcing[v])
            partner = jnp.where(row & 1 == 0, pltpu.roll(rest, 7, 0), pltpu.roll(rest, 1, 0))
            new.append(y[at[4] : at[4] + 8] + coef[4] * rest + coef[5] * partner)
        return jnp.concatenate(new, axis=0)

    mids = []
    for h in range(2):
        pair = (up_ref, hi_ref) if h else (lo_ref, down_ref)
        mids.append(
            sweep(
                hi_turn_ref if h else lo_turn_ref,
                jnp.concatenate([ref[0:40, :] for ref in pair], axis=0),
                [gcoef_ref[h, i] for i in range(6)],
                [gf_ref[h, v] for v in range(5)],
            )
        )
    for h in range(2):
        new = sweep(
            plain_ref,
            jnp.concatenate([mid_ref[1], mids[1]] if h else [mids[0], mid_ref[0]], axis=0),
            [ecoef_ref[h, i] for i in range(6)],
            [ef_ref[h, v] for v in range(5)],
        )
        (up_out if h else down_out)[...] = new
        if last:
            press = pw_ref[0] * new[0:8]
            for v in range(1, 5):
                press = press + pw_ref[v] * new[8 * v : 8 * v + 8]
            press_ref[h] = press
            weight = jnp.where(
                (row >> 1) & 1 == 0,
                jnp.broadcast_to(cell_ref[6 * h : 6 * h + 1, :], (8, cells)),
                jnp.broadcast_to(cell_ref[6 * h + 1 : 6 * h + 2, :], (8, cells)),
            )
            work = weight * press if h == 0 else work + weight * press
    if last:
        work = jnp.broadcast_to(jnp.sum(work, axis=1, keepdims=True), (8, LANES))
        both = work + pltpu.roll(work, 6, 0)
        work_ref[0:2, :] = both[0:2] + part_work_ref[0:2, :]
        work_ref[2:4, :] = both[4:6] + part_work_ref[2:4, :]


def inner_kernel(pw_ref, x_ref, idx_ref, hot_ref, cell_ref, out_ref, work_ref, table_ref):
    cells = x_ref.shape[-1]
    chunk = idx_ref.shape[-1]
    parts = idx_ref.shape[0]
    groups = cells // WIDE
    half = 16 * groups
    row = lax.broadcasted_iota(jnp.int32, (8, cells), 0)
    kept = (row >= 2) & (row < 6)
    press = []
    for i in range(4):
        value = pw_ref[0] * x_ref[i // 2, i % 2, 0]
        for v in range(1, 5):
            value = value + pw_ref[v] * x_ref[i // 2, i % 2, v]
        value = jnp.where(kept, value, 0.0)
        press.append(value)
        work = jnp.sum(jnp.sum(value * cell_ref[...], axis=1, keepdims=True), axis=0, keepdims=True)
        work_ref[i : i + 1, :] = jnp.broadcast_to(work, (1, LANES))
    for i in range(2):
        value = press[2 * i] + pltpu.roll(press[2 * i + 1], 4, 0)
        high = value.astype(jnp.bfloat16).astype(jnp.float32)
        for g in range(groups):
            at = (i * groups + g) * 8
            table_ref[at : at + 8, :] = high[:, g * WIDE : (g + 1) * WIDE]
            table_ref[half + at : half + at + 8, :] = (value - high)[:, g * WIDE : (g + 1) * WIDE]
    table = table_ref[...].astype(jnp.bfloat16)
    row = lax.broadcasted_iota(jnp.int32, (8, chunk), 0)
    place = jnp.where((row >= 2) & (row < 6), row, (row + 4) & 7) * groups
    mine = (row >= 2) & (row < 6)

    def one(d, _):
        both = jnp.dot(table, hot_ref[d], preferred_element_type=jnp.float32)
        found = both[:half] + both[half:]
        top = jnp.broadcast_to(idx_ref[d] >> 8, (8, chunk))
        res = []
        for i in range(2):
            total = jnp.zeros((8, chunk), jnp.float32)
            for g in range(groups):
                at = (i * groups + g) * 8
                total = jnp.where(top == place + g, found[at : at + 8], total)
            res.append(jnp.sum(jnp.where(mine, total, 0.0), axis=0, keepdims=True))
            res.append(jnp.sum(jnp.where(mine, 0.0, total), axis=0, keepdims=True))
        out_ref[d] = jnp.concatenate(res, axis=0)
        return 0

    lax.fori_loop(0, parts, one, 0, unroll=16)


def surface_kernel(press_ref, idx_ref, hot_ref, inner_ref, work_ref, out_ref):
    cells = press_ref.shape[-1]
    chunk = idx_ref.shape[-1]
    parts = idx_ref.shape[0]
    groups = cells // WIDE
    half = 16 * groups
    tiles = [press_ref[h, :, g * WIDE : (g + 1) * WIDE] for h in range(2) for g in range(groups)]
    value = jnp.concatenate(tiles, axis=0)
    high = value.astype(jnp.bfloat16)
    low = (value - high.astype(jnp.float32)).astype(jnp.bfloat16)
    table = jnp.concatenate([high, low], axis=0)
    row = lax.broadcasted_iota(jnp.int32, (8, chunk), 0)
    place = ((row >> 1) & 1) * groups

    def one(d, _):
        both = jnp.dot(table, hot_ref[d], preferred_element_type=jnp.float32)
        found = both[:half] + both[half:]
        top = jnp.broadcast_to(idx_ref[d] >> 8, (8, chunk))
        total = jnp.zeros((8, chunk), jnp.float32)
        for h in range(2):
            for g in range(groups):
                at = (h * groups + g) * 8
                total = jnp.where(top == place + (6 * h * groups + g), found[at : at + 8], total)
        total = total + pltpu.roll(total, 6, 0)
        out_ref[d, 0:2, 0:chunk] = inner_ref[d, 0:2, :] + total[0:2]
        out_ref[d, 2:4, 0:chunk] = inner_ref[d, 2:4, :] + total[4:6]
        out_ref[d, :, chunk : chunk + LANES] = work_ref[...]
        return 0

    lax.fori_loop(0, parts, one, 0, unroll=16)


def merge_kernel(x_ref, down_ref, up_ref, out_ref):
    for n in range(20):
        p, c, v = n // 10, n // 5 % 2, n % 5
        out_ref[p, c, v] = x_ref[p, c, v]
        for h, ref in enumerate((down_ref, up_ref)):
            for r in range(2):
                at, to = 8 * v + 4 * p + 2 * r + c, 6 * h + r
                out_ref[p, c, v, to : to + 1, :] = ref[at : at + 1, :]


def work_kernel(table_ref, x_ref, work_ref):
    chunk = x_ref.shape[-1] - LANES
    rows = jnp.concatenate([x_ref[d, :, chunk:] for d in range(x_ref.shape[0])], axis=0)
    work = jnp.dot(
        table_ref[...], rows, precision=HIGHEST, preferred_element_type=jnp.float32
    )
    for i in range(work_ref.shape[1] // LANES):
        work_ref[:, i * LANES : (i + 1) * LANES] = work


def phase_kernel(table_ref, x_ref, out_ref):
    parts = x_ref.shape[0]
    chunk = out_ref.shape[-1]
    table = table_ref[...]
    high = table.astype(jnp.bfloat16).astype(jnp.float32)
    table = jnp.concatenate([high, high, table - high], axis=1).astype(jnp.bfloat16)
    rows = jnp.concatenate([x_ref[d, :, 0:chunk] for d in range(parts)], axis=0)
    y = multiply(table, rows)
    for d in range(parts):
        out_ref[d] = y[4 * d : 4 * d + 4]


def place_kernel(x_ref, work_ref, out_ref, modal_ref):
    chunk = x_ref.shape[-1]
    for d in range(x_ref.shape[0]):
        for m in range(2):
            out_ref[m, :, d * chunk : (d + 1) * chunk] = x_ref[d, 2 * m : 2 * m + 2, :]
    lane = lax.broadcasted_iota(jnp.int32, (1, 2), 1)
    for m in range(2):
        re = jnp.broadcast_to(work_ref[2 * m : 2 * m + 1, 0:1], (1, 2))
        im = jnp.broadcast_to(work_ref[2 * m + 1 : 2 * m + 2, 0:1], (1, 2))
        modal_ref[m : m + 1, :] = jnp.where(lane == 0, re, im)


def phase_table(phase_index, blades):
    ids = jnp.arange(blades, dtype=jnp.int32)
    turns = ids[:, None] * phase_index[None, :] % blades
    angle = 2.0 * math.pi / blades * turns.astype(jnp.float32)
    cos, sin = jnp.cos(angle) / blades, jnp.sin(angle) / blades
    top = jnp.stack([cos, -sin], axis=2).reshape(blades, 2 * blades)
    bottom = jnp.stack([sin, cos], axis=2).reshape(blades, 2 * blades)
    return jnp.stack([top, bottom], axis=1).reshape(2 * blades, 2 * blades)


def per_device(
    previous,
    forcing,
    jacobians,
    coupling,
    diagonal,
    inertia,
    pressure_weights,
    surface_cells,
    modal_weights,
    phase_index,
):
    f32 = jnp.float32
    blades = phase_index.shape[0]
    cells = previous.shape[-1]
    entries = surface_cells.shape[0]
    devices = lax.axis_size("phase")
    count = lax.axis_size("space")
    here = lax.axis_index("space")
    forward = [(i, (i + 1) % count) for i in range(count)]
    backward = [((i + 1) % count, i) for i in range(count)]

    local_index = lax.dynamic_slice_in_dim(phase_index, lax.axis_index("phase") * 2, 2)
    angles = 2.0 * math.pi / blades * local_index.astype(f32)
    cos, sin = jnp.cos(angles), jnp.sin(angles)
    low_end, high_end = here == 0, here == count - 1
    turn = jnp.stack(
        [
            jnp.where(low_end, cos, 1.0),
            jnp.where(low_end, -sin, 0.0),
            jnp.where(high_end, cos, 1.0),
            jnp.where(high_end, sin, 0.0),
        ],
        axis=1,
    ).reshape(8)
    table = phase_table(phase_index, blades)
    chunk = entries // devices
    idx = surface_cells.reshape(devices, 1, chunk)

    coef, up, down, state, forcing = call(
        pack_kernel,
        "pack",
        [((6, 8, cells), f32), ((66, cells), f32), ((66, cells), f32)]
        + [(previous.shape, f32)] * 2,
        [
            pltpu.VMEM((8, cells), f32),
            pltpu.VMEM((8, cells), f32),
            pltpu.SemaphoreType.DMA((11,)),
        ],
        1 << 20,
        [
            pltpu.with_memory_space_constraint(a, pltpu.HBM)
            for a in (previous, forcing, coupling, diagonal, inertia)
        ],
        [HBM] * 5,
    )
    bf16 = jnp.bfloat16
    own, *tables = call(
        tables_kernel,
        "tables",
        [((160, 144), bf16)] + [((200, 240), bf16)] * 3,
        [],
        1 << 20,
        [jacobians, turn],
        [SMEM] * 2,
    )
    hot, cell_weight = call(
        hot_kernel,
        "onehot",
        [((devices, WIDE, chunk), bf16), ((8, cells), f32)],
        [pltpu.VMEM((96 * cells // 1024, WIDE), f32)],
        8 << 20,
        [idx, modal_weights.reshape(devices, 1, chunk)],
        [VMEM] * 2,
    )
    steps = ITERS // WIDTH
    edge_shape = (2, 5, 8, cells)
    for step in range(steps):
        first, last = step == 0, step == steps - 1
        lo = lax.ppermute(up, "space", forward)
        hi = lax.ppermute(down, "space", backward)
        operands = [state, forcing, coef, own] + ([] if first else [down, up])
        got = call(
            functools.partial(pre_kernel, first),
            "pre",
            [(previous.shape, f32), ((2, 40, cells), f32)]
            + ([(edge_shape, f32), ((2, 6, 8, cells), f32)] if first else []),
            [pltpu.VMEM((2, 48, cells), f32), pltpu.VMEM((2, 160, cells), f32)],
            40 << 20,
            operands,
            [VMEM] * len(operands),
        )
        state, mid = got[:2]
        if first:
            edges = got[2:]
            ghosts = ()
        if step == 1:
            mid, hot, cell_weight = lax.optimization_barrier((mid, hot, cell_weight))
        outs = [((40, cells), f32)] * 2
        operands = [turn, *tables, *edges, lo, hi, up, down, mid, *ghosts]
        specs = [SMEM] + [VMEM] * (len(operands) - 1)
        if first:
            outs += [(edge_shape, f32), ((2, 6, 8, cells), f32)]
        if last:
            inner, inner_work = call(
                inner_kernel,
                "inner",
                [((devices, 4, chunk), f32), ((4, LANES), f32)],
                [pltpu.VMEM((128, WIDE), f32)],
                20 << 20,
                [pressure_weights, state, idx, hot, cell_weight],
                [SMEM] + [VMEM] * 4,
            )
            outs += [((2, 8, cells), f32), ((4, LANES), f32)]
            operands += [cell_weight, inner_work, pressure_weights]
            specs += [VMEM, VMEM, SMEM]
        down, up, *got = call(
            functools.partial(post_kernel, first, last),
            "post",
            outs,
            [],
            20 << 20,
            operands,
            specs,
        )
        if first:
            ghosts = got
    press, work = got
    (mine,) = call(
        surface_kernel,
        "surface",
        [((devices, 4, chunk + LANES), f32)],
        [],
        1 << 28,
        [press, idx, hot, inner, work],
        [VMEM] * 5,
    )
    (state,) = call(
        merge_kernel, "merge", [(previous.shape, f32)], [], 1 << 20, [state, down, up], [VMEM] * 3
    )

    every = lax.all_to_all(mine, "phase", 0, 0, tiled=True)
    every, state = lax.optimization_barrier((every, state))
    own_table = lax.dynamic_slice_in_dim(table, lax.axis_index("phase") * 4, 4)
    (work,) = call(
        work_kernel, "work", [((4, 2048), f32)], [], 1 << 16, [own_table, every], [VMEM] * 2
    )
    work, ready = lax.optimization_barrier((work, every))

    def across(bits):
        return lax.ppermute(work, "space", [(i, i ^ bits) for i in range(count)])

    work = (work + across(8))[:, :LANES]
    work = work + across(4)
    work = (work + across(1)) + (across(2) + across(3))
    (turned,) = call(
        phase_kernel,
        "phases",
        [((devices, 4, chunk), f32)],
        [],
        1 << 24,
        [table, ready],
        [VMEM] * 2,
    )
    blocks = lax.all_to_all(turned, "phase", 0, 0, tiled=True)
    influence, modal_work = call(
        place_kernel,
        "place",
        [((2, 2, entries), f32), ((2, 2), f32)],
        [],
        1 << 16,
        [blocks, work],
        [VMEM] * 2,
    )
    return state, influence, modal_work


def solution(mesh):
    in_specs = (
        P("phase", None, None, "space", None),
        P("phase", None, None, "space", None),
        P(),
        P(None, "space", None),
        P("space", None),
        P("space", None),
        P(),
        P("space"),
        P("space"),
        P(),
    )
    out_specs = (P("phase", None, None, "space", None), P("phase", None, "space"), P("phase", None))
    return jax.shard_map(
        per_device, mesh=mesh, in_specs=in_specs, out_specs=out_specs, check_vma=False
    )
```

```python
import functools
import math

import jax
import jax.numpy as jnp
from jax import lax
from jax.experimental import pallas as pl
from jax.experimental.pallas import tpu as pltpu
from jax.sharding import PartitionSpec as P

ITERS = 6
WIDTH = 2
RELAX = 0.8
LANES = 128
WIDE = 256
HIGHEST = lax.Precision.HIGHEST

VMEM = pl.BlockSpec(memory_space=pltpu.VMEM)
SMEM = pl.BlockSpec(memory_space=pltpu.SMEM)
HBM = pl.BlockSpec(memory_space=pltpu.HBM)


def call(kernel, name, out_shapes, scratch, flops, operands, in_specs, out_specs=None):
    return pl.pallas_call(
        kernel,
        name=name,
        out_shape=[jax.ShapeDtypeStruct(s, d) for s, d in out_shapes],
        in_specs=in_specs,
        out_specs=out_specs or [VMEM] * len(out_shapes),
        scratch_shapes=scratch,
        compiler_params=pltpu.CompilerParams(vmem_limit_bytes=40 * 1024 * 1024),
        cost_estimate=pl.CostEstimate(
            flops=flops, bytes_accessed=1 << 20, transcendentals=0
        ),
    )(*operands)


def pack_kernel(
    x_hbm, f_hbm, cpl_hbm, diag_hbm, inert_hbm, coef_ref, up_ref, down_ref, diag_ref, inert_ref, xe_ref, fe_ref, sems
):
    edges = [
        pltpu.make_async_copy(x_hbm.at[:, :, :, 6 * h : 6 * h + 2], xe_ref.at[h], sems.at[h])
        for h in range(2)
    ]
    coefs = [
        pltpu.make_async_copy(src, dst, sems.at[i])
        for i, (src, dst) in enumerate(
            [(diag_hbm, diag_ref), (inert_hbm, inert_ref), (cpl_hbm, coef_ref.at[0:4])], 2
        )
    ]
    force = [
        pltpu.make_async_copy(f_hbm.at[:, :, :, 7 * h : 7 * h + 1], fe_ref.at[h], sems.at[5 + h])
        for h in range(2)
    ]
    for copy in edges + coefs + force:
        copy.start()
    for h, ref in enumerate((down_ref, up_ref)):
        edges[h].wait()
        for p in range(2):
            for c in range(2):
                for v in range(5):
                    for r in range(2):
                        at = 8 * v + 4 * p + 2 * r + c
                        ref[at : at + 1, :] = xe_ref[h, p, c, v, r : r + 1, :]
    for copy in coefs:
        copy.wait()
    diag = diag_ref[...]
    inert = inert_ref[...]
    scale = RELAX / (diag * diag + inert * inert)
    coef_ref[4] = diag * scale
    coef_ref[5] = inert * scale
    for i in range(6):
        up_ref[60 + i : 61 + i, :] = coef_ref[i, 7:8, :]
        down_ref[60 + i : 61 + i, :] = coef_ref[i, 0:1, :]
    for h, ref in enumerate((down_ref, up_ref)):
        force[h].wait()
        for p in range(2):
            for c in range(2):
                for v in range(5):
                    at = 40 + 4 * v + 2 * p + c
                    ref[at : at + 1, :] = fe_ref[h, p, c, v, :, :]


def tables_kernel(jac_ref, rot_ref, own_ref, plain_ref, lo_ref, hi_ref):
    def split(a):
        high = a.astype(jnp.bfloat16).astype(jnp.float32)
        return jnp.concatenate([high, high, a - high], axis=1).astype(jnp.bfloat16)

    j = lax.broadcasted_iota(jnp.int32, (8, 48), 0)
    k = lax.broadcasted_iota(jnp.int32, (8, 48), 1)
    tiles = []
    for d in range(4):
        near = (jnp.where(j == 0, -99, j - 1), jnp.where(j == 7, -99, j + 1), j, j)[d]
        for v in range(5):
            total = jnp.zeros((8, 48), jnp.float32)
            for w in range(5):
                total = jnp.where(k == 8 * w + near, jac_ref[d, v, w], total)
            tiles.append(total)
    own_ref[...] = split(jnp.concatenate(tiles, axis=0))

    row = lax.broadcasted_iota(jnp.int32, (8, 80), 0)
    col = lax.broadcasted_iota(jnp.int32, (8, 80), 1)
    second = col >= 40
    inner = jnp.where(second, col - 40, col)
    var = inner >> 3
    from_row = jnp.where(second, 2, 0) + ((inner >> 1) & 1)
    to_row = 1 + ((row >> 1) & 1)
    part, from_part = row & 1, inner & 1
    phase = row >> 2
    same_phase = phase == ((inner >> 2) & 1)

    def turn(c, s):
        cos = jnp.where(phase == 0, rot_ref[c], rot_ref[4 + c])
        sin = jnp.where(phase == 0, rot_ref[s], rot_ref[4 + s])
        return jnp.where(part == from_part, cos, jnp.where(part == 0, -sin, sin))

    straight = jnp.where(part == from_part, 1.0, 0.0)
    factors = (
        straight,
        jnp.where(second, straight, turn(0, 1)),
        jnp.where(second, turn(2, 3), straight),
    )
    tiles = [[], [], []]
    for d in range(5):
        near = to_row + (-1, 1, 0, 0, 0)[d]
        here = same_phase & (from_row == near)
        for v in range(5):
            if d == 4:
                value = jnp.where(var == v, 1.0 - RELAX, 0.0)
            else:
                value = jnp.zeros((8, 80), jnp.float32)
                for w in range(5):
                    value = jnp.where(var == w, jac_ref[d, v, w], value)
            value = jnp.where(here, value, 0.0)
            for i in range(3):
                tiles[i].append(value * factors[i])
    for i, ref in enumerate((plain_ref, lo_ref, hi_ref)):
        ref[...] = split(jnp.concatenate(tiles[i], axis=0))


def hot_kernel(idx_ref, hot_ref):
    shape = hot_ref.shape[1:]

    def one(d, _):
        low = jnp.broadcast_to(idx_ref[d] & (WIDE - 1), shape)
        hot = jnp.where(lax.broadcasted_iota(jnp.int32, shape, 0) == low, 1.0, 0.0)
        hot_ref[d] = hot.astype(jnp.bfloat16)
        return 0

    lax.fori_loop(0, hot_ref.shape[0], one, 0)


def multiply(table, b):
    high = b.astype(jnp.bfloat16)
    low = (b - high.astype(jnp.float32)).astype(jnp.bfloat16)
    return jnp.dot(
        table,
        jnp.concatenate([high, low, high], axis=0),
        preferred_element_type=jnp.float32,
    )


def remainder(y, coef, forcing):
    cells = forcing.shape[-1]
    lane = lax.broadcasted_iota(jnp.int32, (8, cells), 1)
    before = jnp.where(lane == 0, 0.0, pltpu.roll(y[2], 1, 1))
    after = jnp.where(lane == cells - 1, 0.0, pltpu.roll(y[3], cells - 1, 1))
    return forcing - coef[0] * y[0] - coef[1] * y[1] - coef[2] * before - coef[3] * after


def pre_kernel(first, x_ref, f_ref, coef_ref, own_ref, *refs):
    if first:
        x_hbm, f_hbm = x_ref, f_ref
        next_ref, mid_ref, ef_ref, ecoef_ref, f_ref, b_ref, y_ref, x_ref, sems = refs
        copies = [
            pltpu.make_async_copy(src.at[p, c], dst.at[p, c], sems.at[4 * p + 2 * i + c])
            for p in range(2)
            for i, (src, dst) in enumerate(((x_hbm, x_ref), (f_hbm, f_ref)))
            for c in range(2)
        ]
        for copy in copies:
            copy.start()
    else:
        edge_refs, (next_ref, mid_ref, b_ref, y_ref) = refs[:2], refs[2:]
    cells = x_ref.shape[-1]
    if first:
        row = lax.broadcasted_iota(jnp.int32, (8, cells), 0)
        for h in range(2):
            for i in range(6):
                tile = jnp.where(
                    (row >> 1) & 1 == 0,
                    jnp.broadcast_to(coef_ref[i, 6 * h : 6 * h + 1, :], (8, cells)),
                    jnp.broadcast_to(coef_ref[i, 6 * h + 1 : 6 * h + 2, :], (8, cells)),
                )
                ecoef_ref[h, i] = jnp.where(row & 1 == 0, tile, -tile) if i == 5 else tile
    for c in range(2):
        b_ref[c, 40:48, :] = jnp.zeros((8, cells), jnp.float32)
    coef = [coef_ref[i] for i in range(6)]
    for p in range(2):
        if first:
            for copy in copies[4 * p : 4 * p + 4]:
                copy.wait()
        for c in range(2):
            b_ref[c, 0:40, :] = x_ref[p, c].reshape(40, cells)
            if first:
                for h in range(2):
                    for v in range(5):
                        for r in range(2):
                            at, row = 4 * p + 2 * r + c, 6 * h + r
                            ef_ref[h, v, at : at + 1, :] = f_ref[p, c, v, row : row + 1, :]
            else:
                for h in range(2):
                    for v in range(5):
                        for r in range(2):
                            at, to = 8 * v + 4 * p + 2 * r + c, 8 * v + 6 * h + r
                            b_ref[c, to : to + 1, :] = edge_refs[h][at : at + 1, :]
        for sweep in range(2):
            for c in range(2):
                y_ref[c] = multiply(own_ref[...], b_ref[c])
            for v in range(5):
                re, im = (
                    remainder(
                        [y_ref[c, 40 * d + 8 * v : 40 * d + 8 * v + 8, :] for d in range(4)],
                        coef,
                        f_ref[p, c, v],
                    )
                    for c in range(2)
                )
                add = (coef[4] * re + coef[5] * im, coef[4] * im - coef[5] * re)
                for c in range(2):
                    new = (1.0 - RELAX) * b_ref[c, 8 * v : 8 * v + 8, :] + add[c]
                    if sweep == 0:
                        b_ref[c, 8 * v : 8 * v + 8, :] = new
                        for h in range(2):
                            for r in range(2):
                                at = 8 * v + 4 * p + 2 * r + c
                                mid_ref[h, at : at + 1, :] = new[4 * h + r + 1 : 4 * h + r + 2, :]
                    else:
                        next_ref[p, c, v] = new


def post_kernel(first, last, rot_ref, plain_ref, lo_turn_ref, hi_turn_ref, ef_ref, ecoef_ref, lo_ref, hi_ref, up_ref, down_ref, mid_ref, *refs):
    if first:
        down_out, up_out, gf_ref, gcoef_ref = refs
    elif last:
        gf_ref, gcoef_ref, pw_ref, down_out, up_out, press_ref = refs
    else:
        gf_ref, gcoef_ref, down_out, up_out = refs
    cells = lo_ref.shape[-1]
    row = lax.broadcasted_iota(jnp.int32, (8, cells), 0)

    if first:
        for h in range(2):
            rows = (lo_ref, down_ref) if h == 0 else (up_ref, hi_ref)
            for i in range(6):
                tile = jnp.where(
                    (row >> 1) & 1 == 0,
                    jnp.broadcast_to(rows[0][60 + i : 61 + i, :], (8, cells)),
                    jnp.broadcast_to(rows[1][60 + i : 61 + i, :], (8, cells)),
                )
                gcoef_ref[h, i] = jnp.where(row & 1 == 0, tile, -tile) if i == 5 else tile
            ghost, base = (lo_ref, 0) if h == 0 else (hi_ref, 2)
            for v in range(5):
                for p in range(2):
                    cos, sin = rot_ref[4 * p + base], rot_ref[4 * p + base + 1]
                    at = 40 + 4 * v + 2 * p
                    re = ghost[at : at + 1, :]
                    im = ghost[at + 1 : at + 2, :]
                    turned = (cos * re - sin * im, sin * re + cos * im)
                    to = 4 * p + 2 * h
                    gf_ref[h, v, to : to + 1, :] = turned[0]
                    gf_ref[h, v, to + 1 : to + 2, :] = turned[1]
                    to = 4 * p + 2 - 2 * h
                    gf_ref[h, v, to : to + 2, :] = (down_ref if h == 0 else up_ref)[at : at + 2, :]

    def sweep(table, b, coef, forcing):
        y = multiply(table[...], b)
        new = []
        for v in range(5):
            at = [40 * d + 8 * v for d in range(5)]
            rest = remainder([y[at[d] : at[d] + 8] for d in range(4)], coef, forcing[v])
            partner = jnp.where(row & 1 == 0, pltpu.roll(rest, 7, 0), pltpu.roll(rest, 1, 0))
            new.append(y[at[4] : at[4] + 8] + coef[4] * rest + coef[5] * partner)
        return jnp.concatenate(new, axis=0)

    mids = []
    for h in range(2):
        pair = (up_ref, hi_ref) if h else (lo_ref, down_ref)
        mids.append(
            sweep(
                hi_turn_ref if h else lo_turn_ref,
                jnp.concatenate([ref[0:40, :] for ref in pair], axis=0),
                [gcoef_ref[h, i] for i in range(6)],
                [gf_ref[h, v] for v in range(5)],
            )
        )
    for h in range(2):
        new = sweep(
            plain_ref,
            jnp.concatenate([mid_ref[1], mids[1]] if h else [mids[0], mid_ref[0]], axis=0),
            [ecoef_ref[h, i] for i in range(6)],
            [ef_ref[h, v] for v in range(5)],
        )
        (up_out if h else down_out)[...] = new
        if last:
            press = pw_ref[0] * new[0:8]
            for v in range(1, 5):
                press = press + pw_ref[v] * new[8 * v : 8 * v + 8]
            press_ref[h] = press


def inner_kernel(pw_ref, x_ref, idx_ref, hot_ref, out_ref, table_ref):
    cells = x_ref.shape[-1]
    chunk = idx_ref.shape[-1]
    parts = idx_ref.shape[0]
    groups = cells // WIDE
    half = 16 * groups
    row = lax.broadcasted_iota(jnp.int32, (8, cells), 0)
    kept = (row >= 2) & (row < 6)
    press = []
    for i in range(4):
        value = pw_ref[0] * x_ref[i // 2, i % 2, 0]
        for v in range(1, 5):
            value = value + pw_ref[v] * x_ref[i // 2, i % 2, v]
        value = jnp.where(kept, value, 0.0)
        press.append(value)
    for i in range(2):
        value = press[2 * i] + pltpu.roll(press[2 * i + 1], 4, 0)
        high = value.astype(jnp.bfloat16).astype(jnp.float32)
        for g in range(groups):
            at = (i * groups + g) * 8
            table_ref[at : at + 8, :] = high[:, g * WIDE : (g + 1) * WIDE]
            table_ref[half + at : half + at + 8, :] = (value - high)[:, g * WIDE : (g + 1) * WIDE]
    table = table_ref[...].astype(jnp.bfloat16)
    row = lax.broadcasted_iota(jnp.int32, (8, chunk), 0)
    place = jnp.where((row >= 2) & (row < 6), row, (row + 4) & 7) * groups
    mine = (row >= 2) & (row < 6)

    def one(d, _):
        both = jnp.dot(table, hot_ref[d], preferred_element_type=jnp.float32)
        found = both[:half] + both[half:]
        top = jnp.broadcast_to(idx_ref[d] >> 8, (8, chunk))
        res = []
        for i in range(2):
            total = jnp.zeros((8, chunk), jnp.float32)
            for g in range(groups):
                at = (i * groups + g) * 8
                total = jnp.where(top == place + g, found[at : at + 8], total)
            res.append(jnp.sum(jnp.where(mine, total, 0.0), axis=0, keepdims=True))
            res.append(jnp.sum(jnp.where(mine, 0.0, total), axis=0, keepdims=True))
        out_ref[d] = jnp.concatenate(res, axis=0)
        return 0

    lax.fori_loop(0, parts, one, 0, unroll=16)


def surface_kernel(press_ref, idx_ref, hot_ref, inner_ref, weight_ref, out_ref):
    cells = press_ref.shape[-1]
    chunk = idx_ref.shape[-1]
    parts = idx_ref.shape[0]
    groups = cells // WIDE
    half = 16 * groups
    tiles = [press_ref[h, :, g * WIDE : (g + 1) * WIDE] for h in range(2) for g in range(groups)]
    value = jnp.concatenate(tiles, axis=0)
    high = value.astype(jnp.bfloat16)
    low = (value - high.astype(jnp.float32)).astype(jnp.bfloat16)
    table = jnp.concatenate([high, low], axis=0)
    row = lax.broadcasted_iota(jnp.int32, (8, chunk), 0)
    place = ((row >> 1) & 1) * groups

    def one(d, work):
        both = jnp.dot(table, hot_ref[d], preferred_element_type=jnp.float32)
        found = both[:half] + both[half:]
        top = jnp.broadcast_to(idx_ref[d] >> 8, (8, chunk))
        total = jnp.zeros((8, chunk), jnp.float32)
        for h in range(2):
            for g in range(groups):
                at = (h * groups + g) * 8
                total = jnp.where(top == place + (6 * h * groups + g), found[at : at + 8], total)
        total = total + pltpu.roll(total, 6, 0)
        values = inner_ref[d] + jnp.concatenate([total[0:2], total[4:6]], axis=0)
        out_ref[d, :, 0:chunk] = values
        return work + values * weight_ref[d]

    work = lax.fori_loop(0, parts, one, jnp.zeros((4, chunk), jnp.float32), unroll=16)
    work = jnp.broadcast_to(jnp.sum(work, axis=1, keepdims=True), (4, LANES))
    for d in range(parts):
        out_ref[d, :, chunk : chunk + LANES] = work


def merge_kernel(x_ref, down_ref, up_ref, out_ref):
    for n in range(20):
        p, c, v = n // 10, n // 5 % 2, n % 5
        out_ref[p, c, v] = x_ref[p, c, v]
        for h, ref in enumerate((down_ref, up_ref)):
            for r in range(2):
                at, to = 8 * v + 4 * p + 2 * r + c, 6 * h + r
                out_ref[p, c, v, to : to + 1, :] = ref[at : at + 1, :]


def work_kernel(table_ref, x_ref, work_ref):
    chunk = x_ref.shape[-1] - LANES
    rows = jnp.concatenate([x_ref[d, :, chunk:] for d in range(x_ref.shape[0])], axis=0)
    work = jnp.dot(
        table_ref[...], rows, precision=HIGHEST, preferred_element_type=jnp.float32
    )
    for i in range(work_ref.shape[1] // LANES):
        work_ref[:, i * LANES : (i + 1) * LANES] = work


def phase_kernel(table_ref, x_ref, out_ref):
    parts = x_ref.shape[0]
    chunk = out_ref.shape[-1]
    table = table_ref[...]
    high = table.astype(jnp.bfloat16).astype(jnp.float32)
    table = jnp.concatenate([high, high, table - high], axis=1).astype(jnp.bfloat16)
    rows = jnp.concatenate([x_ref[d, :, 0:chunk] for d in range(parts)], axis=0)
    y = multiply(table, rows)
    for d in range(parts):
        out_ref[d] = y[4 * d : 4 * d + 4]


def place_kernel(x_ref, work_ref, out_ref, modal_ref):
    chunk = x_ref.shape[-1]
    for d in range(x_ref.shape[0]):
        for m in range(2):
            out_ref[m, :, d * chunk : (d + 1) * chunk] = x_ref[d, 2 * m : 2 * m + 2, :]
    lane = lax.broadcasted_iota(jnp.int32, (1, 2), 1)
    for m in range(2):
        re = jnp.broadcast_to(work_ref[2 * m : 2 * m + 1, 0:1], (1, 2))
        im = jnp.broadcast_to(work_ref[2 * m + 1 : 2 * m + 2, 0:1], (1, 2))
        modal_ref[m : m + 1, :] = jnp.where(lane == 0, re, im)


def phase_table(phase_index, blades):
    ids = jnp.arange(blades, dtype=jnp.int32)
    turns = ids[:, None] * phase_index[None, :] % blades
    angle = 2.0 * math.pi / blades * turns.astype(jnp.float32)
    cos, sin = jnp.cos(angle) / blades, jnp.sin(angle) / blades
    top = jnp.stack([cos, -sin], axis=2).reshape(blades, 2 * blades)
    bottom = jnp.stack([sin, cos], axis=2).reshape(blades, 2 * blades)
    return jnp.stack([top, bottom], axis=1).reshape(2 * blades, 2 * blades)


def per_device(
    previous,
    forcing,
    jacobians,
    coupling,
    diagonal,
    inertia,
    pressure_weights,
    surface_cells,
    modal_weights,
    phase_index,
):
    f32 = jnp.float32
    blades = phase_index.shape[0]
    cells = previous.shape[-1]
    entries = surface_cells.shape[0]
    devices = lax.axis_size("phase")
    count = lax.axis_size("space")
    here = lax.axis_index("space")
    forward = [(i, (i + 1) % count) for i in range(count)]
    backward = [((i + 1) % count, i) for i in range(count)]

    local_index = lax.dynamic_slice_in_dim(phase_index, lax.axis_index("phase") * 2, 2)
    angles = 2.0 * math.pi / blades * local_index.astype(f32)
    cos, sin = jnp.cos(angles), jnp.sin(angles)
    low_end, high_end = here == 0, here == count - 1
    turn = jnp.stack(
        [
            jnp.where(low_end, cos, 1.0),
            jnp.where(low_end, -sin, 0.0),
            jnp.where(high_end, cos, 1.0),
            jnp.where(high_end, sin, 0.0),
        ],
        axis=1,
    ).reshape(8)
    table = phase_table(phase_index, blades)
    chunk = entries // devices
    idx = surface_cells.reshape(devices, 1, chunk)

    def in_hbm(a):
        return pltpu.with_memory_space_constraint(a, pltpu.HBM)

    state, forcing = in_hbm(previous), in_hbm(forcing)
    coef, up, down = call(
        pack_kernel,
        "pack",
        [((6, 8, cells), f32), ((66, cells), f32), ((66, cells), f32)],
        [
            pltpu.VMEM((8, cells), f32),
            pltpu.VMEM((8, cells), f32),
            pltpu.VMEM((2, 2, 2, 5, 2, cells), f32),
            pltpu.VMEM((2, 2, 2, 5, 1, cells), f32),
            pltpu.SemaphoreType.DMA((7,)),
        ],
        1 << 20,
        [state, forcing] + [in_hbm(a) for a in (coupling, diagonal, inertia)],
        [HBM] * 5,
    )
    bf16 = jnp.bfloat16
    own, *tables = call(
        tables_kernel,
        "tables",
        [((160, 144), bf16)] + [((200, 240), bf16)] * 3,
        [],
        1 << 20,
        [jacobians, turn],
        [SMEM] * 2,
    )
    (hot,) = call(
        hot_kernel,
        "onehot",
        [((devices, WIDE, chunk), bf16)],
        [],
        8 << 20,
        [idx],
        [VMEM],
    )
    steps = ITERS // WIDTH
    edge_shape = (2, 5, 8, cells)
    for step in range(steps):
        first, last = step == 0, step == steps - 1
        lo = lax.ppermute(up, "space", forward)
        hi = lax.ppermute(down, "space", backward)
        operands = [state, forcing, coef, own] + ([] if first else [down, up])
        got = call(
            functools.partial(pre_kernel, first),
            "pre",
            [(previous.shape, f32), ((2, 40, cells), f32)]
            + ([(edge_shape, f32), ((2, 6, 8, cells), f32), (previous.shape, f32)] if first else []),
            [pltpu.VMEM((2, 48, cells), f32), pltpu.VMEM((2, 160, cells), f32)]
            + ([pltpu.VMEM(previous.shape, f32), pltpu.SemaphoreType.DMA((8,))] if first else []),
            40 << 20,
            operands,
            [HBM] * 2 + [VMEM] * 2 if first else [VMEM] * len(operands),
        )
        state, mid = got[:2]
        if first:
            edges, forcing = got[2:4], got[4]
            ghosts = ()
        if step == 1:
            mid, hot = lax.optimization_barrier((mid, hot))
        outs = [((40, cells), f32)] * 2
        operands = [turn, *tables, *edges, lo, hi, up, down, mid, *ghosts]
        specs = [SMEM] + [VMEM] * (len(operands) - 1)
        if first:
            outs += [(edge_shape, f32), ((2, 6, 8, cells), f32)]
        if last:
            (inner,) = call(
                inner_kernel,
                "inner",
                [((devices, 4, chunk), f32)],
                [pltpu.VMEM((128, WIDE), f32)],
                20 << 20,
                [pressure_weights, state, idx, hot],
                [SMEM] + [VMEM] * 3,
            )
            outs += [((2, 8, cells), f32)]
            operands += [pressure_weights]
            specs += [SMEM]
        down, up, *got = call(
            functools.partial(post_kernel, first, last),
            "post",
            outs,
            [],
            20 << 20,
            operands,
            specs,
        )
        if first:
            ghosts = got
    (press,) = got
    (mine,) = call(
        surface_kernel,
        "surface",
        [((devices, 4, chunk + LANES), f32)],
        [],
        1 << 28,
        [press, idx, hot, inner, modal_weights.reshape(devices, 1, chunk)],
        [VMEM] * 5,
    )
    (state,) = call(
        merge_kernel, "merge", [(previous.shape, f32)], [], 1 << 20, [state, down, up], [VMEM] * 3
    )

    every = lax.all_to_all(mine, "phase", 0, 0, tiled=True)
    every, state = lax.optimization_barrier((every, state))
    own_table = lax.dynamic_slice_in_dim(table, lax.axis_index("phase") * 4, 4)
    (work,) = call(
        work_kernel, "work", [((4, 2048), f32)], [], 1 << 16, [own_table, every], [VMEM] * 2
    )
    work, ready = lax.optimization_barrier((work, every))

    def across(bits):
        return lax.ppermute(work, "space", [(i, i ^ bits) for i in range(count)])

    work = (work + across(2))[:, :LANES]
    work = (work + across(4)) + (across(8) + across(12))
    work = work + across(1)
    (turned,) = call(
        phase_kernel,
        "phases",
        [((devices, 4, chunk), f32)],
        [],
        1 << 24,
        [table, ready],
        [VMEM] * 2,
    )
    blocks = lax.all_to_all(turned, "phase", 0, 0, tiled=True)
    influence, modal_work = call(
        place_kernel,
        "place",
        [((2, 2, entries), f32), ((2, 2), f32)],
        [],
        1 << 16,
        [blocks, work],
        [VMEM] * 2,
    )
    return state, influence, modal_work


def solution(mesh):
    in_specs = (
        P("phase", None, None, "space", None),
        P("phase", None, None, "space", None),
        P(),
        P(None, "space", None),
        P("space", None),
        P("space", None),
        P(),
        P("space"),
        P("space"),
        P(),
    )
    out_specs = (P("phase", None, None, "space", None), P("phase", None, "space"), P("phase", None))
    return jax.shard_map(
        per_device, mesh=mesh, in_specs=in_specs, out_specs=out_specs, check_vma=False
    )
```

```python
import functools
import math

import jax
import jax.numpy as jnp
from jax import lax
from jax.experimental import pallas as pl
from jax.experimental.pallas import tpu as pltpu
from jax.sharding import PartitionSpec as P

ITERS = 6
WIDTH = 2
RELAX = 0.8
LANES = 128
WIDE = 256
HIGHEST = lax.Precision.HIGHEST

VMEM = pl.BlockSpec(memory_space=pltpu.VMEM)
SMEM = pl.BlockSpec(memory_space=pltpu.SMEM)
HBM = pl.BlockSpec(memory_space=pltpu.HBM)


def call(kernel, name, out_shapes, scratch, flops, operands, in_specs, out_specs=None):
    return pl.pallas_call(
        kernel,
        name=name,
        out_shape=[jax.ShapeDtypeStruct(s, d) for s, d in out_shapes],
        in_specs=in_specs,
        out_specs=out_specs or [VMEM] * len(out_shapes),
        scratch_shapes=scratch,
        compiler_params=pltpu.CompilerParams(vmem_limit_bytes=20 * 1024 * 1024),
        cost_estimate=pl.CostEstimate(
            flops=flops, bytes_accessed=1 << 20, transcendentals=0
        ),
    )(*operands)


def pack_kernel(
    x_hbm, f_hbm, cpl_hbm, diag_hbm, inert_hbm, coef_ref, up_ref, down_ref, diag_ref, inert_ref, xe_ref, fe_ref, sems
):
    edges = [
        pltpu.make_async_copy(x_hbm.at[:, :, :, 6 * h : 6 * h + 2], xe_ref.at[h], sems.at[h])
        for h in range(2)
    ]
    coefs = [
        pltpu.make_async_copy(src, dst, sems.at[i])
        for i, (src, dst) in enumerate(
            [(diag_hbm, diag_ref), (inert_hbm, inert_ref), (cpl_hbm, coef_ref.at[0:4])], 2
        )
    ]
    force = [
        pltpu.make_async_copy(f_hbm.at[:, :, :, 7 * h : 7 * h + 1], fe_ref.at[h], sems.at[5 + h])
        for h in range(2)
    ]
    for copy in edges + coefs + force:
        copy.start()
    for h, ref in enumerate((down_ref, up_ref)):
        edges[h].wait()
        for p in range(2):
            for c in range(2):
                for v in range(5):
                    for r in range(2):
                        at = 8 * v + 4 * p + 2 * r + c
                        ref[at : at + 1, :] = xe_ref[h, p, c, v, r : r + 1, :]
    for copy in coefs:
        copy.wait()
    diag = diag_ref[...]
    inert = inert_ref[...]
    scale = RELAX / (diag * diag + inert * inert)
    coef_ref[4] = diag * scale
    coef_ref[5] = inert * scale
    for i in range(6):
        up_ref[60 + i : 61 + i, :] = coef_ref[i, 7:8, :]
        down_ref[60 + i : 61 + i, :] = coef_ref[i, 0:1, :]
    for h, ref in enumerate((down_ref, up_ref)):
        force[h].wait()
        for p in range(2):
            for c in range(2):
                for v in range(5):
                    at = 40 + 4 * v + 2 * p + c
                    ref[at : at + 1, :] = fe_ref[h, p, c, v, :, :]


def tables_kernel(jac_ref, rot_ref, own_ref, plain_ref, lo_ref, hi_ref):
    def split(a):
        high = a.astype(jnp.bfloat16).astype(jnp.float32)
        return jnp.concatenate([high, high, a - high], axis=1).astype(jnp.bfloat16)

    j = lax.broadcasted_iota(jnp.int32, (8, 48), 0)
    k = lax.broadcasted_iota(jnp.int32, (8, 48), 1)
    tiles = []
    for d in range(4):
        near = (jnp.where(j == 0, -99, j - 1), jnp.where(j == 7, -99, j + 1), j, j)[d]
        for v in range(5):
            total = jnp.zeros((8, 48), jnp.float32)
            for w in range(5):
                total = jnp.where(k == 8 * w + near, jac_ref[d, v, w], total)
            tiles.append(total)
    own_ref[...] = split(jnp.concatenate(tiles, axis=0))

    row = lax.broadcasted_iota(jnp.int32, (8, 80), 0)
    col = lax.broadcasted_iota(jnp.int32, (8, 80), 1)
    second = col >= 40
    inner = jnp.where(second, col - 40, col)
    var = inner >> 3
    from_row = jnp.where(second, 2, 0) + ((inner >> 1) & 1)
    to_row = 1 + ((row >> 1) & 1)
    part, from_part = row & 1, inner & 1
    phase = row >> 2
    same_phase = phase == ((inner >> 2) & 1)

    def turn(c, s):
        cos = jnp.where(phase == 0, rot_ref[c], rot_ref[4 + c])
        sin = jnp.where(phase == 0, rot_ref[s], rot_ref[4 + s])
        return jnp.where(part == from_part, cos, jnp.where(part == 0, -sin, sin))

    straight = jnp.where(part == from_part, 1.0, 0.0)
    factors = (
        straight,
        jnp.where(second, straight, turn(0, 1)),
        jnp.where(second, turn(2, 3), straight),
    )
    tiles = [[], [], []]
    for d in range(5):
        near = to_row + (-1, 1, 0, 0, 0)[d]
        here = same_phase & (from_row == near)
        for v in range(5):
            if d == 4:
                value = jnp.where(var == v, 1.0 - RELAX, 0.0)
            else:
                value = jnp.zeros((8, 80), jnp.float32)
                for w in range(5):
                    value = jnp.where(var == w, jac_ref[d, v, w], value)
            value = jnp.where(here, value, 0.0)
            for i in range(3):
                tiles[i].append(value * factors[i])
    for i, ref in enumerate((plain_ref, lo_ref, hi_ref)):
        ref[...] = split(jnp.concatenate(tiles[i], axis=0))


def hot_kernel(idx_ref, hot_ref):
    shape = hot_ref.shape[1:]

    def one(d, _):
        low = jnp.broadcast_to(idx_ref[d] & (WIDE - 1), shape)
        hot = jnp.where(lax.broadcasted_iota(jnp.int32, shape, 0) == low, 1.0, 0.0)
        hot_ref[d] = hot.astype(jnp.bfloat16)
        return 0

    lax.fori_loop(0, hot_ref.shape[0], one, 0)


def multiply(table, b):
    high = b.astype(jnp.bfloat16)
    low = (b - high.astype(jnp.float32)).astype(jnp.bfloat16)
    return jnp.dot(
        table,
        jnp.concatenate([high, low, high], axis=0),
        preferred_element_type=jnp.float32,
    )


def remainder(y, coef, forcing):
    cells = forcing.shape[-1]
    lane = lax.broadcasted_iota(jnp.int32, (8, cells), 1)
    before = jnp.where(lane == 0, 0.0, pltpu.roll(y[2], 1, 1))
    after = jnp.where(lane == cells - 1, 0.0, pltpu.roll(y[3], cells - 1, 1))
    return forcing - coef[0] * y[0] - coef[1] * y[1] - coef[2] * before - coef[3] * after


def pre_kernel(first, x_ref, f_ref, coef_ref, own_ref, *refs):
    if first:
        x_hbm, f_hbm = x_ref, f_ref
        next_ref, mid_ref, ef_ref, ecoef_ref, f_ref, b_ref, y_ref, x_ref, sems = refs
        copies = [
            pltpu.make_async_copy(src.at[p, c], dst.at[p, c], sems.at[4 * p + 2 * i + c])
            for p in range(2)
            for i, (src, dst) in enumerate(((x_hbm, x_ref), (f_hbm, f_ref)))
            for c in range(2)
        ]
        for copy in copies:
            copy.start()
    else:
        edge_refs, (next_ref, mid_ref, b_ref, y_ref) = refs[:2], refs[2:]
    cells = x_ref.shape[-1]
    if first:
        row = lax.broadcasted_iota(jnp.int32, (8, cells), 0)
        for h in range(2):
            for i in range(6):
                tile = jnp.where(
                    (row >> 1) & 1 == 0,
                    jnp.broadcast_to(coef_ref[i, 6 * h : 6 * h + 1, :], (8, cells)),
                    jnp.broadcast_to(coef_ref[i, 6 * h + 1 : 6 * h + 2, :], (8, cells)),
                )
                ecoef_ref[h, i] = jnp.where(row & 1 == 0, tile, -tile) if i == 5 else tile
    for c in range(2):
        b_ref[c, 40:48, :] = jnp.zeros((8, cells), jnp.float32)
    coef = [coef_ref[i] for i in range(6)]
    for p in range(2):
        if first:
            for copy in copies[4 * p : 4 * p + 4]:
                copy.wait()
        for c in range(2):
            b_ref[c, 0:40, :] = x_ref[p, c].reshape(40, cells)
            if first:
                for h in range(2):
                    for v in range(5):
                        for r in range(2):
                            at, row = 4 * p + 2 * r + c, 6 * h + r
                            ef_ref[h, v, at : at + 1, :] = f_ref[p, c, v, row : row + 1, :]
            else:
                for h in range(2):
                    for v in range(5):
                        for r in range(2):
                            at, to = 8 * v + 4 * p + 2 * r + c, 8 * v + 6 * h + r
                            b_ref[c, to : to + 1, :] = edge_refs[h][at : at + 1, :]
        for sweep in range(2):
            for c in range(2):
                y_ref[c] = multiply(own_ref[...], b_ref[c])
            for v in range(5):
                re, im = (
                    remainder(
                        [y_ref[c, 40 * d + 8 * v : 40 * d + 8 * v + 8, :] for d in range(4)],
                        coef,
                        f_ref[p, c, v],
                    )
                    for c in range(2)
                )
                add = (coef[4] * re + coef[5] * im, coef[4] * im - coef[5] * re)
                for c in range(2):
                    new = (1.0 - RELAX) * b_ref[c, 8 * v : 8 * v + 8, :] + add[c]
                    if sweep == 0:
                        b_ref[c, 8 * v : 8 * v + 8, :] = new
                        for h in range(2):
                            for r in range(2):
                                at = 8 * v + 4 * p + 2 * r + c
                                mid_ref[h, at : at + 1, :] = new[4 * h + r + 1 : 4 * h + r + 2, :]
                    else:
                        next_ref[p, c, v] = new


def post_kernel(first, last, plain_ref, lo_turn_ref, hi_turn_ref, ef_ref, ecoef_ref, lo_ref, hi_ref, up_ref, down_ref, mid_ref, *refs):
    if first:
        rot_ref, down_out, up_out, gf_ref, gcoef_ref = refs
    elif last:
        gf_ref, gcoef_ref, pw_ref, down_out, up_out, press_ref = refs
    else:
        gf_ref, gcoef_ref, down_out, up_out = refs
    cells = lo_ref.shape[-1]
    row = lax.broadcasted_iota(jnp.int32, (8, cells), 0)

    if first:
        for h in range(2):
            rows = (lo_ref, down_ref) if h == 0 else (up_ref, hi_ref)
            for i in range(6):
                tile = jnp.where(
                    (row >> 1) & 1 == 0,
                    jnp.broadcast_to(rows[0][60 + i : 61 + i, :], (8, cells)),
                    jnp.broadcast_to(rows[1][60 + i : 61 + i, :], (8, cells)),
                )
                gcoef_ref[h, i] = jnp.where(row & 1 == 0, tile, -tile) if i == 5 else tile
            ghost, base = (lo_ref, 0) if h == 0 else (hi_ref, 2)
            for v in range(5):
                for p in range(2):
                    i = 4 * p + base
                    cos, sin = rot_ref[i : i + 1, :], rot_ref[i + 1 : i + 2, :]
                    at = 40 + 4 * v + 2 * p
                    re = ghost[at : at + 1, :]
                    im = ghost[at + 1 : at + 2, :]
                    turned = (cos * re - sin * im, sin * re + cos * im)
                    to = 4 * p + 2 * h
                    gf_ref[h, v, to : to + 1, :] = turned[0]
                    gf_ref[h, v, to + 1 : to + 2, :] = turned[1]
                    to = 4 * p + 2 - 2 * h
                    gf_ref[h, v, to : to + 2, :] = (down_ref if h == 0 else up_ref)[at : at + 2, :]

    def sweep(table, b, coef, forcing):
        y = multiply(table[...], b)
        new = []
        for v in range(5):
            at = [40 * d + 8 * v for d in range(5)]
            rest = remainder([y[at[d] : at[d] + 8] for d in range(4)], coef, forcing[v])
            partner = jnp.where(row & 1 == 0, pltpu.roll(rest, 7, 0), pltpu.roll(rest, 1, 0))
            new.append(y[at[4] : at[4] + 8] + coef[4] * rest + coef[5] * partner)
        return jnp.concatenate(new, axis=0)

    mids = []
    for h in range(2):
        pair = (up_ref, hi_ref) if h else (lo_ref, down_ref)
        mids.append(
            sweep(
                hi_turn_ref if h else lo_turn_ref,
                jnp.concatenate([ref[0:40, :] for ref in pair], axis=0),
                [gcoef_ref[h, i] for i in range(6)],
                [gf_ref[h, v] for v in range(5)],
            )
        )
    for h in range(2):
        new = sweep(
            plain_ref,
            jnp.concatenate([mid_ref[1], mids[1]] if h else [mids[0], mid_ref[0]], axis=0),
            [ecoef_ref[h, i] for i in range(6)],
            [ef_ref[h, v] for v in range(5)],
        )
        (up_out if h else down_out)[...] = new
        if last:
            press = pw_ref[0:1, :] * new[0:8]
            for v in range(1, 5):
                press = press + pw_ref[v : v + 1, :] * new[8 * v : 8 * v + 8]
            press_ref[h] = press


def inner_kernel(pw_ref, x_ref, idx_ref, hot_ref, out_ref, table_ref):
    cells = x_ref.shape[-1]
    chunk = idx_ref.shape[-1]
    parts = idx_ref.shape[0]
    groups = cells // WIDE
    half = 16 * groups
    row = lax.broadcasted_iota(jnp.int32, (8, cells), 0)
    kept = (row >= 2) & (row < 6)
    press = []
    for i in range(4):
        value = pw_ref[0] * x_ref[i // 2, i % 2, 0]
        for v in range(1, 5):
            value = value + pw_ref[v] * x_ref[i // 2, i % 2, v]
        value = jnp.where(kept, value, 0.0)
        press.append(value)
    for i in range(2):
        value = press[2 * i] + pltpu.roll(press[2 * i + 1], 4, 0)
        high = value.astype(jnp.bfloat16).astype(jnp.float32)
        for g in range(groups):
            at = (i * groups + g) * 8
            table_ref[at : at + 8, :] = high[:, g * WIDE : (g + 1) * WIDE]
            table_ref[half + at : half + at + 8, :] = (value - high)[:, g * WIDE : (g + 1) * WIDE]
    table = table_ref[...].astype(jnp.bfloat16)
    row = lax.broadcasted_iota(jnp.int32, (8, chunk), 0)
    place = jnp.where((row >= 2) & (row < 6), row, (row + 4) & 7) * groups
    mine = (row >= 2) & (row < 6)

    def one(d, _):
        both = jnp.dot(table, hot_ref[d], preferred_element_type=jnp.float32)
        found = both[:half] + both[half:]
        top = jnp.broadcast_to(idx_ref[d] >> 8, (8, chunk))
        res = []
        for i in range(2):
            total = jnp.zeros((8, chunk), jnp.float32)
            for g in range(groups):
                at = (i * groups + g) * 8
                total = jnp.where(top == place + g, found[at : at + 8], total)
            res.append(jnp.sum(jnp.where(mine, total, 0.0), axis=0, keepdims=True))
            res.append(jnp.sum(jnp.where(mine, 0.0, total), axis=0, keepdims=True))
        out_ref[d] = jnp.concatenate(res, axis=0)
        return 0

    lax.fori_loop(0, parts, one, 0, unroll=16)


def surface_kernel(press_ref, idx_ref, hot_ref, inner_ref, weight_ref, out_ref):
    cells = press_ref.shape[-1]
    chunk = idx_ref.shape[-1]
    parts = idx_ref.shape[0]
    groups = cells // WIDE
    half = 16 * groups
    tiles = [press_ref[h, :, g * WIDE : (g + 1) * WIDE] for h in range(2) for g in range(groups)]
    value = jnp.concatenate(tiles, axis=0)
    high = value.astype(jnp.bfloat16)
    low = (value - high.astype(jnp.float32)).astype(jnp.bfloat16)
    table = jnp.concatenate([high, low], axis=0)
    row = lax.broadcasted_iota(jnp.int32, (8, chunk), 0)
    place = ((row >> 1) & 1) * groups

    def one(d, work):
        both = jnp.dot(table, hot_ref[d], preferred_element_type=jnp.float32)
        found = both[:half] + both[half:]
        top = jnp.broadcast_to(idx_ref[d] >> 8, (8, chunk))
        total = jnp.zeros((8, chunk), jnp.float32)
        for h in range(2):
            for g in range(groups):
                at = (h * groups + g) * 8
                total = jnp.where(top == place + (6 * h * groups + g), found[at : at + 8], total)
        total = total + pltpu.roll(total, 6, 0)
        values = inner_ref[d] + jnp.concatenate([total[0:2], total[4:6]], axis=0)
        out_ref[d, :, 0:chunk] = values
        return work + values * weight_ref[d]

    work = lax.fori_loop(0, parts, one, jnp.zeros((4, chunk), jnp.float32), unroll=16)
    work = jnp.broadcast_to(jnp.sum(work, axis=1, keepdims=True), (4, LANES))
    for d in range(parts):
        out_ref[d, :, chunk : chunk + LANES] = work


def merge_kernel(x_ref, down_ref, up_ref, out_ref):
    for n in range(20):
        p, c, v = n // 10, n // 5 % 2, n % 5
        out_ref[p, c, v] = x_ref[p, c, v]
        for h, ref in enumerate((down_ref, up_ref)):
            for r in range(2):
                at, to = 8 * v + 4 * p + 2 * r + c, 6 * h + r
                out_ref[p, c, v, to : to + 1, :] = ref[at : at + 1, :]


def work_kernel(table_ref, x_ref, work_ref):
    chunk = x_ref.shape[-1] - LANES
    rows = jnp.concatenate([x_ref[d, :, chunk:] for d in range(x_ref.shape[0])], axis=0)
    work = jnp.dot(
        table_ref[...], rows, precision=HIGHEST, preferred_element_type=jnp.float32
    )
    for i in range(work_ref.shape[1] // LANES):
        work_ref[:, i * LANES : (i + 1) * LANES] = work


def phase_kernel(table_ref, x_ref, out_ref):
    parts = x_ref.shape[0]
    chunk = out_ref.shape[-1]
    table = table_ref[...]
    high = table.astype(jnp.bfloat16).astype(jnp.float32)
    table = jnp.concatenate([high, high, table - high], axis=1).astype(jnp.bfloat16)
    rows = jnp.concatenate([x_ref[d, :, 0:chunk] for d in range(parts)], axis=0)
    y = multiply(table, rows)
    for d in range(parts):
        out_ref[d] = y[4 * d : 4 * d + 4]


def place_kernel(x_ref, work_ref, out_ref, modal_ref):
    chunk = x_ref.shape[-1]
    for d in range(x_ref.shape[0]):
        for m in range(2):
            out_ref[m, :, d * chunk : (d + 1) * chunk] = x_ref[d, 2 * m : 2 * m + 2, :]
    lane = lax.broadcasted_iota(jnp.int32, (1, 2), 1)
    for m in range(2):
        re = jnp.broadcast_to(work_ref[2 * m : 2 * m + 1, 0:1], (1, 2))
        im = jnp.broadcast_to(work_ref[2 * m + 1 : 2 * m + 2, 0:1], (1, 2))
        modal_ref[m : m + 1, :] = jnp.where(lane == 0, re, im)


def phase_table(phase_index, blades):
    ids = jnp.arange(blades, dtype=jnp.int32)
    turns = ids[:, None] * phase_index[None, :] % blades
    angle = 2.0 * math.pi / blades * turns.astype(jnp.float32)
    cos, sin = jnp.cos(angle) / blades, jnp.sin(angle) / blades
    top = jnp.stack([cos, -sin], axis=2).reshape(blades, 2 * blades)
    bottom = jnp.stack([sin, cos], axis=2).reshape(blades, 2 * blades)
    return jnp.stack([top, bottom], axis=1).reshape(2 * blades, 2 * blades)


def per_device(
    previous,
    forcing,
    jacobians,
    coupling,
    diagonal,
    inertia,
    pressure_weights,
    surface_cells,
    modal_weights,
    phase_index,
):
    f32 = jnp.float32
    blades = phase_index.shape[0]
    cells = previous.shape[-1]
    entries = surface_cells.shape[0]
    devices = lax.axis_size("phase")
    count = lax.axis_size("space")
    here = lax.axis_index("space")
    forward = [(i, (i + 1) % count) for i in range(count)]
    backward = [((i + 1) % count, i) for i in range(count)]

    local_index = lax.dynamic_slice_in_dim(phase_index, lax.axis_index("phase") * 2, 2)
    angles = 2.0 * math.pi / blades * local_index.astype(f32)
    cos, sin = jnp.cos(angles), jnp.sin(angles)
    low_end, high_end = here == 0, here == count - 1
    turn = jnp.stack(
        [
            jnp.where(low_end, cos, 1.0),
            jnp.where(low_end, -sin, 0.0),
            jnp.where(high_end, cos, 1.0),
            jnp.where(high_end, sin, 0.0),
        ],
        axis=1,
    ).reshape(8)
    table = phase_table(phase_index, blades)
    chunk = entries // devices
    idx = surface_cells.reshape(devices, 1, chunk)

    def in_hbm(a):
        return pltpu.with_memory_space_constraint(a, pltpu.HBM)

    state, forcing = in_hbm(previous), in_hbm(forcing)
    coef, up, down = call(
        pack_kernel,
        "pack",
        [((6, 8, cells), f32), ((66, cells), f32), ((66, cells), f32)],
        [
            pltpu.VMEM((8, cells), f32),
            pltpu.VMEM((8, cells), f32),
            pltpu.VMEM((2, 2, 2, 5, 2, cells), f32),
            pltpu.VMEM((2, 2, 2, 5, 1, cells), f32),
            pltpu.SemaphoreType.DMA((7,)),
        ],
        1 << 20,
        [state, forcing] + [in_hbm(a) for a in (coupling, diagonal, inertia)],
        [HBM] * 5,
    )
    bf16 = jnp.bfloat16
    own, *tables = call(
        tables_kernel,
        "tables",
        [((160, 144), bf16)] + [((200, 240), bf16)] * 3,
        [],
        1 << 20,
        [jacobians, turn],
        [SMEM] * 2,
    )
    (hot,) = call(
        hot_kernel,
        "onehot",
        [((devices, WIDE, chunk), bf16)],
        [],
        8 << 20,
        [idx],
        [VMEM],
    )
    steps = ITERS // WIDTH
    edge_shape = (2, 5, 8, cells)
    for step in range(steps):
        first, last = step == 0, step == steps - 1
        lo = lax.ppermute(up, "space", forward)
        hi = lax.ppermute(down, "space", backward)
        operands = [state, forcing, coef, own] + ([] if first else [down, up])
        got = call(
            functools.partial(pre_kernel, first),
            "pre",
            [(previous.shape, f32), ((2, 40, cells), f32)]
            + ([(edge_shape, f32), ((2, 6, 8, cells), f32), (previous.shape, f32)] if first else []),
            [pltpu.VMEM((2, 48, cells), f32), pltpu.VMEM((2, 160, cells), f32)]
            + ([pltpu.VMEM(previous.shape, f32), pltpu.SemaphoreType.DMA((8,))] if first else []),
            40 << 20,
            operands,
            [HBM] * 2 + [VMEM] * 2 if first else [VMEM] * len(operands),
        )
        state, mid = got[:2]
        if first:
            edges, forcing = got[2:4], got[4]
            ghosts = ()
        if step == 1:
            mid, hot = lax.optimization_barrier((mid, hot))
        outs = [((40, cells), f32)] * 2
        operands = [*tables, *edges, lo, hi, up, down, mid, *ghosts]
        if first:
            operands += [jnp.broadcast_to(turn[:, None], (8, cells))]
            outs += [(edge_shape, f32), ((2, 6, 8, cells), f32)]
        if last:
            (inner,) = call(
                inner_kernel,
                "inner",
                [((devices, 4, chunk), f32)],
                [pltpu.VMEM((128, WIDE), f32)],
                20 << 20,
                [pressure_weights, state, idx, hot],
                [SMEM] + [VMEM] * 3,
            )
            outs += [((2, 8, cells), f32)]
            operands += [jnp.broadcast_to(pressure_weights[:, None], (5, cells))]
        down, up, *got = call(
            functools.partial(post_kernel, first, last),
            "post",
            outs,
            [],
            20 << 20,
            operands,
            [VMEM] * len(operands),
        )
        if first:
            ghosts = got
    (press,) = got
    (mine,) = call(
        surface_kernel,
        "surface",
        [((devices, 4, chunk + LANES), f32)],
        [],
        1 << 28,
        [press, idx, hot, inner, modal_weights.reshape(devices, 1, chunk)],
        [VMEM] * 5,
    )
    (state,) = call(
        merge_kernel, "merge", [(previous.shape, f32)], [], 1 << 20, [state, down, up], [VMEM] * 3
    )

    every = lax.all_to_all(mine, "phase", 0, 0, tiled=True)
    every, state = lax.optimization_barrier((every, state))
    own_table = lax.dynamic_slice_in_dim(table, lax.axis_index("phase") * 4, 4)
    (work,) = call(
        work_kernel, "work", [((4, 2048), f32)], [], 1 << 16, [own_table, every], [VMEM] * 2
    )
    work, ready = lax.optimization_barrier((work, every))

    def across(bits):
        return lax.ppermute(work, "space", [(i, i ^ bits) for i in range(count)])

    work = (work + across(2))[:, :LANES]
    work = (work + across(4)) + (across(8) + across(12))
    work = work + across(1)
    (turned,) = call(
        phase_kernel,
        "phases",
        [((devices, 4, chunk), f32)],
        [],
        1 << 24,
        [table, ready],
        [VMEM] * 2,
    )
    blocks = lax.all_to_all(turned, "phase", 0, 0, tiled=True)
    influence, modal_work = call(
        place_kernel,
        "place",
        [((2, 2, entries), f32), ((2, 2), f32)],
        [],
        1 << 16,
        [blocks, work],
        [VMEM] * 2,
    )
    return state, influence, modal_work


def solution(mesh):
    in_specs = (
        P("phase", None, None, "space", None),
        P("phase", None, None, "space", None),
        P(),
        P(None, "space", None),
        P("space", None),
        P("space", None),
        P(),
        P("space"),
        P("space"),
        P(),
    )
    out_specs = (P("phase", None, None, "space", None), P("phase", None, "space"), P("phase", None))
    return jax.shard_map(
        per_device, mesh=mesh, in_specs=in_specs, out_specs=out_specs, check_vma=False
    )
```

```python
import functools
import math

import jax
import jax.numpy as jnp
from jax import lax
from jax.experimental import pallas as pl
from jax.experimental.pallas import tpu as pltpu
from jax.sharding import PartitionSpec as P

ITERS = 6
WIDTH = 2
RELAX = 0.8
LANES = 128
WIDE = 256
HIGHEST = lax.Precision.HIGHEST

VMEM = pl.BlockSpec(memory_space=pltpu.VMEM)
SMEM = pl.BlockSpec(memory_space=pltpu.SMEM)
HBM = pl.BlockSpec(memory_space=pltpu.HBM)


def call(kernel, name, out_shapes, scratch, flops, operands, in_specs, out_specs=None):
    return pl.pallas_call(
        kernel,
        name=name,
        out_shape=[jax.ShapeDtypeStruct(s, d) for s, d in out_shapes],
        in_specs=in_specs,
        out_specs=out_specs or [VMEM] * len(out_shapes),
        scratch_shapes=scratch,
        compiler_params=pltpu.CompilerParams(vmem_limit_bytes=20 * 1024 * 1024),
        cost_estimate=pl.CostEstimate(
            flops=flops, bytes_accessed=1 << 20, transcendentals=0
        ),
    )(*operands)


def pack_kernel(
    x_hbm, f_hbm, cpl_hbm, diag_hbm, inert_hbm, coef_ref, up_ref, down_ref, diag_ref, inert_ref, xe_ref, fe_ref, sems
):
    edges = [
        pltpu.make_async_copy(x_hbm.at[:, :, :, 6 * h : 6 * h + 2], xe_ref.at[h], sems.at[h])
        for h in range(2)
    ]
    coefs = [
        pltpu.make_async_copy(src, dst, sems.at[i])
        for i, (src, dst) in enumerate(
            [(diag_hbm, diag_ref), (inert_hbm, inert_ref), (cpl_hbm, coef_ref.at[0:4])], 2
        )
    ]
    force = [
        pltpu.make_async_copy(f_hbm.at[:, :, :, 7 * h : 7 * h + 1], fe_ref.at[h], sems.at[5 + h])
        for h in range(2)
    ]
    for copy in edges + coefs + force:
        copy.start()
    for h, ref in enumerate((down_ref, up_ref)):
        edges[h].wait()
        for p in range(2):
            for c in range(2):
                for v in range(5):
                    for r in range(2):
                        at = 8 * v + 4 * p + 2 * r + c
                        ref[at : at + 1, :] = xe_ref[h, p, c, v, r : r + 1, :]
    for copy in coefs:
        copy.wait()
    diag = diag_ref[...]
    inert = inert_ref[...]
    scale = RELAX / (diag * diag + inert * inert)
    coef_ref[4] = diag * scale
    coef_ref[5] = inert * scale
    for i in range(6):
        up_ref[60 + i : 61 + i, :] = coef_ref[i, 7:8, :]
        down_ref[60 + i : 61 + i, :] = coef_ref[i, 0:1, :]
    for h, ref in enumerate((down_ref, up_ref)):
        force[h].wait()
        for p in range(2):
            for c in range(2):
                for v in range(5):
                    at = 40 + 4 * v + 2 * p + c
                    ref[at : at + 1, :] = fe_ref[h, p, c, v, :, :]


def tables_kernel(jac_ref, rot_ref, own_ref, plain_ref, lo_ref, hi_ref):
    def split(a):
        high = a.astype(jnp.bfloat16).astype(jnp.float32)
        return jnp.concatenate([high, high, a - high], axis=1).astype(jnp.bfloat16)

    j = lax.broadcasted_iota(jnp.int32, (8, 48), 0)
    k = lax.broadcasted_iota(jnp.int32, (8, 48), 1)
    tiles = []
    for d in range(4):
        near = (jnp.where(j == 0, -99, j - 1), jnp.where(j == 7, -99, j + 1), j, j)[d]
        for v in range(5):
            total = jnp.zeros((8, 48), jnp.float32)
            for w in range(5):
                total = jnp.where(k == 8 * w + near, jac_ref[d, v, w], total)
            tiles.append(total)
    own_ref[...] = split(jnp.concatenate(tiles, axis=0))

    row = lax.broadcasted_iota(jnp.int32, (8, 80), 0)
    col = lax.broadcasted_iota(jnp.int32, (8, 80), 1)
    second = col >= 40
    inner = jnp.where(second, col - 40, col)
    var = inner >> 3
    from_row = jnp.where(second, 2, 0) + ((inner >> 1) & 1)
    to_row = 1 + ((row >> 1) & 1)
    part, from_part = row & 1, inner & 1
    phase = row >> 2
    same_phase = phase == ((inner >> 2) & 1)

    def turn(c, s):
        cos = jnp.where(phase == 0, rot_ref[c], rot_ref[4 + c])
        sin = jnp.where(phase == 0, rot_ref[s], rot_ref[4 + s])
        return jnp.where(part == from_part, cos, jnp.where(part == 0, -sin, sin))

    straight = jnp.where(part == from_part, 1.0, 0.0)
    factors = (
        straight,
        jnp.where(second, straight, turn(0, 1)),
        jnp.where(second, turn(2, 3), straight),
    )
    tiles = [[], [], []]
    for d in range(5):
        near = to_row + (-1, 1, 0, 0, 0)[d]
        here = same_phase & (from_row == near)
        for v in range(5):
            if d == 4:
                value = jnp.where(var == v, 1.0 - RELAX, 0.0)
            else:
                value = jnp.zeros((8, 80), jnp.float32)
                for w in range(5):
                    value = jnp.where(var == w, jac_ref[d, v, w], value)
            value = jnp.where(here, value, 0.0)
            for i in range(3):
                tiles[i].append(value * factors[i])
    for i, ref in enumerate((plain_ref, lo_ref, hi_ref)):
        ref[...] = split(jnp.concatenate(tiles[i], axis=0))


def hot_kernel(idx_ref, hot_ref):
    shape = hot_ref.shape[1:]

    def one(d, _):
        low = jnp.broadcast_to(idx_ref[d] & (WIDE - 1), shape)
        hot = jnp.where(lax.broadcasted_iota(jnp.int32, shape, 0) == low, 1.0, 0.0)
        hot_ref[d] = hot.astype(jnp.bfloat16)
        return 0

    lax.fori_loop(0, hot_ref.shape[0], one, 0)


def multiply(table, b):
    high = b.astype(jnp.bfloat16)
    low = (b - high.astype(jnp.float32)).astype(jnp.bfloat16)
    return jnp.dot(
        table,
        jnp.concatenate([high, low, high], axis=0),
        preferred_element_type=jnp.float32,
    )


def remainder(y, coef, forcing):
    cells = forcing.shape[-1]
    lane = lax.broadcasted_iota(jnp.int32, (8, cells), 1)
    before = jnp.where(lane == 0, 0.0, pltpu.roll(y[2], 1, 1))
    after = jnp.where(lane == cells - 1, 0.0, pltpu.roll(y[3], cells - 1, 1))
    return forcing - coef[0] * y[0] - coef[1] * y[1] - coef[2] * before - coef[3] * after


def pre_kernel(first, x_ref, f_ref, coef_ref, own_ref, *refs):
    if first:
        x_hbm, f_hbm = x_ref, f_ref
        next_ref, mid_ref, ef_ref, ecoef_ref, f_ref, b_ref, y_ref, x_ref, sems = refs
        copies = [
            pltpu.make_async_copy(src.at[p, c], dst.at[p, c], sems.at[4 * p + 2 * i + c])
            for p in range(2)
            for i, (src, dst) in enumerate(((x_hbm, x_ref), (f_hbm, f_ref)))
            for c in range(2)
        ]
        for copy in copies:
            copy.start()
    else:
        edge_refs, (next_ref, mid_ref, b_ref, y_ref) = refs[:2], refs[2:]
    cells = x_ref.shape[-1]
    if first:
        row = lax.broadcasted_iota(jnp.int32, (8, cells), 0)
        for h in range(2):
            for i in range(6):
                tile = jnp.where(
                    (row >> 1) & 1 == 0,
                    jnp.broadcast_to(coef_ref[i, 6 * h : 6 * h + 1, :], (8, cells)),
                    jnp.broadcast_to(coef_ref[i, 6 * h + 1 : 6 * h + 2, :], (8, cells)),
                )
                ecoef_ref[h, i] = jnp.where(row & 1 == 0, tile, -tile) if i == 5 else tile
    for c in range(2):
        b_ref[c, 40:48, :] = jnp.zeros((8, cells), jnp.float32)
    coef = [coef_ref[i] for i in range(6)]
    for p in range(2):
        if first:
            for copy in copies[4 * p : 4 * p + 4]:
                copy.wait()
        for c in range(2):
            b_ref[c, 0:40, :] = x_ref[p, c].reshape(40, cells)
            if first:
                for h in range(2):
                    for v in range(5):
                        for r in range(2):
                            at, row = 4 * p + 2 * r + c, 6 * h + r
                            ef_ref[h, v, at : at + 1, :] = f_ref[p, c, v, row : row + 1, :]
            else:
                for h in range(2):
                    for v in range(5):
                        for r in range(2):
                            at, to = 8 * v + 4 * p + 2 * r + c, 8 * v + 6 * h + r
                            b_ref[c, to : to + 1, :] = edge_refs[h][at : at + 1, :]
        for sweep in range(2):
            for c in range(2):
                y_ref[c] = multiply(own_ref[...], b_ref[c])
            for v in range(5):
                re, im = (
                    remainder(
                        [y_ref[c, 40 * d + 8 * v : 40 * d + 8 * v + 8, :] for d in range(4)],
                        coef,
                        f_ref[p, c, v],
                    )
                    for c in range(2)
                )
                add = (coef[4] * re + coef[5] * im, coef[4] * im - coef[5] * re)
                for c in range(2):
                    new = (1.0 - RELAX) * b_ref[c, 8 * v : 8 * v + 8, :] + add[c]
                    if sweep == 0:
                        b_ref[c, 8 * v : 8 * v + 8, :] = new
                        for h in range(2):
                            for r in range(2):
                                at = 8 * v + 4 * p + 2 * r + c
                                mid_ref[h, at : at + 1, :] = new[4 * h + r + 1 : 4 * h + r + 2, :]
                    else:
                        next_ref[p, c, v] = new


def post_kernel(first, last, plain_ref, lo_turn_ref, hi_turn_ref, ef_ref, ecoef_ref, lo_ref, hi_ref, up_ref, down_ref, mid_ref, *refs):
    if first:
        rot_ref, down_out, up_out, gf_ref, gcoef_ref = refs
    elif last:
        gf_ref, gcoef_ref, pw_ref, idx_ref, hot_ref, inner_ref, weight_ref, down_out, up_out, surface_ref = refs
        presses = []
    else:
        gf_ref, gcoef_ref, down_out, up_out = refs
    cells = lo_ref.shape[-1]
    row = lax.broadcasted_iota(jnp.int32, (8, cells), 0)

    if first:
        for h in range(2):
            rows = (lo_ref, down_ref) if h == 0 else (up_ref, hi_ref)
            for i in range(6):
                tile = jnp.where(
                    (row >> 1) & 1 == 0,
                    jnp.broadcast_to(rows[0][60 + i : 61 + i, :], (8, cells)),
                    jnp.broadcast_to(rows[1][60 + i : 61 + i, :], (8, cells)),
                )
                gcoef_ref[h, i] = jnp.where(row & 1 == 0, tile, -tile) if i == 5 else tile
            ghost, base = (lo_ref, 0) if h == 0 else (hi_ref, 2)
            for v in range(5):
                for p in range(2):
                    i = 4 * p + base
                    cos, sin = rot_ref[i : i + 1, :], rot_ref[i + 1 : i + 2, :]
                    at = 40 + 4 * v + 2 * p
                    re = ghost[at : at + 1, :]
                    im = ghost[at + 1 : at + 2, :]
                    turned = (cos * re - sin * im, sin * re + cos * im)
                    to = 4 * p + 2 * h
                    gf_ref[h, v, to : to + 1, :] = turned[0]
                    gf_ref[h, v, to + 1 : to + 2, :] = turned[1]
                    to = 4 * p + 2 - 2 * h
                    gf_ref[h, v, to : to + 2, :] = (down_ref if h == 0 else up_ref)[at : at + 2, :]

    def sweep(table, b, coef, forcing):
        y = multiply(table[...], b)
        new = []
        for v in range(5):
            at = [40 * d + 8 * v for d in range(5)]
            rest = remainder([y[at[d] : at[d] + 8] for d in range(4)], coef, forcing[v])
            partner = jnp.where(row & 1 == 0, pltpu.roll(rest, 7, 0), pltpu.roll(rest, 1, 0))
            new.append(y[at[4] : at[4] + 8] + coef[4] * rest + coef[5] * partner)
        return jnp.concatenate(new, axis=0)

    mids = []
    for h in range(2):
        pair = (up_ref, hi_ref) if h else (lo_ref, down_ref)
        mids.append(
            sweep(
                hi_turn_ref if h else lo_turn_ref,
                jnp.concatenate([ref[0:40, :] for ref in pair], axis=0),
                [gcoef_ref[h, i] for i in range(6)],
                [gf_ref[h, v] for v in range(5)],
            )
        )
    for h in range(2):
        new = sweep(
            plain_ref,
            jnp.concatenate([mid_ref[1], mids[1]] if h else [mids[0], mid_ref[0]], axis=0),
            [ecoef_ref[h, i] for i in range(6)],
            [ef_ref[h, v] for v in range(5)],
        )
        (up_out if h else down_out)[...] = new
        if last:
            press = pw_ref[0:1, :] * new[0:8]
            for v in range(1, 5):
                press = press + pw_ref[v : v + 1, :] * new[8 * v : 8 * v + 8]
            presses.append(press)
    if last:
        surface(presses, idx_ref, hot_ref, inner_ref, weight_ref, surface_ref)


def inner_kernel(pw_ref, x_ref, idx_ref, hot_ref, out_ref, table_ref):
    cells = x_ref.shape[-1]
    chunk = idx_ref.shape[-1]
    parts = idx_ref.shape[0]
    groups = cells // WIDE
    half = 16 * groups
    row = lax.broadcasted_iota(jnp.int32, (8, cells), 0)
    kept = (row >= 2) & (row < 6)
    press = []
    for i in range(4):
        value = pw_ref[0:1, :] * x_ref[i // 2, i % 2, 0]
        for v in range(1, 5):
            value = value + pw_ref[v : v + 1, :] * x_ref[i // 2, i % 2, v]
        value = jnp.where(kept, value, 0.0)
        press.append(value)
    for i in range(2):
        value = press[2 * i] + pltpu.roll(press[2 * i + 1], 4, 0)
        high = value.astype(jnp.bfloat16).astype(jnp.float32)
        for g in range(groups):
            at = (i * groups + g) * 8
            table_ref[at : at + 8, :] = high[:, g * WIDE : (g + 1) * WIDE]
            table_ref[half + at : half + at + 8, :] = (value - high)[:, g * WIDE : (g + 1) * WIDE]
    table = table_ref[...].astype(jnp.bfloat16)
    row = lax.broadcasted_iota(jnp.int32, (8, chunk), 0)
    place = jnp.where((row >= 2) & (row < 6), row, (row + 4) & 7) * groups
    mine = (row >= 2) & (row < 6)

    def one(d, _):
        both = jnp.dot(table, hot_ref[d], preferred_element_type=jnp.float32)
        found = both[:half] + both[half:]
        top = jnp.broadcast_to(idx_ref[d] >> 8, (8, chunk))
        res = []
        for i in range(2):
            total = jnp.zeros((8, chunk), jnp.float32)
            for g in range(groups):
                at = (i * groups + g) * 8
                total = jnp.where(top == place + g, found[at : at + 8], total)
            res.append(jnp.sum(jnp.where(mine, total, 0.0), axis=0, keepdims=True))
            res.append(jnp.sum(jnp.where(mine, 0.0, total), axis=0, keepdims=True))
        out_ref[d] = jnp.concatenate(res, axis=0)
        return 0

    lax.fori_loop(0, parts, one, 0, unroll=16)


def surface(presses, idx_ref, hot_ref, inner_ref, weight_ref, out_ref):
    cells = presses[0].shape[-1]
    chunk = idx_ref.shape[-1]
    parts = idx_ref.shape[0]
    groups = cells // WIDE
    half = 16 * groups
    tiles = [x[:, g * WIDE : (g + 1) * WIDE] for x in presses for g in range(groups)]
    value = jnp.concatenate(tiles, axis=0)
    high = value.astype(jnp.bfloat16)
    low = (value - high.astype(jnp.float32)).astype(jnp.bfloat16)
    table = jnp.concatenate([high, low], axis=0)
    row = lax.broadcasted_iota(jnp.int32, (8, chunk), 0)
    place = ((row >> 1) & 1) * groups

    def one(d, work):
        both = jnp.dot(table, hot_ref[d], preferred_element_type=jnp.float32)
        found = both[:half] + both[half:]
        top = jnp.broadcast_to(idx_ref[d] >> 8, (8, chunk))
        total = jnp.zeros((8, chunk), jnp.float32)
        for h in range(2):
            for g in range(groups):
                at = (h * groups + g) * 8
                total = jnp.where(top == place + (6 * h * groups + g), found[at : at + 8], total)
        total = total + pltpu.roll(total, 6, 0)
        values = inner_ref[d] + jnp.concatenate([total[0:2], total[4:6]], axis=0)
        for p in range(2):
            out_ref[d, :, p * chunk : (p + 1) * chunk] = values[2 * p : 2 * p + 2]
        return work + values * weight_ref[d]

    work = lax.fori_loop(0, parts, one, jnp.zeros((4, chunk), jnp.float32), unroll=16)
    work = jnp.broadcast_to(jnp.sum(work, axis=1, keepdims=True), (4, LANES))
    lane = lax.broadcasted_iota(jnp.int32, (2, LANES), 1)
    work = jnp.where(lane < LANES // 2, work[0:2], work[2:4])
    for d in range(parts):
        out_ref[d, :, 2 * chunk : 2 * chunk + LANES] = work


def merge_kernel(x_ref, down_ref, up_ref, out_ref):
    for n in range(20):
        p, c, v = n // 10, n // 5 % 2, n % 5
        out_ref[p, c, v] = x_ref[p, c, v]
        for h, ref in enumerate((down_ref, up_ref)):
            for r in range(2):
                at, to = 8 * v + 4 * p + 2 * r + c, 6 * h + r
                out_ref[p, c, v, to : to + 1, :] = ref[at : at + 1, :]


def phase_kernel(table_ref, work_table_ref, x_ref, out_ref, work_ref):
    parts = x_ref.shape[0]
    chunk = out_ref.shape[-1]
    rows = jnp.concatenate([x_ref[d, :, 2 * chunk :] for d in range(parts)], axis=0)
    work = [
        jnp.dot(work_table_ref[p], rows, precision=HIGHEST, preferred_element_type=jnp.float32)
        for p in range(2)
    ]
    half = LANES // 2
    work = jnp.broadcast_to(work[0][:, 0:1] + work[1][:, half : half + 1], (4, LANES))
    for i in range(work_ref.shape[1] // LANES):
        work_ref[:, i * LANES : (i + 1) * LANES] = work
    table = table_ref[...]
    high = table.astype(jnp.bfloat16).astype(jnp.float32)
    table = jnp.concatenate([high, high, table - high], axis=1).astype(jnp.bfloat16)
    rows = jnp.concatenate(
        [x_ref[d, :, p * chunk : (p + 1) * chunk] for d in range(parts) for p in range(2)], axis=0
    )
    y = multiply(table, rows)
    for d in range(parts):
        for m in range(2):
            out_ref[d, m] = y[4 * d + 2 * m : 4 * d + 2 * m + 2]


def place_kernel(x_ref, work_ref, out_ref, modal_ref):
    chunk = x_ref.shape[-1]
    for d in range(x_ref.shape[0]):
        for m in range(2):
            out_ref[m, :, d * chunk : (d + 1) * chunk] = x_ref[d, m]
    lane = lax.broadcasted_iota(jnp.int32, (1, 2), 1)
    for m in range(2):
        re = jnp.broadcast_to(work_ref[2 * m : 2 * m + 1, 0:1], (1, 2))
        im = jnp.broadcast_to(work_ref[2 * m + 1 : 2 * m + 2, 0:1], (1, 2))
        modal_ref[m : m + 1, :] = jnp.where(lane == 0, re, im)


def phase_table(phase_index, blades):
    ids = jnp.arange(blades, dtype=jnp.int32)
    turns = ids[:, None] * phase_index[None, :] % blades
    angle = 2.0 * math.pi / blades * turns.astype(jnp.float32)
    cos, sin = jnp.cos(angle) / blades, jnp.sin(angle) / blades
    top = jnp.stack([cos, -sin], axis=2).reshape(blades, 2 * blades)
    bottom = jnp.stack([sin, cos], axis=2).reshape(blades, 2 * blades)
    return jnp.stack([top, bottom], axis=1).reshape(2 * blades, 2 * blades)


def per_device(
    previous,
    forcing,
    jacobians,
    coupling,
    diagonal,
    inertia,
    pressure_weights,
    surface_cells,
    modal_weights,
    phase_index,
):
    f32 = jnp.float32
    blades = phase_index.shape[0]
    cells = previous.shape[-1]
    entries = surface_cells.shape[0]
    devices = lax.axis_size("phase")
    count = lax.axis_size("space")
    here = lax.axis_index("space")
    forward = [(i, (i + 1) % count) for i in range(count)]
    backward = [((i + 1) % count, i) for i in range(count)]

    local_index = lax.dynamic_slice_in_dim(phase_index, lax.axis_index("phase") * 2, 2)
    angles = 2.0 * math.pi / blades * local_index.astype(f32)
    cos, sin = jnp.cos(angles), jnp.sin(angles)
    low_end, high_end = here == 0, here == count - 1
    turn = jnp.stack(
        [
            jnp.where(low_end, cos, 1.0),
            jnp.where(low_end, -sin, 0.0),
            jnp.where(high_end, cos, 1.0),
            jnp.where(high_end, sin, 0.0),
        ],
        axis=1,
    ).reshape(8)
    table = phase_table(phase_index, blades)
    chunk = entries // devices
    idx = surface_cells.reshape(devices, 1, chunk)

    def in_hbm(a):
        return pltpu.with_memory_space_constraint(a, pltpu.HBM)

    state, forcing = in_hbm(previous), in_hbm(forcing)
    coef, up, down = call(
        pack_kernel,
        "pack",
        [((6, 8, cells), f32), ((66, cells), f32), ((66, cells), f32)],
        [
            pltpu.VMEM((8, cells), f32),
            pltpu.VMEM((8, cells), f32),
            pltpu.VMEM((2, 2, 2, 5, 2, cells), f32),
            pltpu.VMEM((2, 2, 2, 5, 1, cells), f32),
            pltpu.SemaphoreType.DMA((7,)),
        ],
        1 << 20,
        [state, forcing] + [in_hbm(a) for a in (coupling, diagonal, inertia)],
        [HBM] * 5,
    )
    bf16 = jnp.bfloat16
    own, *tables = call(
        tables_kernel,
        "tables",
        [((160, 144), bf16)] + [((200, 240), bf16)] * 3,
        [],
        1 << 20,
        [jacobians, turn],
        [SMEM] * 2,
    )
    (hot,) = call(
        hot_kernel,
        "onehot",
        [((devices, WIDE, chunk), bf16)],
        [],
        8 << 20,
        [idx],
        [VMEM],
    )
    pressure_rows = jnp.broadcast_to(pressure_weights[:, None], (5, cells))
    steps = ITERS // WIDTH
    edge_shape = (2, 5, 8, cells)
    for step in range(steps):
        first, last = step == 0, step == steps - 1
        lo = lax.ppermute(up, "space", forward)
        hi = lax.ppermute(down, "space", backward)
        operands = [state, forcing, coef, own] + ([] if first else [down, up])
        got = call(
            functools.partial(pre_kernel, first),
            "pre",
            [(previous.shape, f32), ((2, 40, cells), f32)]
            + ([(edge_shape, f32), ((2, 6, 8, cells), f32), (previous.shape, f32)] if first else []),
            [pltpu.VMEM((2, 48, cells), f32), pltpu.VMEM((2, 160, cells), f32)]
            + ([pltpu.VMEM(previous.shape, f32), pltpu.SemaphoreType.DMA((8,))] if first else []),
            40 << 20,
            operands,
            [HBM] * 2 + [VMEM] * 2 if first else [VMEM] * len(operands),
        )
        state, mid = got[:2]
        if first:
            edges, forcing = got[2:4], got[4]
            ghosts = ()
        if step == 1:
            mid, hot = lax.optimization_barrier((mid, hot))
        outs = [((40, cells), f32)] * 2
        operands = [*tables, *edges, lo, hi, up, down, mid, *ghosts]
        if first:
            operands += [jnp.broadcast_to(turn[:, None], (8, cells))]
            outs += [(edge_shape, f32), ((2, 6, 8, cells), f32)]
        if last:
            (inner,) = call(
                inner_kernel,
                "inner",
                [((devices, 4, chunk), f32)],
                [pltpu.VMEM((128, WIDE), f32)],
                20 << 20,
                [pressure_rows, state, idx, hot],
                [VMEM] * 4,
            )
            outs += [((devices, 2, 2 * chunk + LANES), f32)]
            operands += [
                pressure_rows,
                idx,
                hot,
                inner,
                modal_weights.reshape(devices, 1, chunk),
            ]
        down, up, *got = call(
            functools.partial(post_kernel, first, last),
            "post",
            outs,
            [],
            20 << 20,
            operands,
            [VMEM] * len(operands),
        )
        if first:
            ghosts = got
    (mine,) = got
    (state,) = call(
        merge_kernel, "merge", [(previous.shape, f32)], [], 1 << 20, [state, down, up], [VMEM] * 3
    )

    every = lax.all_to_all(mine, "phase", 0, 0, tiled=True)
    every, state = lax.optimization_barrier((every, state))
    own_table = lax.dynamic_slice_in_dim(table, lax.axis_index("phase") * 4, 4)
    work_table = own_table.reshape(4, devices, 2, 2).transpose(2, 0, 1, 3).reshape(2, 4, -1)
    turned, work = call(
        phase_kernel,
        "phases",
        [((devices, 2, 2, chunk), f32), ((4, 2048), f32)],
        [],
        1 << 24,
        [table, work_table, every],
        [VMEM] * 3,
    )

    def across(bits):
        return lax.ppermute(work, "space", [(i, i ^ bits) for i in range(count)])

    work = (work + across(2))[:, :LANES]
    work = (work + across(4)) + (across(8) + across(12))
    work = work + across(1)
    blocks = lax.all_to_all(turned, "phase", 0, 0, tiled=True)
    influence, modal_work = call(
        place_kernel,
        "place",
        [((2, 2, entries), f32), ((2, 2), f32)],
        [],
        1 << 16,
        [blocks, work],
        [VMEM] * 2,
    )
    return state, influence, modal_work


def solution(mesh):
    in_specs = (
        P("phase", None, None, "space", None),
        P("phase", None, None, "space", None),
        P(),
        P(None, "space", None),
        P("space", None),
        P("space", None),
        P(),
        P("space"),
        P("space"),
        P(),
    )
    out_specs = (P("phase", None, None, "space", None), P("phase", None, "space"), P("phase", None))
    return jax.shard_map(
        per_device, mesh=mesh, in_specs=in_specs, out_specs=out_specs, check_vma=False
    )
```

```python
import functools
import math

import jax
import jax.numpy as jnp
from jax import lax
from jax.experimental import pallas as pl
from jax.experimental.pallas import tpu as pltpu
from jax.sharding import PartitionSpec as P

ITERS = 6
WIDTH = 2
RELAX = 0.8
LANES = 128
WIDE = 256
HIGHEST = lax.Precision.HIGHEST

VMEM = pl.BlockSpec(memory_space=pltpu.VMEM)
SMEM = pl.BlockSpec(memory_space=pltpu.SMEM)
HBM = pl.BlockSpec(memory_space=pltpu.HBM)


def call(kernel, name, out_shapes, scratch, flops, operands, in_specs, out_specs=None):
    return pl.pallas_call(
        kernel,
        name=name,
        out_shape=[jax.ShapeDtypeStruct(s, d) for s, d in out_shapes],
        in_specs=in_specs,
        out_specs=out_specs or [VMEM] * len(out_shapes),
        scratch_shapes=scratch,
        compiler_params=pltpu.CompilerParams(vmem_limit_bytes=20 * 1024 * 1024),
        cost_estimate=pl.CostEstimate(
            flops=flops, bytes_accessed=1 << 20, transcendentals=0
        ),
    )(*operands)


def pack_kernel(
    x_hbm, f_hbm, cpl_hbm, diag_hbm, inert_hbm, coef_ref, up_ref, down_ref, diag_ref, inert_ref, xe_ref, fe_ref, sems
):
    edges = [
        pltpu.make_async_copy(x_hbm.at[:, :, :, 6 * h : 6 * h + 2], xe_ref.at[h], sems.at[h])
        for h in range(2)
    ]
    coefs = [
        pltpu.make_async_copy(src, dst, sems.at[i])
        for i, (src, dst) in enumerate(
            [(diag_hbm, diag_ref), (inert_hbm, inert_ref), (cpl_hbm, coef_ref.at[0:4])], 2
        )
    ]
    force = [
        pltpu.make_async_copy(f_hbm.at[:, :, :, 7 * h : 7 * h + 1], fe_ref.at[h], sems.at[5 + h])
        for h in range(2)
    ]
    for copy in edges + coefs + force:
        copy.start()
    for h, ref in enumerate((down_ref, up_ref)):
        edges[h].wait()
        for p in range(2):
            for c in range(2):
                for v in range(5):
                    for r in range(2):
                        at = 8 * v + 4 * p + 2 * r + c
                        ref[at : at + 1, :] = xe_ref[h, p, c, v, r : r + 1, :]
    for copy in coefs:
        copy.wait()
    diag = diag_ref[...]
    inert = inert_ref[...]
    scale = RELAX / (diag * diag + inert * inert)
    coef_ref[4] = diag * scale
    coef_ref[5] = inert * scale
    for i in range(6):
        up_ref[60 + i : 61 + i, :] = coef_ref[i, 7:8, :]
        down_ref[60 + i : 61 + i, :] = coef_ref[i, 0:1, :]
    for h, ref in enumerate((down_ref, up_ref)):
        force[h].wait()
        for p in range(2):
            for c in range(2):
                for v in range(5):
                    at = 40 + 4 * v + 2 * p + c
                    ref[at : at + 1, :] = fe_ref[h, p, c, v, :, :]


def tables_kernel(jac_ref, rot_ref, own_ref, plain_ref, lo_ref, hi_ref):
    def split(a):
        high = a.astype(jnp.bfloat16).astype(jnp.float32)
        return jnp.concatenate([high, high, a - high], axis=1).astype(jnp.bfloat16)

    j = lax.broadcasted_iota(jnp.int32, (8, 48), 0)
    k = lax.broadcasted_iota(jnp.int32, (8, 48), 1)
    tiles = []
    for d in range(4):
        near = (jnp.where(j == 0, -99, j - 1), jnp.where(j == 7, -99, j + 1), j, j)[d]
        for v in range(5):
            total = jnp.zeros((8, 48), jnp.float32)
            for w in range(5):
                total = jnp.where(k == 8 * w + near, jac_ref[d, v, w], total)
            tiles.append(total)
    own_ref[...] = split(jnp.concatenate(tiles, axis=0))

    row = lax.broadcasted_iota(jnp.int32, (8, 80), 0)
    col = lax.broadcasted_iota(jnp.int32, (8, 80), 1)
    second = col >= 40
    inner = jnp.where(second, col - 40, col)
    var = inner >> 3
    from_row = jnp.where(second, 2, 0) + ((inner >> 1) & 1)
    to_row = 1 + ((row >> 1) & 1)
    part, from_part = row & 1, inner & 1
    phase = row >> 2
    same_phase = phase == ((inner >> 2) & 1)

    def turn(c, s):
        cos = jnp.where(phase == 0, rot_ref[c], rot_ref[4 + c])
        sin = jnp.where(phase == 0, rot_ref[s], rot_ref[4 + s])
        return jnp.where(part == from_part, cos, jnp.where(part == 0, -sin, sin))

    straight = jnp.where(part == from_part, 1.0, 0.0)
    factors = (
        straight,
        jnp.where(second, straight, turn(0, 1)),
        jnp.where(second, turn(2, 3), straight),
    )
    tiles = [[], [], []]
    for d in range(5):
        near = to_row + (-1, 1, 0, 0, 0)[d]
        here = same_phase & (from_row == near)
        for v in range(5):
            if d == 4:
                value = jnp.where(var == v, 1.0 - RELAX, 0.0)
            else:
                value = jnp.zeros((8, 80), jnp.float32)
                for w in range(5):
                    value = jnp.where(var == w, jac_ref[d, v, w], value)
            value = jnp.where(here, value, 0.0)
            for i in range(3):
                tiles[i].append(value * factors[i])
    for i, ref in enumerate((plain_ref, lo_ref, hi_ref)):
        ref[...] = split(jnp.concatenate(tiles[i], axis=0))


def hot_kernel(idx_ref, hot_ref):
    shape = hot_ref.shape[1:]

    def one(d, _):
        low = jnp.broadcast_to(idx_ref[d] & (WIDE - 1), shape)
        hot = jnp.where(lax.broadcasted_iota(jnp.int32, shape, 0) == low, 1.0, 0.0)
        hot_ref[d] = hot.astype(jnp.bfloat16)
        return 0

    lax.fori_loop(0, hot_ref.shape[0], one, 0)


def multiply(table, b):
    high = b.astype(jnp.bfloat16)
    low = (b - high.astype(jnp.float32)).astype(jnp.bfloat16)
    return jnp.dot(
        table,
        jnp.concatenate([high, low, high], axis=0),
        preferred_element_type=jnp.float32,
    )


def remainder(y, coef, forcing):
    cells = forcing.shape[-1]
    lane = lax.broadcasted_iota(jnp.int32, (8, cells), 1)
    before = jnp.where(lane == 0, 0.0, pltpu.roll(y[2], 1, 1))
    after = jnp.where(lane == cells - 1, 0.0, pltpu.roll(y[3], cells - 1, 1))
    return forcing - coef[0] * y[0] - coef[1] * y[1] - coef[2] * before - coef[3] * after


def pre_kernel(first, x_ref, f_ref, coef_ref, own_ref, *refs):
    if first:
        x_hbm, f_hbm = x_ref, f_ref
        next_ref, mid_ref, ef_ref, ecoef_ref, f_ref, b_ref, y_ref, x_ref, sems = refs
        copies = [
            pltpu.make_async_copy(src.at[p, c], dst.at[p, c], sems.at[4 * p + 2 * i + c])
            for p in range(2)
            for i, (src, dst) in enumerate(((x_hbm, x_ref), (f_hbm, f_ref)))
            for c in range(2)
        ]
        for copy in copies:
            copy.start()
    else:
        edge_refs, (next_ref, mid_ref, b_ref, y_ref) = refs[:2], refs[2:]
    cells = x_ref.shape[-1]
    if first:
        row = lax.broadcasted_iota(jnp.int32, (8, cells), 0)
        for h in range(2):
            for i in range(6):
                tile = jnp.where(
                    (row >> 1) & 1 == 0,
                    jnp.broadcast_to(coef_ref[i, 6 * h : 6 * h + 1, :], (8, cells)),
                    jnp.broadcast_to(coef_ref[i, 6 * h + 1 : 6 * h + 2, :], (8, cells)),
                )
                ecoef_ref[h, i] = jnp.where(row & 1 == 0, tile, -tile) if i == 5 else tile
    for c in range(2):
        b_ref[c, 40:48, :] = jnp.zeros((8, cells), jnp.float32)
    coef = [coef_ref[i] for i in range(6)]
    for p in range(2):
        if first:
            for copy in copies[4 * p : 4 * p + 4]:
                copy.wait()
        for c in range(2):
            b_ref[c, 0:40, :] = x_ref[p, c].reshape(40, cells)
            if first:
                for h in range(2):
                    for v in range(5):
                        for r in range(2):
                            at, row = 4 * p + 2 * r + c, 6 * h + r
                            ef_ref[h, v, at : at + 1, :] = f_ref[p, c, v, row : row + 1, :]
            else:
                for h in range(2):
                    for v in range(5):
                        for r in range(2):
                            at, to = 8 * v + 4 * p + 2 * r + c, 8 * v + 6 * h + r
                            b_ref[c, to : to + 1, :] = edge_refs[h][at : at + 1, :]
        for sweep in range(2):
            for c in range(2):
                y_ref[c] = multiply(own_ref[...], b_ref[c])
            for v in range(5):
                re, im = (
                    remainder(
                        [y_ref[c, 40 * d + 8 * v : 40 * d + 8 * v + 8, :] for d in range(4)],
                        coef,
                        f_ref[p, c, v],
                    )
                    for c in range(2)
                )
                add = (coef[4] * re + coef[5] * im, coef[4] * im - coef[5] * re)
                for c in range(2):
                    new = (1.0 - RELAX) * b_ref[c, 8 * v : 8 * v + 8, :] + add[c]
                    if sweep == 0:
                        b_ref[c, 8 * v : 8 * v + 8, :] = new
                        for h in range(2):
                            for r in range(2):
                                at = 8 * v + 4 * p + 2 * r + c
                                mid_ref[h, at : at + 1, :] = new[4 * h + r + 1 : 4 * h + r + 2, :]
                    else:
                        next_ref[p, c, v] = new


def post_kernel(first, last, plain_ref, lo_turn_ref, hi_turn_ref, ef_ref, ecoef_ref, lo_ref, hi_ref, up_ref, down_ref, mid_ref, *refs):
    if first:
        rot_ref, down_out, up_out, gf_ref, gcoef_ref = refs
    elif last:
        gf_ref, gcoef_ref, pw_ref, idx_ref, hot_ref, inner_ref, weight_ref, down_out, up_out, surface_ref = refs
        presses = []
    else:
        gf_ref, gcoef_ref, down_out, up_out = refs
    cells = lo_ref.shape[-1]
    row = lax.broadcasted_iota(jnp.int32, (8, cells), 0)

    if first:
        for h in range(2):
            rows = (lo_ref, down_ref) if h == 0 else (up_ref, hi_ref)
            for i in range(6):
                tile = jnp.where(
                    (row >> 1) & 1 == 0,
                    jnp.broadcast_to(rows[0][60 + i : 61 + i, :], (8, cells)),
                    jnp.broadcast_to(rows[1][60 + i : 61 + i, :], (8, cells)),
                )
                gcoef_ref[h, i] = jnp.where(row & 1 == 0, tile, -tile) if i == 5 else tile
            ghost, base = (lo_ref, 0) if h == 0 else (hi_ref, 2)
            for v in range(5):
                for p in range(2):
                    i = 4 * p + base
                    cos, sin = rot_ref[i : i + 1, :], rot_ref[i + 1 : i + 2, :]
                    at = 40 + 4 * v + 2 * p
                    re = ghost[at : at + 1, :]
                    im = ghost[at + 1 : at + 2, :]
                    turned = (cos * re - sin * im, sin * re + cos * im)
                    to = 4 * p + 2 * h
                    gf_ref[h, v, to : to + 1, :] = turned[0]
                    gf_ref[h, v, to + 1 : to + 2, :] = turned[1]
                    to = 4 * p + 2 - 2 * h
                    gf_ref[h, v, to : to + 2, :] = (down_ref if h == 0 else up_ref)[at : at + 2, :]

    def sweep(table, b, coef, forcing):
        y = multiply(table[...], b)
        new = []
        for v in range(5):
            at = [40 * d + 8 * v for d in range(5)]
            rest = remainder([y[at[d] : at[d] + 8] for d in range(4)], coef, forcing[v])
            partner = jnp.where(row & 1 == 0, pltpu.roll(rest, 7, 0), pltpu.roll(rest, 1, 0))
            new.append(y[at[4] : at[4] + 8] + coef[4] * rest + coef[5] * partner)
        return jnp.concatenate(new, axis=0)

    mids = []
    for h in range(2):
        pair = (up_ref, hi_ref) if h else (lo_ref, down_ref)
        mids.append(
            sweep(
                hi_turn_ref if h else lo_turn_ref,
                jnp.concatenate([ref[0:40, :] for ref in pair], axis=0),
                [gcoef_ref[h, i] for i in range(6)],
                [gf_ref[h, v] for v in range(5)],
            )
        )
    for h in range(2):
        new = sweep(
            plain_ref,
            jnp.concatenate([mid_ref[1], mids[1]] if h else [mids[0], mid_ref[0]], axis=0),
            [ecoef_ref[h, i] for i in range(6)],
            [ef_ref[h, v] for v in range(5)],
        )
        (up_out if h else down_out)[...] = new
        if last:
            press = pw_ref[0:1, :] * new[0:8]
            for v in range(1, 5):
                press = press + pw_ref[v : v + 1, :] * new[8 * v : 8 * v + 8]
            presses.append(press)
    if last:
        surface(presses, idx_ref, hot_ref, inner_ref, weight_ref, surface_ref)


def inner_kernel(pw_ref, x_ref, idx_ref, hot_ref, out_ref, table_ref):
    cells = x_ref.shape[-1]
    chunk = idx_ref.shape[-1]
    parts = idx_ref.shape[0]
    groups = cells // WIDE
    half = 16 * groups
    row = lax.broadcasted_iota(jnp.int32, (8, cells), 0)
    kept = (row >= 2) & (row < 6)
    press = []
    for i in range(4):
        value = pw_ref[0:1, :] * x_ref[i // 2, i % 2, 0]
        for v in range(1, 5):
            value = value + pw_ref[v : v + 1, :] * x_ref[i // 2, i % 2, v]
        value = jnp.where(kept, value, 0.0)
        press.append(value)
    for i in range(2):
        value = press[2 * i] + pltpu.roll(press[2 * i + 1], 4, 0)
        high = value.astype(jnp.bfloat16).astype(jnp.float32)
        for g in range(groups):
            at = (i * groups + g) * 8
            table_ref[at : at + 8, :] = high[:, g * WIDE : (g + 1) * WIDE]
            table_ref[half + at : half + at + 8, :] = (value - high)[:, g * WIDE : (g + 1) * WIDE]
    table = table_ref[...].astype(jnp.bfloat16)
    row = lax.broadcasted_iota(jnp.int32, (8, chunk), 0)
    place = jnp.where((row >= 2) & (row < 6), row, (row + 4) & 7) * groups
    mine = (row >= 2) & (row < 6)

    def one(d, _):
        both = jnp.dot(table, hot_ref[d], preferred_element_type=jnp.float32)
        found = both[:half] + both[half:]
        top = jnp.broadcast_to(idx_ref[d] >> 8, (8, chunk))
        res = []
        for i in range(2):
            total = jnp.zeros((8, chunk), jnp.float32)
            for g in range(groups):
                at = (i * groups + g) * 8
                total = jnp.where(top == place + g, found[at : at + 8], total)
            res.append(jnp.sum(jnp.where(mine, total, 0.0), axis=0, keepdims=True))
            res.append(jnp.sum(jnp.where(mine, 0.0, total), axis=0, keepdims=True))
        out_ref[d] = jnp.concatenate(res, axis=0)
        return 0

    lax.fori_loop(0, parts, one, 0, unroll=16)


def surface(presses, idx_ref, hot_ref, inner_ref, weight_ref, out_ref):
    cells = presses[0].shape[-1]
    chunk = idx_ref.shape[-1]
    parts = idx_ref.shape[0]
    groups = cells // WIDE
    half = 16 * groups
    tiles = [x[:, g * WIDE : (g + 1) * WIDE] for x in presses for g in range(groups)]
    value = jnp.concatenate(tiles, axis=0)
    high = value.astype(jnp.bfloat16)
    low = (value - high.astype(jnp.float32)).astype(jnp.bfloat16)
    table = jnp.concatenate([high, low], axis=0)
    row = lax.broadcasted_iota(jnp.int32, (8, chunk), 0)
    place = ((row >> 1) & 1) * groups

    def one(d, work):
        both = jnp.dot(table, hot_ref[d], preferred_element_type=jnp.float32)
        found = both[:half] + both[half:]
        top = jnp.broadcast_to(idx_ref[d] >> 8, (8, chunk))
        total = jnp.zeros((8, chunk), jnp.float32)
        for h in range(2):
            for g in range(groups):
                at = (h * groups + g) * 8
                total = jnp.where(top == place + (6 * h * groups + g), found[at : at + 8], total)
        total = total + pltpu.roll(total, 6, 0)
        values = inner_ref[d] + jnp.concatenate([total[0:2], total[4:6]], axis=0)
        for p in range(2):
            out_ref[d, :, p * chunk : (p + 1) * chunk] = values[2 * p : 2 * p + 2]
        return work + values * weight_ref[d]

    work = lax.fori_loop(0, parts, one, jnp.zeros((4, chunk), jnp.float32), unroll=16)
    work = jnp.broadcast_to(jnp.sum(work, axis=1, keepdims=True), (4, LANES))
    lane = lax.broadcasted_iota(jnp.int32, (2, LANES), 1)
    work = jnp.where(lane < LANES // 2, work[0:2], work[2:4])
    for d in range(parts):
        out_ref[d, :, 2 * chunk : 2 * chunk + LANES] = work


def merge_kernel(x_ref, down_ref, up_ref, out_ref):
    for n in range(20):
        p, c, v = n // 10, n // 5 % 2, n % 5
        out_ref[p, c, v] = x_ref[p, c, v]
        for h, ref in enumerate((down_ref, up_ref)):
            for r in range(2):
                at, to = 8 * v + 4 * p + 2 * r + c, 6 * h + r
                out_ref[p, c, v, to : to + 1, :] = ref[at : at + 1, :]


def phase_kernel(table_ref, work_table_ref, x_ref, out_ref, work_ref):
    parts = x_ref.shape[0]
    chunk = out_ref.shape[-1]
    rows = jnp.concatenate([x_ref[d, :, 2 * chunk :] for d in range(parts)], axis=0)
    work = [
        jnp.dot(work_table_ref[p], rows, precision=HIGHEST, preferred_element_type=jnp.float32)
        for p in range(2)
    ]
    half = LANES // 2
    work = jnp.broadcast_to(work[0][:, 0:1] + work[1][:, half : half + 1], (4, LANES))
    for i in range(work_ref.shape[1] // LANES):
        work_ref[:, i * LANES : (i + 1) * LANES] = work
    table = table_ref[...]
    high = table.astype(jnp.bfloat16).astype(jnp.float32)
    table = jnp.concatenate([high, high, table - high], axis=1).astype(jnp.bfloat16)
    rows = jnp.concatenate(
        [x_ref[d, :, p * chunk : (p + 1) * chunk] for d in range(parts) for p in range(2)], axis=0
    )
    y = multiply(table, rows)
    for d in range(parts):
        for m in range(2):
            out_ref[d, m] = y[4 * d + 2 * m : 4 * d + 2 * m + 2]


def place_kernel(x_ref, work_ref, out_ref, modal_ref):
    chunk = x_ref.shape[-1]
    for d in range(x_ref.shape[0]):
        for m in range(2):
            out_ref[m, :, d * chunk : (d + 1) * chunk] = x_ref[d, m]
    lane = lax.broadcasted_iota(jnp.int32, (1, 2), 1)
    for m in range(2):
        re = jnp.broadcast_to(work_ref[2 * m : 2 * m + 1, 0:1], (1, 2))
        im = jnp.broadcast_to(work_ref[2 * m + 1 : 2 * m + 2, 0:1], (1, 2))
        modal_ref[m : m + 1, :] = jnp.where(lane == 0, re, im)


def phase_table(phase_index, blades):
    ids = jnp.arange(blades, dtype=jnp.int32)
    turns = ids[:, None] * phase_index[None, :] % blades
    angle = 2.0 * math.pi / blades * turns.astype(jnp.float32)
    cos, sin = jnp.cos(angle) / blades, jnp.sin(angle) / blades
    top = jnp.stack([cos, -sin], axis=2).reshape(blades, 2 * blades)
    bottom = jnp.stack([sin, cos], axis=2).reshape(blades, 2 * blades)
    return jnp.stack([top, bottom], axis=1).reshape(2 * blades, 2 * blades)


def per_device(
    previous,
    forcing,
    jacobians,
    coupling,
    diagonal,
    inertia,
    pressure_weights,
    surface_cells,
    modal_weights,
    phase_index,
):
    f32 = jnp.float32
    blades = phase_index.shape[0]
    cells = previous.shape[-1]
    entries = surface_cells.shape[0]
    devices = lax.axis_size("phase")
    count = lax.axis_size("space")
    here = lax.axis_index("space")
    even = here % 2 == 0
    inner_pairs = [(i, i ^ 1) for i in range(count)]
    outer = [(i, (i - 1 + 2 * (i % 2)) % count) for i in range(count)]

    local_index = lax.dynamic_slice_in_dim(phase_index, lax.axis_index("phase") * 2, 2)
    angles = 2.0 * math.pi / blades * local_index.astype(f32)
    cos, sin = jnp.cos(angles), jnp.sin(angles)
    low_end, high_end = here == 0, here == count - 1
    turn = jnp.stack(
        [
            jnp.where(low_end, cos, 1.0),
            jnp.where(low_end, -sin, 0.0),
            jnp.where(high_end, cos, 1.0),
            jnp.where(high_end, sin, 0.0),
        ],
        axis=1,
    ).reshape(8)
    table = phase_table(phase_index, blades)
    chunk = entries // devices
    idx = surface_cells.reshape(devices, 1, chunk)

    def in_hbm(a):
        return pltpu.with_memory_space_constraint(a, pltpu.HBM)

    state, forcing = in_hbm(previous), in_hbm(forcing)
    coef, up, down = call(
        pack_kernel,
        "pack",
        [((6, 8, cells), f32), ((66, cells), f32), ((66, cells), f32)],
        [
            pltpu.VMEM((8, cells), f32),
            pltpu.VMEM((8, cells), f32),
            pltpu.VMEM((2, 2, 2, 5, 2, cells), f32),
            pltpu.VMEM((2, 2, 2, 5, 1, cells), f32),
            pltpu.SemaphoreType.DMA((7,)),
        ],
        1 << 20,
        [state, forcing] + [in_hbm(a) for a in (coupling, diagonal, inertia)],
        [HBM] * 5,
    )
    bf16 = jnp.bfloat16
    own, *tables = call(
        tables_kernel,
        "tables",
        [((160, 144), bf16)] + [((200, 240), bf16)] * 3,
        [],
        1 << 20,
        [jacobians, turn],
        [SMEM] * 2,
    )
    (hot,) = call(
        hot_kernel,
        "onehot",
        [((devices, WIDE, chunk), bf16)],
        [],
        8 << 20,
        [idx],
        [VMEM],
    )
    pressure_rows = jnp.broadcast_to(pressure_weights[:, None], (5, cells))
    steps = ITERS // WIDTH
    edge_shape = (2, 5, 8, cells)
    for step in range(steps):
        first, last = step == 0, step == steps - 1
        apart = lax.ppermute(jnp.where(even, down, up), "space", outer)
        inside = lax.ppermute(jnp.where(even, up, down), "space", inner_pairs)
        lo = jnp.where(even, apart, inside)
        hi = jnp.where(even, inside, apart)
        operands = [state, forcing, coef, own] + ([] if first else [down, up])
        got = call(
            functools.partial(pre_kernel, first),
            "pre",
            [(previous.shape, f32), ((2, 40, cells), f32)]
            + ([(edge_shape, f32), ((2, 6, 8, cells), f32), (previous.shape, f32)] if first else []),
            [pltpu.VMEM((2, 48, cells), f32), pltpu.VMEM((2, 160, cells), f32)]
            + ([pltpu.VMEM(previous.shape, f32), pltpu.SemaphoreType.DMA((8,))] if first else []),
            40 << 20,
            operands,
            [HBM] * 2 + [VMEM] * 2 if first else [VMEM] * len(operands),
        )
        state, mid = got[:2]
        if first:
            edges, forcing = got[2:4], got[4]
            ghosts = ()
        if step == 1:
            mid, hot = lax.optimization_barrier((mid, hot))
        outs = [((40, cells), f32)] * 2
        operands = [*tables, *edges, lo, hi, up, down, mid, *ghosts]
        if first:
            operands += [jnp.broadcast_to(turn[:, None], (8, cells))]
            outs += [(edge_shape, f32), ((2, 6, 8, cells), f32)]
        if last:
            (inner,) = call(
                inner_kernel,
                "inner",
                [((devices, 4, chunk), f32)],
                [pltpu.VMEM((128, WIDE), f32)],
                20 << 20,
                [pressure_rows, state, idx, hot],
                [VMEM] * 4,
            )
            outs += [((devices, 2, 2 * chunk + LANES), f32)]
            operands += [
                pressure_rows,
                idx,
                hot,
                inner,
                modal_weights.reshape(devices, 1, chunk),
            ]
        down, up, *got = call(
            functools.partial(post_kernel, first, last),
            "post",
            outs,
            [],
            20 << 20,
            operands,
            [VMEM] * len(operands),
        )
        if first:
            ghosts = got
    (mine,) = got
    (state,) = call(
        merge_kernel, "merge", [(previous.shape, f32)], [], 1 << 20, [state, down, up], [VMEM] * 3
    )

    every = lax.all_to_all(mine, "phase", 0, 0, tiled=True)
    every, state = lax.optimization_barrier((every, state))
    own_table = lax.dynamic_slice_in_dim(table, lax.axis_index("phase") * 4, 4)
    work_table = own_table.reshape(4, devices, 2, 2).transpose(2, 0, 1, 3).reshape(2, 4, -1)
    turned, work = call(
        phase_kernel,
        "phases",
        [((devices, 2, 2, chunk), f32), ((4, 2048), f32)],
        [],
        1 << 24,
        [table, work_table, every],
        [VMEM] * 3,
    )

    def across(bits):
        return lax.ppermute(work, "space", [(i, i ^ bits) for i in range(count)])

    work = (work + across(2))[:, :LANES]
    work = (work + across(4)) + (across(8) + across(12))
    work = work + across(1)
    blocks = lax.all_to_all(turned, "phase", 0, 0, tiled=True)
    influence, modal_work = call(
        place_kernel,
        "place",
        [((2, 2, entries), f32), ((2, 2), f32)],
        [],
        1 << 16,
        [blocks, work],
        [VMEM] * 2,
    )
    return state, influence, modal_work


def solution(mesh):
    in_specs = (
        P("phase", None, None, "space", None),
        P("phase", None, None, "space", None),
        P(),
        P(None, "space", None),
        P("space", None),
        P("space", None),
        P(),
        P("space"),
        P("space"),
        P(),
    )
    out_specs = (P("phase", None, None, "space", None), P("phase", None, "space"), P("phase", None))
    return jax.shard_map(
        per_device, mesh=mesh, in_specs=in_specs, out_specs=out_specs, check_vma=False
    )
```

```python
import functools
import math

import jax
import jax.numpy as jnp
from jax import lax
from jax.experimental import pallas as pl
from jax.experimental.pallas import tpu as pltpu
from jax.sharding import PartitionSpec as P

ITERS = 6
WIDTH = 2
RELAX = 0.8
LANES = 128
WIDE = 256
HIGHEST = lax.Precision.HIGHEST

VMEM = pl.BlockSpec(memory_space=pltpu.VMEM)
SMEM = pl.BlockSpec(memory_space=pltpu.SMEM)
HBM = pl.BlockSpec(memory_space=pltpu.HBM)


def call(kernel, name, out_shapes, scratch, flops, operands, in_specs, out_specs=None):
    return pl.pallas_call(
        kernel,
        name=name,
        out_shape=[jax.ShapeDtypeStruct(s, d) for s, d in out_shapes],
        in_specs=in_specs,
        out_specs=out_specs or [VMEM] * len(out_shapes),
        scratch_shapes=scratch,
        compiler_params=pltpu.CompilerParams(vmem_limit_bytes=20 * 1024 * 1024),
        cost_estimate=pl.CostEstimate(
            flops=flops, bytes_accessed=1 << 20, transcendentals=0
        ),
    )(*operands)


def pack_kernel(
    x_hbm, f_hbm, cpl_hbm, diag_hbm, inert_hbm, coef_ref, up_ref, down_ref, diag_ref, inert_ref, xe_ref, fe_ref, sems
):
    edges = [
        pltpu.make_async_copy(x_hbm.at[:, :, :, 6 * h : 6 * h + 2], xe_ref.at[h], sems.at[h])
        for h in range(2)
    ]
    coefs = [
        pltpu.make_async_copy(src, dst, sems.at[i])
        for i, (src, dst) in enumerate(
            [(diag_hbm, diag_ref), (inert_hbm, inert_ref), (cpl_hbm, coef_ref.at[0:4])], 2
        )
    ]
    force = [
        pltpu.make_async_copy(f_hbm.at[:, :, :, 7 * h : 7 * h + 1], fe_ref.at[h], sems.at[5 + h])
        for h in range(2)
    ]
    for copy in edges + coefs + force:
        copy.start()
    for h, ref in enumerate((down_ref, up_ref)):
        edges[h].wait()
        for p in range(2):
            for c in range(2):
                for v in range(5):
                    for r in range(2):
                        at = 8 * v + 4 * p + 2 * r + c
                        ref[at : at + 1, :] = xe_ref[h, p, c, v, r : r + 1, :]
    for copy in coefs:
        copy.wait()
    diag = diag_ref[...]
    inert = inert_ref[...]
    scale = RELAX / (diag * diag + inert * inert)
    coef_ref[4] = diag * scale
    coef_ref[5] = inert * scale
    for i in range(6):
        up_ref[60 + i : 61 + i, :] = coef_ref[i, 7:8, :]
        down_ref[60 + i : 61 + i, :] = coef_ref[i, 0:1, :]
    for h, ref in enumerate((down_ref, up_ref)):
        force[h].wait()
        for p in range(2):
            for c in range(2):
                for v in range(5):
                    at = 40 + 4 * v + 2 * p + c
                    ref[at : at + 1, :] = fe_ref[h, p, c, v, :, :]


def tables_kernel(jac_ref, rot_ref, own_ref, plain_ref, lo_ref, hi_ref):
    def split(a):
        high = a.astype(jnp.bfloat16).astype(jnp.float32)
        return jnp.concatenate([high, high, a - high], axis=1).astype(jnp.bfloat16)

    j = lax.broadcasted_iota(jnp.int32, (8, 48), 0)
    k = lax.broadcasted_iota(jnp.int32, (8, 48), 1)
    tiles = []
    for d in range(4):
        near = (jnp.where(j == 0, -99, j - 1), jnp.where(j == 7, -99, j + 1), j, j)[d]
        for v in range(5):
            total = jnp.zeros((8, 48), jnp.float32)
            for w in range(5):
                total = jnp.where(k == 8 * w + near, jac_ref[d, v, w], total)
            tiles.append(total)
    own_ref[...] = split(jnp.concatenate(tiles, axis=0))

    row = lax.broadcasted_iota(jnp.int32, (8, 80), 0)
    col = lax.broadcasted_iota(jnp.int32, (8, 80), 1)
    second = col >= 40
    inner = jnp.where(second, col - 40, col)
    var = inner >> 3
    from_row = jnp.where(second, 2, 0) + ((inner >> 1) & 1)
    to_row = 1 + ((row >> 1) & 1)
    part, from_part = row & 1, inner & 1
    phase = row >> 2
    same_phase = phase == ((inner >> 2) & 1)

    def turn(c, s):
        cos = jnp.where(phase == 0, rot_ref[c], rot_ref[4 + c])
        sin = jnp.where(phase == 0, rot_ref[s], rot_ref[4 + s])
        return jnp.where(part == from_part, cos, jnp.where(part == 0, -sin, sin))

    straight = jnp.where(part == from_part, 1.0, 0.0)
    factors = (
        straight,
        jnp.where(second, straight, turn(0, 1)),
        jnp.where(second, turn(2, 3), straight),
    )
    tiles = [[], [], []]
    for d in range(5):
        near = to_row + (-1, 1, 0, 0, 0)[d]
        here = same_phase & (from_row == near)
        for v in range(5):
            if d == 4:
                value = jnp.where(var == v, 1.0 - RELAX, 0.0)
            else:
                value = jnp.zeros((8, 80), jnp.float32)
                for w in range(5):
                    value = jnp.where(var == w, jac_ref[d, v, w], value)
            value = jnp.where(here, value, 0.0)
            for i in range(3):
                tiles[i].append(value * factors[i])
    spare = jnp.zeros((8, 80), jnp.float32)
    for i, ref in enumerate((plain_ref, lo_ref, hi_ref)):
        ref[...] = split(jnp.concatenate(tiles[i] + [spare], axis=0))


def hot_kernel(idx_ref, hot_ref):
    shape = hot_ref.shape[1:]

    def one(d, _):
        low = jnp.broadcast_to(idx_ref[d] & (WIDE - 1), shape)
        hot = jnp.where(lax.broadcasted_iota(jnp.int32, shape, 0) == low, 1.0, 0.0)
        hot_ref[d] = hot.astype(jnp.bfloat16)
        return 0

    lax.fori_loop(0, hot_ref.shape[0], one, 0)


def multiply(table, b):
    high = b.astype(jnp.bfloat16)
    low = (b - high.astype(jnp.float32)).astype(jnp.bfloat16)
    return jnp.dot(
        table,
        jnp.concatenate([high, low, high], axis=0),
        preferred_element_type=jnp.float32,
    )


def remainder(y, coef, forcing):
    cells = forcing.shape[-1]
    lane = lax.broadcasted_iota(jnp.int32, (8, cells), 1)
    before = jnp.where(lane == 0, 0.0, pltpu.roll(y[2], 1, 1))
    after = jnp.where(lane == cells - 1, 0.0, pltpu.roll(y[3], cells - 1, 1))
    return forcing - coef[0] * y[0] - coef[1] * y[1] - coef[2] * before - coef[3] * after


def pre_kernel(first, x_ref, f_ref, coef_ref, own_ref, *refs):
    if first:
        x_hbm, f_hbm = x_ref, f_ref
        next_ref, mid_ref, ef_ref, ecoef_ref, f_ref, b_ref, y_ref, x_ref, sems = refs
        copies = [
            pltpu.make_async_copy(src.at[p, c], dst.at[p, c], sems.at[4 * p + 2 * i + c])
            for p in range(2)
            for i, (src, dst) in enumerate(((x_hbm, x_ref), (f_hbm, f_ref)))
            for c in range(2)
        ]
        for copy in copies:
            copy.start()
    else:
        edge_refs, (next_ref, mid_ref, b_ref, y_ref) = refs[:2], refs[2:]
    cells = x_ref.shape[-1]
    if first:
        row = lax.broadcasted_iota(jnp.int32, (8, cells), 0)
        for h in range(2):
            for i in range(6):
                tile = jnp.where(
                    (row >> 1) & 1 == 0,
                    jnp.broadcast_to(coef_ref[i, 6 * h : 6 * h + 1, :], (8, cells)),
                    jnp.broadcast_to(coef_ref[i, 6 * h + 1 : 6 * h + 2, :], (8, cells)),
                )
                ecoef_ref[h, i] = jnp.where(row & 1 == 0, tile, -tile) if i == 5 else tile
    for c in range(2):
        b_ref[c, 40:48, :] = jnp.zeros((8, cells), jnp.float32)
    coef = [coef_ref[i] for i in range(6)]
    for p in range(2):
        if first:
            for copy in copies[4 * p : 4 * p + 4]:
                copy.wait()
        for c in range(2):
            b_ref[c, 0:40, :] = x_ref[p, c].reshape(40, cells)
            if first:
                for h in range(2):
                    for v in range(5):
                        for r in range(2):
                            at, row = 4 * p + 2 * r + c, 6 * h + r
                            ef_ref[h, v, at : at + 1, :] = f_ref[p, c, v, row : row + 1, :]
            else:
                for h in range(2):
                    for v in range(5):
                        for r in range(2):
                            at, to = 8 * v + 4 * p + 2 * r + c, 8 * v + 6 * h + r
                            b_ref[c, to : to + 1, :] = edge_refs[h][at : at + 1, :]
        for sweep in range(2):
            for c in range(2):
                y_ref[c] = multiply(own_ref[...], b_ref[c])
            for v in range(5):
                re, im = (
                    remainder(
                        [y_ref[c, 40 * d + 8 * v : 40 * d + 8 * v + 8, :] for d in range(4)],
                        coef,
                        f_ref[p, c, v],
                    )
                    for c in range(2)
                )
                add = (coef[4] * re + coef[5] * im, coef[4] * im - coef[5] * re)
                for c in range(2):
                    new = (1.0 - RELAX) * b_ref[c, 8 * v : 8 * v + 8, :] + add[c]
                    if sweep == 0:
                        b_ref[c, 8 * v : 8 * v + 8, :] = new
                        for h in range(2):
                            for r in range(2):
                                at = 8 * v + 4 * p + 2 * r + c
                                mid_ref[h, at : at + 1, :] = new[4 * h + r + 1 : 4 * h + r + 2, :]
                    else:
                        next_ref[p, c, v] = new


def post_kernel(first, last, plain_ref, lo_turn_ref, hi_turn_ref, ef_ref, ecoef_ref, lo_ref, hi_ref, up_ref, down_ref, mid_ref, *refs):
    if first:
        rot_ref, down_out, up_out, gf_ref, gcoef_ref = refs
    elif last:
        gf_ref, gcoef_ref, pw_ref, idx_ref, hot_ref, inner_ref, weight_ref, down_out, up_out, surface_ref = refs
        presses = []
    else:
        gf_ref, gcoef_ref, down_out, up_out = refs
    cells = lo_ref.shape[-1]
    row = lax.broadcasted_iota(jnp.int32, (8, cells), 0)

    if first:
        for h in range(2):
            rows = (lo_ref, down_ref) if h == 0 else (up_ref, hi_ref)
            for i in range(6):
                tile = jnp.where(
                    (row >> 1) & 1 == 0,
                    jnp.broadcast_to(rows[0][60 + i : 61 + i, :], (8, cells)),
                    jnp.broadcast_to(rows[1][60 + i : 61 + i, :], (8, cells)),
                )
                gcoef_ref[h, i] = jnp.where(row & 1 == 0, tile, -tile) if i == 5 else tile
            ghost, base = (lo_ref, 0) if h == 0 else (hi_ref, 2)
            for v in range(5):
                for p in range(2):
                    i = 4 * p + base
                    cos, sin = rot_ref[i : i + 1, :], rot_ref[i + 1 : i + 2, :]
                    at = 40 + 4 * v + 2 * p
                    re = ghost[at : at + 1, :]
                    im = ghost[at + 1 : at + 2, :]
                    turned = (cos * re - sin * im, sin * re + cos * im)
                    to = 4 * p + 2 * h
                    gf_ref[h, v, to : to + 1, :] = turned[0]
                    gf_ref[h, v, to + 1 : to + 2, :] = turned[1]
                    to = 4 * p + 2 - 2 * h
                    gf_ref[h, v, to : to + 2, :] = (down_ref if h == 0 else up_ref)[at : at + 2, :]

    def sweep(table, b, coef, forcing):
        y = multiply(table[...], b)
        new = []
        for v in range(5):
            at = [40 * d + 8 * v for d in range(5)]
            rest = remainder([y[at[d] : at[d] + 8] for d in range(4)], coef, forcing[v])
            partner = jnp.where(row & 1 == 0, pltpu.roll(rest, 7, 0), pltpu.roll(rest, 1, 0))
            new.append(y[at[4] : at[4] + 8] + coef[4] * rest + coef[5] * partner)
        return jnp.concatenate(new, axis=0)

    mids = []
    for h in range(2):
        pair = (up_ref, hi_ref) if h else (lo_ref, down_ref)
        mids.append(
            sweep(
                hi_turn_ref if h else lo_turn_ref,
                jnp.concatenate([ref[0:40, :] for ref in pair], axis=0),
                [gcoef_ref[h, i] for i in range(6)],
                [gf_ref[h, v] for v in range(5)],
            )
        )
    for h in range(2):
        new = sweep(
            plain_ref,
            jnp.concatenate([mid_ref[1], mids[1]] if h else [mids[0], mid_ref[0]], axis=0),
            [ecoef_ref[h, i] for i in range(6)],
            [ef_ref[h, v] for v in range(5)],
        )
        (up_out if h else down_out)[...] = new
        if last:
            press = pw_ref[0:1, :] * new[0:8]
            for v in range(1, 5):
                press = press + pw_ref[v : v + 1, :] * new[8 * v : 8 * v + 8]
            presses.append(press)
    if last:
        surface(presses, idx_ref, hot_ref, inner_ref, weight_ref, surface_ref)


def inner_kernel(pw_ref, x_ref, idx_ref, hot_ref, out_ref, table_ref):
    cells = x_ref.shape[-1]
    chunk = idx_ref.shape[-1]
    parts = idx_ref.shape[0]
    groups = cells // WIDE
    half = 16 * groups
    row = lax.broadcasted_iota(jnp.int32, (8, cells), 0)
    kept = (row >= 2) & (row < 6)
    press = []
    for i in range(4):
        value = pw_ref[0:1, :] * x_ref[i // 2, i % 2, 0]
        for v in range(1, 5):
            value = value + pw_ref[v : v + 1, :] * x_ref[i // 2, i % 2, v]
        value = jnp.where(kept, value, 0.0)
        press.append(value)
    for i in range(2):
        value = press[2 * i] + pltpu.roll(press[2 * i + 1], 4, 0)
        high = value.astype(jnp.bfloat16).astype(jnp.float32)
        for g in range(groups):
            at = (i * groups + g) * 8
            table_ref[at : at + 8, :] = high[:, g * WIDE : (g + 1) * WIDE]
            table_ref[half + at : half + at + 8, :] = (value - high)[:, g * WIDE : (g + 1) * WIDE]
    table = table_ref[...].astype(jnp.bfloat16)
    row = lax.broadcasted_iota(jnp.int32, (8, chunk), 0)
    place = jnp.where((row >= 2) & (row < 6), row, (row + 4) & 7) * groups
    mine = (row >= 2) & (row < 6)

    def one(d, _):
        both = jnp.dot(table, hot_ref[d], preferred_element_type=jnp.float32)
        found = both[:half] + both[half:]
        top = jnp.broadcast_to(idx_ref[d] >> 8, (8, chunk))
        res = []
        for i in range(2):
            total = jnp.zeros((8, chunk), jnp.float32)
            for g in range(groups):
                at = (i * groups + g) * 8
                total = jnp.where(top == place + g, found[at : at + 8], total)
            res.append(jnp.sum(jnp.where(mine, total, 0.0), axis=0, keepdims=True))
            res.append(jnp.sum(jnp.where(mine, 0.0, total), axis=0, keepdims=True))
        out_ref[d] = jnp.concatenate(res, axis=0)
        return 0

    lax.fori_loop(0, parts, one, 0, unroll=16)


def surface(presses, idx_ref, hot_ref, inner_ref, weight_ref, out_ref):
    cells = presses[0].shape[-1]
    chunk = idx_ref.shape[-1]
    parts = idx_ref.shape[0]
    groups = cells // WIDE
    half = 16 * groups
    tiles = [x[:, g * WIDE : (g + 1) * WIDE] for x in presses for g in range(groups)]
    value = jnp.concatenate(tiles, axis=0)
    high = value.astype(jnp.bfloat16)
    low = (value - high.astype(jnp.float32)).astype(jnp.bfloat16)
    table = jnp.concatenate([high, low], axis=0)
    row = lax.broadcasted_iota(jnp.int32, (8, chunk), 0)
    place = ((row >> 1) & 1) * groups

    def one(d, work):
        both = jnp.dot(table, hot_ref[d], preferred_element_type=jnp.float32)
        found = both[:half] + both[half:]
        top = jnp.broadcast_to(idx_ref[d] >> 8, (8, chunk))
        total = jnp.zeros((8, chunk), jnp.float32)
        for h in range(2):
            for g in range(groups):
                at = (h * groups + g) * 8
                total = jnp.where(top == place + (6 * h * groups + g), found[at : at + 8], total)
        total = total + pltpu.roll(total, 6, 0)
        values = inner_ref[d] + jnp.concatenate([total[0:2], total[4:6]], axis=0)
        for p in range(2):
            out_ref[d, :, p * chunk : (p + 1) * chunk] = values[2 * p : 2 * p + 2]
        return work + values * weight_ref[d]

    work = lax.fori_loop(0, parts, one, jnp.zeros((4, chunk), jnp.float32), unroll=16)
    work = jnp.broadcast_to(jnp.sum(work, axis=1, keepdims=True), (4, LANES))
    lane = lax.broadcasted_iota(jnp.int32, (2, LANES), 1)
    work = jnp.where(lane < LANES // 2, work[0:2], work[2:4])
    for d in range(parts):
        out_ref[d, :, 2 * chunk : 2 * chunk + LANES] = work


def merge_kernel(x_ref, down_ref, up_ref, out_ref):
    for n in range(20):
        p, c, v = n // 10, n // 5 % 2, n % 5
        out_ref[p, c, v] = x_ref[p, c, v]
        for h, ref in enumerate((down_ref, up_ref)):
            for r in range(2):
                at, to = 8 * v + 4 * p + 2 * r + c, 6 * h + r
                out_ref[p, c, v, to : to + 1, :] = ref[at : at + 1, :]


def phase_kernel(table_ref, work_table_ref, x_ref, out_ref, work_ref):
    parts = x_ref.shape[0]
    chunk = out_ref.shape[-1]
    rows = jnp.concatenate([x_ref[d, :, 2 * chunk :] for d in range(parts)], axis=0)
    work = [
        jnp.dot(work_table_ref[p], rows, precision=HIGHEST, preferred_element_type=jnp.float32)
        for p in range(2)
    ]
    half = LANES // 2
    work = jnp.broadcast_to(work[0][:, 0:1] + work[1][:, half : half + 1], (4, LANES))
    for i in range(work_ref.shape[1] // LANES):
        work_ref[:, i * LANES : (i + 1) * LANES] = work
    table = table_ref[...]
    high = table.astype(jnp.bfloat16).astype(jnp.float32)
    table = jnp.concatenate([high, high, table - high], axis=1).astype(jnp.bfloat16)
    rows = jnp.concatenate(
        [x_ref[d, :, p * chunk : (p + 1) * chunk] for d in range(parts) for p in range(2)], axis=0
    )
    y = multiply(table, rows)
    for d in range(parts):
        for m in range(2):
            out_ref[d, m] = y[4 * d + 2 * m : 4 * d + 2 * m + 2]


def place_kernel(x_ref, work_ref, out_ref, modal_ref):
    chunk = x_ref.shape[-1]
    for d in range(x_ref.shape[0]):
        for m in range(2):
            out_ref[m, :, d * chunk : (d + 1) * chunk] = x_ref[d, m]
    lane = lax.broadcasted_iota(jnp.int32, (1, 2), 1)
    for m in range(2):
        re = jnp.broadcast_to(work_ref[2 * m : 2 * m + 1, 0:1], (1, 2))
        im = jnp.broadcast_to(work_ref[2 * m + 1 : 2 * m + 2, 0:1], (1, 2))
        modal_ref[m : m + 1, :] = jnp.where(lane == 0, re, im)


def phase_table(phase_index, blades):
    ids = jnp.arange(blades, dtype=jnp.int32)
    turns = ids[:, None] * phase_index[None, :] % blades
    angle = 2.0 * math.pi / blades * turns.astype(jnp.float32)
    cos, sin = jnp.cos(angle) / blades, jnp.sin(angle) / blades
    top = jnp.stack([cos, -sin], axis=2).reshape(blades, 2 * blades)
    bottom = jnp.stack([sin, cos], axis=2).reshape(blades, 2 * blades)
    return jnp.stack([top, bottom], axis=1).reshape(2 * blades, 2 * blades)


def per_device(
    previous,
    forcing,
    jacobians,
    coupling,
    diagonal,
    inertia,
    pressure_weights,
    surface_cells,
    modal_weights,
    phase_index,
):
    f32 = jnp.float32
    blades = phase_index.shape[0]
    cells = previous.shape[-1]
    entries = surface_cells.shape[0]
    devices = lax.axis_size("phase")
    count = lax.axis_size("space")
    here = lax.axis_index("space")
    even = here % 2 == 0
    inner_pairs = [(i, i ^ 1) for i in range(count)]
    outer = [(i, (i - 1 + 2 * (i % 2)) % count) for i in range(count)]

    local_index = lax.dynamic_slice_in_dim(phase_index, lax.axis_index("phase") * 2, 2)
    angles = 2.0 * math.pi / blades * local_index.astype(f32)
    cos, sin = jnp.cos(angles), jnp.sin(angles)
    low_end, high_end = here == 0, here == count - 1
    turn = jnp.stack(
        [
            jnp.where(low_end, cos, 1.0),
            jnp.where(low_end, -sin, 0.0),
            jnp.where(high_end, cos, 1.0),
            jnp.where(high_end, sin, 0.0),
        ],
        axis=1,
    ).reshape(8)
    table = phase_table(phase_index, blades)
    chunk = entries // devices
    idx = surface_cells.reshape(devices, 1, chunk)

    def in_hbm(a):
        return pltpu.with_memory_space_constraint(a, pltpu.HBM)

    state, forcing = in_hbm(previous), in_hbm(forcing)
    coef, up, down = call(
        pack_kernel,
        "pack",
        [((6, 8, cells), f32), ((66, cells), f32), ((66, cells), f32)],
        [
            pltpu.VMEM((8, cells), f32),
            pltpu.VMEM((8, cells), f32),
            pltpu.VMEM((2, 2, 2, 5, 2, cells), f32),
            pltpu.VMEM((2, 2, 2, 5, 1, cells), f32),
            pltpu.SemaphoreType.DMA((7,)),
        ],
        1 << 20,
        [state, forcing] + [in_hbm(a) for a in (coupling, diagonal, inertia)],
        [HBM] * 5,
    )
    bf16 = jnp.bfloat16
    own, *tables = call(
        tables_kernel,
        "tables",
        [((160, 144), bf16)] + [((208, 240), bf16)] * 3,
        [],
        1 << 20,
        [jacobians, turn],
        [SMEM] * 2,
    )
    (hot,) = call(
        hot_kernel,
        "onehot",
        [((devices, WIDE, chunk), bf16)],
        [],
        8 << 20,
        [idx],
        [VMEM],
    )
    pressure_rows = jnp.broadcast_to(pressure_weights[:, None], (5, cells))
    steps = ITERS // WIDTH
    edge_shape = (2, 5, 8, cells)
    for step in range(steps):
        first, last = step == 0, step == steps - 1
        apart = lax.ppermute(jnp.where(even, down, up), "space", outer)
        inside = lax.ppermute(jnp.where(even, up, down), "space", inner_pairs)
        lo = jnp.where(even, apart, inside)
        hi = jnp.where(even, inside, apart)
        operands = [state, forcing, coef, own] + ([] if first else [down, up])
        got = call(
            functools.partial(pre_kernel, first),
            "pre",
            [(previous.shape, f32), ((2, 40, cells), f32)]
            + ([(edge_shape, f32), ((2, 6, 8, cells), f32), (previous.shape, f32)] if first else []),
            [pltpu.VMEM((2, 48, cells), f32), pltpu.VMEM((2, 160, cells), f32)]
            + ([pltpu.VMEM(previous.shape, f32), pltpu.SemaphoreType.DMA((8,))] if first else []),
            40 << 20,
            operands,
            [HBM] * 2 + [VMEM] * 2 if first else [VMEM] * len(operands),
        )
        state, mid = got[:2]
        if first:
            edges, forcing = got[2:4], got[4]
            ghosts = ()
        if step == 1:
            mid, hot = lax.optimization_barrier((mid, hot))
        outs = [((40, cells), f32)] * 2
        operands = [*tables, *edges, lo, hi, up, down, mid, *ghosts]
        if first:
            operands += [jnp.broadcast_to(turn[:, None], (8, cells))]
            outs += [(edge_shape, f32), ((2, 6, 8, cells), f32)]
        if last:
            (inner,) = call(
                inner_kernel,
                "inner",
                [((devices, 4, chunk), f32)],
                [pltpu.VMEM((128, WIDE), f32)],
                20 << 20,
                [pressure_rows, state, idx, hot],
                [VMEM] * 4,
            )
            outs += [((devices, 2, 2 * chunk + LANES), f32)]
            operands += [
                pressure_rows,
                idx,
                hot,
                inner,
                modal_weights.reshape(devices, 1, chunk),
            ]
        down, up, *got = call(
            functools.partial(post_kernel, first, last),
            "post",
            outs,
            [],
            20 << 20,
            operands,
            [VMEM] * len(operands),
        )
        if first:
            ghosts = got
    (mine,) = got
    (state,) = call(
        merge_kernel, "merge", [(previous.shape, f32)], [], 1 << 20, [state, down, up], [VMEM] * 3
    )

    every = lax.all_to_all(mine, "phase", 0, 0, tiled=True)
    every, state = lax.optimization_barrier((every, state))
    own_table = lax.dynamic_slice_in_dim(table, lax.axis_index("phase") * 4, 4)
    work_table = own_table.reshape(4, devices, 2, 2).transpose(2, 0, 1, 3).reshape(2, 4, -1)
    turned, work = call(
        phase_kernel,
        "phases",
        [((devices, 2, 2, chunk), f32), ((4, 2048), f32)],
        [],
        1 << 24,
        [table, work_table, every],
        [VMEM] * 3,
    )

    def across(bits):
        return lax.ppermute(work, "space", [(i, i ^ bits) for i in range(count)])

    work = (work + across(2))[:, :LANES]
    work = (work + across(4)) + (across(8) + across(12))
    work = work + across(1)
    blocks = lax.all_to_all(turned, "phase", 0, 0, tiled=True)
    influence, modal_work = call(
        place_kernel,
        "place",
        [((2, 2, entries), f32), ((2, 2), f32)],
        [],
        1 << 16,
        [blocks, work],
        [VMEM] * 2,
    )
    return state, influence, modal_work


def solution(mesh):
    in_specs = (
        P("phase", None, None, "space", None),
        P("phase", None, None, "space", None),
        P(),
        P(None, "space", None),
        P("space", None),
        P("space", None),
        P(),
        P("space"),
        P("space"),
        P(),
    )
    out_specs = (P("phase", None, None, "space", None), P("phase", None, "space"), P("phase", None))
    return jax.shard_map(
        per_device, mesh=mesh, in_specs=in_specs, out_specs=out_specs, check_vma=False
    )
```
